32 devices in a mesh: groups: 2 (over y), row: 4 (over z), col: 4 (over x, core).
Axes of the slice: x: 2, y: 2, z: 4, core: 2. Of those that a mesh axis runs over, the one named last changes fastest.
Arguments:
- features: bfloat16 [4096, 256], P(('groups', 'row', 'col')), parts along dimension 0, may hold values from -6 to 6
- adj_tiles: bfloat16 [32, 4, 2, 128, 128], P(('groups', 'row'), 'col'), parts along dimension 0, may hold values from -0.5 to 0.5
- columns: int32 [32, 4, 2], P(('groups', 'row'), 'col'), parts along dimension 0, may hold values from 0 to 3, as said below
- counts: int32 [32, 4], P(('groups', 'row'), 'col'), parts along dimension 0, may hold values from 1 to 2, as said below
- weight: bfloat16 [256, 256], replicated, may hold values from -0.375 to 0.375
- bias_term: bfloat16 [256], replicated, may hold values from -3 to 3
- cotangent: bfloat16 [4096, 256], P(('groups', 'row', 'col')), parts along dimension 0, may hold values from -6 to 6
Outputs:
- activations: bfloat16 [4096, 256], P(('groups', 'row', 'col')), parts along dimension 0
- grad_features: bfloat16 [4096, 256], P(('groups', 'row', 'col')), parts along dimension 0
- grad_weight: float32 [512, 256], P('groups'), parts along dimension 0
- grad_bias: float32 [512], P('groups'), parts along dimension 0
The draws below stay inside these ranges and needn't reach their ends.
There are 2 independent parts, one for each index of `groups`. The reference program is written for one: setup_inputs(seed, part) draws one part's arguments, and reference() takes and returns one part's arrays. A program takes and returns all parts, laid end to end along the dimension named above; an argument that names none is the same for every part. Nothing has to cross between parts.
Inputs may be any that keep to these rules, and one draw needn't show every extreme that they name: The 2 tile columns of one tile row within one column block are distinct. Slots at counts and beyond hold tiles that are not part of A; some entry equals 2.
All inputs are finite; a program needn't handle non-finite values.
Results may differ from the reference program's by a relative error of at most 0.019.
Values may be sent and summed in bfloat16 or wider, within the bound.
No kernel may reach another device: no remote copies, remote signals or barrier semaphores. Data moves between devices by JAX's collectives and lax.ppermute only.
A program may use at most 128 MiB of HBM per device.

```python
import jax
import jax.numpy as jnp
from jax import lax

F = 256
TILE = 128
ROWS_DEV = 128
NODES = 2048
TILE_ROWS = 16
TR_DEV = 4
CTILES = 4
KMAX = 2
N_ROW = 4
N_COL = 4


def draw_columns(key, part):
    key = jax.random.fold_in(key, 11)
    scores = jax.random.randint(key, (TILE_ROWS, N_COL, CTILES), 0, 1 << 20) * CTILES
    scores = scores + jnp.arange(CTILES, dtype=jnp.int32)
    ordering = jnp.argsort(scores, axis=-1, stable=True)
    return ordering[..., :KMAX].astype(jnp.int32)


def draw_counts(key, part):
    key = jax.random.fold_in(key, 23)
    first_key, second_key, third_key = jax.random.split(key, 3)
    levels = jax.random.randint(first_key, (N_ROW, N_COL), 1, KMAX + 1)
    levels = jnp.repeat(levels, TR_DEV, axis=0)
    randoms = jax.random.randint(second_key, (TILE_ROWS, N_COL), 0, 1 << 20)
    drawn = 1 + randoms % levels
    forced_at = jax.random.randint(third_key, (), 0, TILE_ROWS * N_COL)
    flat_ids = jnp.arange(TILE_ROWS * N_COL, dtype=jnp.int32).reshape(TILE_ROWS, N_COL)
    return jnp.where(flat_ids == forced_at, KMAX, drawn).astype(jnp.int32)


def block_scale(stream_key, dims, pieces, low, high):
    factor_of = 1.0
    for position, blocks in pieces:
        steps = jax.random.uniform(jax.random.fold_in(jax.random.fold_in(stream_key, 6), position), (blocks,), jnp.float32, low / len(pieces), high / len(pieces))
        factor_of = factor_of * jnp.repeat(jnp.exp(steps), dims[position] // blocks).reshape((-1,) + (1,) * (len(dims) - 1 - position))
    return factor_of


def bell_draw(stream_key, dims, width, most, pieces=(), held_as=jnp.bfloat16):
    array = width * jax.random.normal(stream_key, dims, jnp.float32)
    if pieces:
        array = array * block_scale(stream_key, dims, pieces, -0.22, 0.18)
    return jnp.clip(array, -most, most).astype(held_as)


def setup_inputs(seed: int = 0, part: int = 0) -> dict:
    keys = jax.random.split(jax.random.key(seed), 8)
    part_splits = jax.random.split(jax.random.fold_in(keys[7], part), 8)
    features = bell_draw(part_splits[0], (NODES, F), 1.0, 6.0, ((0, 16),))
    adj_tiles = bell_draw(part_splits[1], (TILE_ROWS, N_COL, KMAX, TILE, TILE), (KMAX * TILE // 2) ** -0.5, 0.5, ((0, 4), (1, 4)))
    columns = draw_columns(jax.random.fold_in(jax.random.fold_in(keys[7], part), 71), part)
    counts = draw_counts(jax.random.fold_in(jax.random.fold_in(keys[7], part), 71), part)
    weight = bell_draw(keys[4], (F, F), F ** -0.5, 0.375)
    bias_term = bell_draw(keys[5], (F,), 0.5, 3.0)
    cotangent = bell_draw(part_splits[6], (NODES, F), 1.0, 6.0, ((0, 16),))
    return {"features": features, "adj_tiles": adj_tiles, "columns": columns, "counts": counts, "weight": weight, "bias_term": bias_term, "cotangent": cotangent}


def silu_parts(preact):
    sigmoid_value = jax.nn.sigmoid(preact)
    return preact * sigmoid_value, sigmoid_value * (1.0 + preact * (1.0 - sigmoid_value))


def reference(features, adj_tiles, columns, counts, weight, bias_term, cotangent):
    node_count, feat_width = features.shape
    tile_size = adj_tiles.shape[-1]
    slot_count = adj_tiles.shape[2]
    by_shard = features.reshape(N_ROW, N_COL, ROWS_DEV, feat_width)
    column_blocks = by_shard.transpose(1, 0, 2, 3).reshape(N_COL, CTILES, tile_size, feat_width)
    tile_grid = adj_tiles.reshape(N_ROW, TR_DEV, N_COL, slot_count, tile_size, tile_size)
    column_grid = columns.reshape(N_ROW, TR_DEV, N_COL, slot_count)
    count_grid = counts.reshape(N_ROW, TR_DEV, N_COL)
    slot_ids = jnp.arange(slot_count, dtype=jnp.int32)
    block_ids = jnp.arange(N_COL, dtype=jnp.int32)

    def forward_block(blocks):
        tile_block, col_block, count_block = blocks
        active = slot_ids[None, None, :] < count_block[:, :, None]
        picked = column_blocks[block_ids[None, :, None], col_block]
        picked = jnp.where(active[..., None, None], picked.astype(jnp.float32), jnp.float32(0.0))
        summed = jnp.einsum('tckij,tckjf->tif', tile_block.astype(jnp.float32), picked)
        return summed.reshape(TR_DEV * tile_size, feat_width)

    aggregated = lax.map(forward_block, (tile_grid, column_grid, count_grid)).reshape(node_count, feat_width)
    agg_low = aggregated.astype(jnp.bfloat16)
    preact = jnp.dot(agg_low, weight, preferred_element_type=jnp.float32) + bias_term.astype(jnp.float32)
    activated, derivative = silu_parts(preact)
    activations = activated.astype(jnp.bfloat16)
    grad_pre = (cotangent.astype(jnp.float32) * derivative).astype(jnp.bfloat16)
    grad_weight = jnp.dot(agg_low.T, grad_pre, preferred_element_type=jnp.float32)
    grad_bias = jnp.sum(grad_pre.astype(jnp.float32), axis=0)
    grad_agg = jnp.dot(grad_pre, weight.T, preferred_element_type=jnp.float32).astype(jnp.bfloat16)
    grad_rows = grad_agg.reshape(N_ROW, TR_DEV, tile_size, feat_width)

    def backward_block(running, blocks):
        tile_block, col_block, count_block, grad_block = blocks
        active = slot_ids[None, None, :] < count_block[:, :, None]
        contrib = jnp.einsum('tckij,tif->tckjf', tile_block.astype(jnp.float32), grad_block.astype(jnp.float32))
        contrib = jnp.where(active[..., None, None], contrib, jnp.float32(0.0))
        partial_value = jnp.zeros((N_COL, CTILES, tile_size, feat_width), jnp.float32)
        partial_value = partial_value.at[jnp.broadcast_to(block_ids[None, :, None], col_block.shape), col_block].add(contrib)
        rounded = lax.optimization_barrier(partial_value.astype(jnp.bfloat16)).astype(jnp.float32)
        return running + rounded, None

    start = jnp.zeros((N_COL, CTILES, tile_size, feat_width), jnp.float32)
    running, _ = lax.scan(backward_block, start, (tile_grid, column_grid, count_grid, grad_rows))
    grad_features = running.reshape(N_COL, N_ROW, ROWS_DEV, feat_width).transpose(1, 0, 2, 3)
    grad_features = grad_features.reshape(node_count, feat_width).astype(jnp.bfloat16)
    return activations, grad_features, grad_weight, grad_bias
```

```python
import jax
import jax.numpy as jnp
from jax import lax
from jax.experimental import pallas as pl
from jax.experimental.pallas import tpu as pltpu
from jax.sharding import PartitionSpec as P

BF = jnp.bfloat16
F32 = jnp.float32
LIMIT = 48 * 1024 * 1024


def dot(a, b, ca=1, cb=0):
    return lax.dot_general(a, b, (((ca,), (cb,)), ((), ())), preferred_element_type=F32)


def call(body, outs, scratch=(), smem=0, count=1):
    vm = pl.BlockSpec(memory_space=pltpu.VMEM)
    sm = pl.BlockSpec(memory_space=pltpu.SMEM)
    return pl.pallas_call(
        body,
        in_specs=[sm] * smem + [vm] * (count - smem),
        out_specs=jax.tree.map(lambda _: vm, outs),
        out_shape=outs,
        scratch_shapes=scratch,
        compiler_params=pltpu.CompilerParams(vmem_limit_bytes=LIMIT),
    )


def dense_kernel(n_row, n_col):
    def body(cols_ref, cnts_ref, tiles_ref, a_ref, at_ref):
        trows, _, slots, tile, _ = tiles_ref.shape
        r = lax.axis_index("row")
        c = lax.axis_index("col")
        a_ref[...] = jnp.zeros_like(a_ref)
        at_ref[...] = jnp.zeros_like(at_ref)

        def put(step, carry):
            t = step // slots
            k = step % slots

            @pl.when(k < cnts_ref[t, 0])
            def _():
                q = lax.rem(t - c + n_col, n_col)
                p = lax.rem(cols_ref[t, 0, k] - r + n_row, n_row)
                here = tiles_ref[t, 0, k]
                qs = pl.ds(pl.multiple_of(q * tile, tile), tile)
                ps = pl.ds(pl.multiple_of(p * tile, tile), tile)
                a_ref[qs, ps] = here
                at_ref[ps, qs] = here.T

            return carry

        lax.fori_loop(0, trows * slots, put, 0)

    return body


def forward_kernel(n_row, n_col, tile):
    def body(a_ref, *refs):
        x = jnp.concatenate([ref[...] for ref in refs[:n_row]], axis=0)
        for q, out in enumerate(refs[n_row:]):
            out[...] = dot(a_ref[q * tile : (q + 1) * tile, :], x).astype(BF)

    return body


def middle_kernel(n_col):
    def body(w_ref, b_ref, cot_ref, *refs):
        parts, (act_ref, agg_ref, pre_ref, gagg_ref) = refs[:n_col], refs[n_col:]
        total = parts[0][...].astype(F32)
        for ref in parts[1:]:
            total = total + ref[...].astype(F32)
        agg = total.astype(BF)
        agg_ref[...] = agg
        preact = dot(agg, w_ref[...]) + b_ref[...].astype(F32)
        sig = jax.nn.sigmoid(preact)
        act_ref[...] = (preact * sig).astype(BF)
        grad = cot_ref[...].astype(F32) * (sig * (1.0 + preact * (1.0 - sig)))
        grad = grad.astype(BF)
        pre_ref[...] = grad
        gagg_ref[...] = dot(grad, w_ref[...], 1, 1).astype(BF)

    return body


def weight_kernel(n_dev, rows):
    def body(agg_ref, pre_ref, out_ref):
        pre = pre_ref[...]
        local = dot(agg_ref[...], pre, 0, 0).astype(BF)
        bias = jnp.sum(pre.astype(F32), axis=0, keepdims=True)
        high = bias.astype(BF)
        low = (bias - high.astype(F32)).astype(BF)
        pad = out_ref.shape[1] - rows
        which = lax.broadcasted_iota(jnp.int32, (pad, bias.shape[1]), 0)
        tail = jnp.where(which == 0, high.astype(F32), jnp.where(which == 1, low.astype(F32), 0.0))
        tail = tail.astype(BF)
        for i in range(n_dev):
            out_ref[i, :rows, :] = local[i * rows : (i + 1) * rows, :]
            out_ref[i, rows:, :] = tail

    return body


def weight_sum_kernel(n_dev, rows):
    def body(in_ref, w_ref, b_ref):
        total = in_ref[0].astype(F32)
        for i in range(1, n_dev):
            total = total + in_ref[i].astype(F32)
        w_ref[...] = total[:rows].astype(BF)
        b_ref[...] = (total[rows : rows + 1] + total[rows + 1 : rows + 2])

    return body


def backward_kernel(n_row, n_col, tile):
    def body(at_ref, *refs):
        g = jnp.concatenate([ref[...] for ref in refs[:n_col]], axis=0)
        for p, out in enumerate(refs[n_col:]):
            out[...] = dot(at_ref[p * tile : (p + 1) * tile, :], g).astype(BF)

    return body


def sum_kernel(body_refs, out_ref):
    total = body_refs[0][...].astype(F32)
    for ref in body_refs[1:]:
        total = total + ref[...].astype(F32)
    out_ref[...] = total.astype(BF)


def shift(x, axis, n, by):
    return lax.ppermute(x, axis, [(i, (i + by) % n) for i in range(n)])


def shards(n_row, n_col, features, adj_tiles, columns, counts, weight, bias_term, cotangent):
    rows_dev, width = features.shape
    tile = adj_tiles.shape[-1]
    n_dev = n_row * n_col
    shard = jax.ShapeDtypeStruct((rows_dev, width), BF)

    xs = [features] + [shift(features, "row", n_row, -p) for p in range(1, n_row)]
    a, at = call(
        dense_kernel(n_row, n_col),
        (
            jax.ShapeDtypeStruct((n_col * tile, n_row * tile), BF),
            jax.ShapeDtypeStruct((n_row * tile, n_col * tile), BF),
        ),
        smem=2,
        count=3,
    )(columns, counts, adj_tiles)
    parts = call(forward_kernel(n_row, n_col, tile), (shard,) * n_col, count=1 + n_row)(a, *xs)
    parts = [parts[0]] + [shift(parts[q], "col", n_col, q) for q in range(1, n_col)]
    act, agg, pre, gagg = call(middle_kernel(n_col), (shard,) * 4, count=3 + n_col)(
        weight, bias_term.reshape(1, width), cotangent, *parts
    )
    gs = [gagg] + [shift(gagg, "col", n_col, -q) for q in range(1, n_col)]

    if width % n_dev == 0 and width // n_dev >= 16:
        rows = width // n_dev
        packed = call(
            weight_kernel(n_dev, rows),
            jax.ShapeDtypeStruct((n_dev, rows + 16, width), BF),
            count=2,
        )(agg, pre)
        packed = lax.all_to_all(packed, ("row", "col"), 0, 0)
        part, grad_bias = call(
            weight_sum_kernel(n_dev, rows),
            (jax.ShapeDtypeStruct((rows, width), BF), jax.ShapeDtypeStruct((1, width), F32)),
            count=1,
        )(packed)
        grad_weight = lax.all_gather(part, ("row", "col"), axis=0, tiled=True).astype(F32)
        grad_bias = grad_bias.reshape(width)
    else:
        grad_weight = jnp.dot(agg.T, pre, preferred_element_type=F32)
        grad_bias = jnp.sum(pre.astype(F32), axis=0)
        grad_weight, grad_bias = lax.psum((grad_weight, grad_bias), ("row", "col"))

    fs = call(backward_kernel(n_row, n_col, tile), (shard,) * n_row, count=1 + n_col)(at, *gs)
    fs = [fs[0]] + [shift(fs[p], "row", n_row, p) for p in range(1, n_row)]
    grad_features = call(
        lambda *refs: sum_kernel(refs[:-1], refs[-1]), shard, count=n_row
    )(*fs)
    return act, grad_features, grad_weight, grad_bias


def solution(mesh):
    n_row, n_col = mesh.shape["row"], mesh.shape["col"]
    placed = (
        P(("groups", "row", "col"), None),
        P(("groups", "row"), "col", None, None, None),
        P(("groups", "row"), "col", None),
        P(("groups", "row"), "col"),
        P(),
        P(),
        P(("groups", "row", "col"), None),
    )

    def body(*args):
        return shards(n_row, n_col, *args)

    return jax.shard_map(
        body,
        mesh=mesh,
        in_specs=placed,
        out_specs=(
            P(("groups", "row", "col"), None),
            P(("groups", "row", "col"), None),
            P("groups", None),
            P("groups"),
        ),
        check_vma=False,
    )
```

```python
import jax
import jax.numpy as jnp
from jax import lax
from jax.experimental import pallas as pl
from jax.experimental.pallas import tpu as pltpu
from jax.sharding import PartitionSpec as P

BF = jnp.bfloat16
F32 = jnp.float32
LIMIT = 48 * 1024 * 1024
PAD = 16


def dot(a, b, ca=1, cb=0):
    return lax.dot_general(a, b, (((ca,), (cb,)), ((), ())), preferred_element_type=F32)


def call(body, outs, smem=0, count=1):
    vm = pl.BlockSpec(memory_space=pltpu.VMEM)
    sm = pl.BlockSpec(memory_space=pltpu.SMEM)
    return pl.pallas_call(
        body,
        in_specs=[sm] * smem + [vm] * (count - smem),
        out_specs=jax.tree.map(lambda _: vm, outs),
        out_shape=outs,
        compiler_params=pltpu.CompilerParams(vmem_limit_bytes=LIMIT),
    )


def shape(*dims, dtype=BF):
    return jax.ShapeDtypeStruct(dims, dtype)


def dense_kernel(n_row):
    def body(cols_ref, cnts_ref, tiles_ref, a_ref, at_ref):
        trows, _, slots, tile, _ = tiles_ref.shape
        r = lax.axis_index("row")
        a_ref[...] = jnp.zeros_like(a_ref)
        at_ref[...] = jnp.zeros_like(at_ref)

        def put(step, carry):
            t = step // slots
            k = step % slots

            @pl.when(k < cnts_ref[t, 0])
            def _():
                j = cols_ref[t, 0, k]
                p = lax.rem(j - r + n_row, n_row)
                here = tiles_ref[t, 0, k]
                ts = pl.ds(pl.multiple_of(t * tile, tile), tile)
                a_ref[ts, pl.ds(pl.multiple_of(p * tile, tile), tile)] = here
                at_ref[pl.ds(pl.multiple_of(j * tile, tile), tile), ts] = here.T

            return carry

        lax.fori_loop(0, trows * slots, put, 0)

    return body


def forward_kernel(a_ref, *refs):
    out_ref = refs[-1]
    tile = refs[0].shape[0]
    x = jnp.concatenate([ref[...] for ref in refs[:-1]], axis=0)
    for q in range(out_ref.shape[0]):
        out_ref[q] = dot(a_ref[q * tile : (q + 1) * tile, :], x).astype(BF)


def total_of(ref, first, rows):
    total = ref[0, first : first + rows, :].astype(F32)
    for i in range(1, ref.shape[0]):
        total = total + ref[i, first : first + rows, :].astype(F32)
    return total


def two_rows(line):
    high = line.astype(BF).astype(F32)
    which = lax.broadcasted_iota(jnp.int32, (PAD, line.shape[1]), 0)
    return jnp.where(which == 0, high, jnp.where(which == 1, line - high, 0.0)).astype(BF)


def middle_kernel(parts_ref, w_ref, b_ref, cot_ref, act_ref, out_ref):
    n_col, tile, width = parts_ref.shape
    piece = width // n_col
    agg = total_of(parts_ref, 0, tile).astype(BF)
    preact = dot(agg, w_ref[...]) + b_ref[...].astype(F32)
    sig = jax.nn.sigmoid(preact)
    act_ref[...] = (preact * sig).astype(BF)
    grad = cot_ref[...].astype(F32) * (sig * (1.0 + preact * (1.0 - sig)))
    grad = grad.astype(BF)
    gagg = dot(grad, w_ref[...], 1, 1).astype(BF)
    local = dot(agg, grad, 0, 0).astype(BF)
    tail = two_rows(jnp.sum(grad.astype(F32), axis=0, keepdims=True))
    for i in range(n_col):
        out_ref[i, :tile, :] = gagg
        out_ref[i, tile : tile + piece, :] = local[i * piece : (i + 1) * piece, :]
        out_ref[i, tile + piece :, :] = tail


def backward_kernel(at_ref, in_ref, out_ref):
    n_col = in_ref.shape[0]
    width = in_ref.shape[2]
    tile = at_ref.shape[0] // out_ref.shape[0]
    piece = width // n_col
    g = jnp.concatenate([in_ref[i, :tile, :] for i in range(n_col)], axis=0)
    part = total_of(in_ref, tile, piece).astype(BF)
    lines = total_of(in_ref, tile + piece, PAD)
    tail = two_rows(lines[0:1] + lines[1:2])
    for p in range(out_ref.shape[0]):
        out_ref[p, :tile, :] = dot(at_ref[p * tile : (p + 1) * tile, :], g).astype(BF)
        out_ref[p, tile : tile + piece, :] = part
        out_ref[p, tile + piece :, :] = tail


def quarter_kernel(in_ref, feat_ref, out_ref, bias_ref):
    n_col, piece, _ = out_ref.shape
    tile = feat_ref.shape[0]
    part = total_of(in_ref, tile, piece).astype(BF)
    for i in range(n_col):
        out_ref[i] = part
    feat_ref[...] = total_of(in_ref, 0, tile).astype(BF)
    lines = total_of(in_ref, tile + piece, PAD)
    bias_ref[...] = lines[0:1] + lines[1:2]


def widen_kernel(in_ref, out_ref):
    n_col, piece, _ = in_ref.shape
    for i in range(n_col):
        out_ref[i * piece : (i + 1) * piece, :] = in_ref[i].astype(F32)


def shards(n_row, n_col, features, adj_tiles, columns, counts, weight, bias_term, cotangent):
    tile, width = features.shape
    piece = width // n_col
    xs = [features]
    for p in range(1, n_row):
        xs.append(lax.ppermute(features, "row", [(i, (i - p) % n_row) for i in range(n_row)]))
    a, at = call(
        dense_kernel(n_row),
        (shape(n_col * tile, n_row * tile), shape(n_row * tile, n_col * tile)),
        smem=2,
        count=3,
    )(columns, counts, adj_tiles)
    parts = call(forward_kernel, shape(n_col, tile, width), count=1 + n_row)(a, *xs)
    parts = lax.all_to_all(parts, "col", 0, 0)
    act, packed = call(
        middle_kernel,
        (shape(tile, width), shape(n_col, tile + piece + PAD, width)),
        count=4,
    )(parts, weight, bias_term.reshape(1, width), cotangent)
    packed = lax.all_to_all(packed, "col", 0, 0)
    packed = call(backward_kernel, shape(n_row, tile + piece + PAD, width), count=2)(at, packed)
    packed = lax.all_to_all(packed, "row", 0, 0)
    grad_features, quarters, grad_bias = call(
        quarter_kernel,
        (shape(tile, width), shape(n_col, piece, width), shape(1, width, dtype=F32)),
        count=1,
    )(packed)
    quarters = lax.all_to_all(quarters, "col", 0, 0)
    grad_weight = call(widen_kernel, shape(width, width, dtype=F32), count=1)(quarters)
    return act, grad_features, grad_weight, grad_bias.reshape(width)


def solution(mesh):
    n_row, n_col = mesh.shape["row"], mesh.shape["col"]
    placed = (
        P(("groups", "row", "col"), None),
        P(("groups", "row"), "col", None, None, None),
        P(("groups", "row"), "col", None),
        P(("groups", "row"), "col"),
        P(),
        P(),
        P(("groups", "row", "col"), None),
    )

    def body(*args):
        return shards(n_row, n_col, *args)

    return jax.shard_map(
        body,
        mesh=mesh,
        in_specs=placed,
        out_specs=(
            P(("groups", "row", "col"), None),
            P(("groups", "row", "col"), None),
            P("groups", None),
            P("groups"),
        ),
        check_vma=False,
    )
```

```python
import jax
import jax.numpy as jnp
from jax import lax
from jax.experimental import pallas as pl
from jax.experimental.pallas import tpu as pltpu
from jax.sharding import PartitionSpec as P

BF = jnp.bfloat16
F32 = jnp.float32
LIMIT = 48 * 1024 * 1024
PAD = 16


def dot(a, b, ca=1, cb=0):
    return lax.dot_general(a, b, (((ca,), (cb,)), ((), ())), preferred_element_type=F32)


def call(body, outs, smem=0, count=1, scratch=()):
    vm = pl.BlockSpec(memory_space=pltpu.VMEM)
    sm = pl.BlockSpec(memory_space=pltpu.SMEM)
    return pl.pallas_call(
        body,
        in_specs=[sm] * smem + [vm] * (count - smem),
        out_specs=jax.tree.map(lambda _: vm, outs),
        out_shape=outs,
        scratch_shapes=scratch,
        compiler_params=pltpu.CompilerParams(vmem_limit_bytes=LIMIT),
    )


def shape(*dims, dtype=BF):
    return jax.ShapeDtypeStruct(dims, dtype)


def dense_kernel(cols_ref, cnts_ref, tiles_ref, a_ref, at_ref):
    trows, _, slots, tile, _ = tiles_ref.shape
    r = lax.axis_index("row")
    c = lax.axis_index("col")
    a_ref[...] = jnp.zeros_like(a_ref)
    at_ref[...] = jnp.zeros_like(at_ref)

    def put(step, carry):
        t = step // slots
        k = step % slots

        @pl.when(k < cnts_ref[0, t])
        def _():
            q = jnp.bitwise_xor(t, c)
            p = jnp.bitwise_xor(cols_ref[0, k, t], r)
            here = tiles_ref[t, 0, k]
            qs = pl.ds(pl.multiple_of(q * tile, tile), tile)
            ps = pl.ds(pl.multiple_of(p * tile, tile), tile)
            a_ref[qs, ps] = here
            at_ref[ps, qs] = here.T

        return carry

    lax.fori_loop(0, trows * slots, put, 0)


def forward_kernel(n_row):
    def body(a_ref, *refs):
        tile = refs[0].shape[0]
        x = jnp.concatenate([ref[...] for ref in refs[:n_row]], axis=0)
        for q, out in enumerate(refs[n_row:]):
            out[...] = dot(a_ref[q * tile : (q + 1) * tile, :], x).astype(BF)

    return body


def total_of(refs, first, rows):
    total = refs[0][first : first + rows, :].astype(F32)
    for ref in refs[1:]:
        total = total + ref[first : first + rows, :].astype(F32)
    return total


def two_rows(line):
    high = line.astype(BF).astype(F32)
    which = lax.broadcasted_iota(jnp.int32, (PAD, line.shape[1]), 0)
    return jnp.where(which == 0, high, jnp.where(which == 1, line - high, 0.0)).astype(BF)


def middle_kernel(n_col):
    def body(w_ref, b_ref, cot_ref, *refs):
        parts, act_ref, outs, local_ref = refs[:n_col], refs[n_col], refs[n_col + 1 : -1], refs[-1]
        tile, width = cot_ref.shape
        piece = width // n_col
        c = lax.axis_index("col")
        agg = total_of(parts, 0, tile).astype(BF)
        preact = dot(agg, w_ref[...]) + b_ref[...].astype(F32)
        sig = jax.nn.sigmoid(preact)
        act_ref[...] = (preact * sig).astype(BF)
        grad = cot_ref[...].astype(F32) * (sig * (1.0 + preact * (1.0 - sig)))
        grad = grad.astype(BF)
        gagg = dot(grad, w_ref[...], 1, 1).astype(BF)
        local_ref[...] = dot(agg, grad, 0, 0)
        tail = two_rows(jnp.sum(grad.astype(F32), axis=0, keepdims=True))
        for q, out in enumerate(outs):
            first = pl.multiple_of(jnp.bitwise_xor(c, q) * piece, piece)
            out[:tile, :] = gagg
            out[tile : tile + piece, :] = local_ref[pl.ds(first, piece), :].astype(BF)
            out[tile + piece :, :] = tail

    return body


def backward_kernel(n_col):
    def body(at_ref, *refs):
        ins, outs = refs[:n_col], refs[n_col:]
        tile = at_ref.shape[0] // len(outs)
        piece = ins[0].shape[0] - tile - PAD
        g = jnp.concatenate([ref[:tile, :] for ref in ins], axis=0)
        part = total_of(ins, tile, piece).astype(BF)
        lines = total_of(ins, tile + piece, PAD)
        tail = two_rows(lines[0:1] + lines[1:2])
        for p, out in enumerate(outs):
            out[:tile, :] = dot(at_ref[p * tile : (p + 1) * tile, :], g).astype(BF)
            out[tile : tile + piece, :] = part
            out[tile + piece :, :] = tail

    return body


def quarter_kernel(*refs):
    ins, (feat_ref, out_ref, bias_ref) = refs[:-3], refs[-3:]
    tile, piece = feat_ref.shape[0], out_ref.shape[0]
    out_ref[...] = total_of(ins, tile, piece).astype(BF)
    feat_ref[...] = total_of(ins, 0, tile).astype(BF)
    lines = total_of(ins, tile + piece, PAD)
    bias_ref[...] = lines[0:1] + lines[1:2]


def widen_kernel(*refs):
    ins, out_ref = refs[:-1], refs[-1]
    piece = ins[0].shape[0]
    c = lax.axis_index("col")
    for q, ref in enumerate(ins):
        first = pl.multiple_of(jnp.bitwise_xor(c, q) * piece, piece)
        out_ref[pl.ds(first, piece), :] = ref[...].astype(F32)


def swap(x, axis, n, by):
    return lax.ppermute(x, axis, [(i, i ^ by) for i in range(n)])


def deal(xs, axis):
    n = len(xs)
    got = {by: swap(xs[by], axis, n, by) for by in [*range(2, n), 1]}
    return [xs[0]] + [got[by] for by in range(1, n)]


def spread(x, axis, n):
    return deal([x] * n, axis)


def shards(n_row, n_col, features, adj_tiles, columns, counts, weight, bias_term, cotangent):
    tile, width = features.shape
    piece = width // n_col
    message = shape(tile + piece + PAD, width)
    xs = spread(features, "row", n_row)
    a, at = call(
        dense_kernel,
        (shape(n_col * tile, n_row * tile), shape(n_row * tile, n_col * tile)),
        smem=2,
        count=3,
    )(columns.transpose(1, 2, 0), counts.T, adj_tiles)
    parts = call(forward_kernel(n_row), (shape(tile, width),) * n_col, count=1 + n_row)(a, *xs)
    act, *packed = call(
        middle_kernel(n_col),
        (shape(tile, width),) + (message,) * n_col,
        count=3 + n_col,
        scratch=[pltpu.VMEM((width, width), F32)],
    )(weight, bias_term.reshape(1, width), cotangent, *deal(parts, "col"))
    packed = call(backward_kernel(n_col), (message,) * n_row, count=1 + n_col)(
        at, *deal(packed, "col")
    )
    grad_features, quarter, grad_bias = call(
        quarter_kernel,
        (shape(tile, width), shape(piece, width), shape(1, width, dtype=F32)),
        count=n_row,
    )(*deal(packed, "row"))
    grad_weight = call(widen_kernel, shape(width, width, dtype=F32), count=n_col)(
        *spread(quarter, "col", n_col)
    )
    return act, grad_features, grad_weight, grad_bias.reshape(width)


def solution(mesh):
    n_row, n_col = mesh.shape["row"], mesh.shape["col"]
    placed = (
        P(("groups", "row", "col"), None),
        P(("groups", "row"), "col", None, None, None),
        P(("groups", "row"), "col", None),
        P(("groups", "row"), "col"),
        P(),
        P(),
        P(("groups", "row", "col"), None),
    )

    def body(*args):
        return shards(n_row, n_col, *args)

    return jax.shard_map(
        body,
        mesh=mesh,
        in_specs=placed,
        out_specs=(
            P(("groups", "row", "col"), None),
            P(("groups", "row", "col"), None),
            P("groups", None),
            P("groups"),
        ),
        check_vma=False,
    )
```

```python
import jax
import jax.numpy as jnp
from jax import lax
from jax.experimental import pallas as pl
from jax.experimental.pallas import tpu as pltpu
from jax.sharding import PartitionSpec as P

BF = jnp.bfloat16
F32 = jnp.float32
LIMIT = 48 * 1024 * 1024
PAD = 16


def dot(a, b, ca=1, cb=0):
    return lax.dot_general(a, b, (((ca,), (cb,)), ((), ())), preferred_element_type=F32)


def call(body, outs, smem=0, count=1, scratch=()):
    vm = pl.BlockSpec(memory_space=pltpu.VMEM)
    sm = pl.BlockSpec(memory_space=pltpu.SMEM)
    return pl.pallas_call(
        body,
        in_specs=[sm] * smem + [vm] * (count - smem),
        out_specs=jax.tree.map(lambda _: vm, outs),
        out_shape=outs,
        scratch_shapes=scratch,
        compiler_params=pltpu.CompilerParams(vmem_limit_bytes=LIMIT),
    )


def shape(*dims, dtype=BF):
    return jax.ShapeDtypeStruct(dims, dtype)


def own_piece(c, n_chip):
    return lax.rem(c, 2) * n_chip + lax.div(c, 2)


def dense_kernel(n_chip):
    def body(cols_ref, cnts_ref, tiles_ref, a_ref, at_ref):
        trows, _, slots, tile, _ = tiles_ref.shape
        r = lax.axis_index("row")
        c = lax.axis_index("col")
        a_ref[...] = jnp.zeros_like(a_ref)
        at_ref[...] = jnp.zeros_like(at_ref)

        def put(step, carry):
            t = step // slots
            k = step % slots

            @pl.when(k < cnts_ref[0, t])
            def _():
                q = own_piece(jnp.bitwise_xor(t, c), n_chip)
                p = jnp.bitwise_xor(cols_ref[0, k, t], r)
                here = tiles_ref[t, 0, k]
                qs = pl.ds(pl.multiple_of(q * tile, tile), tile)
                ps = pl.ds(pl.multiple_of(p * tile, tile), tile)
                a_ref[qs, ps] = here
                at_ref[ps, qs] = here.T

            return carry

        lax.fori_loop(0, trows * slots, put, 0)

    return body


def forward_kernel(n_row):
    def body(a_ref, *refs):
        ins, (keep_ref, send_ref) = refs[:n_row], refs[-2:]
        half = keep_ref.shape[0]
        x = jnp.concatenate([ref[...] for ref in ins], axis=0)
        send_ref[...] = dot(a_ref[half:, :], x).astype(BF)
        keep_ref[...] = dot(a_ref[:half, :], x)

    return body


def chip_kernel(keep_ref, got_ref, out_ref):
    out_ref[...] = (keep_ref[...] + got_ref[...].astype(F32)).astype(BF)


def two_rows(line):
    high = line.astype(BF).astype(F32)
    which = lax.broadcasted_iota(jnp.int32, (PAD, line.shape[1]), 0)
    return jnp.where(which == 0, high, jnp.where(which == 1, line - high, 0.0)).astype(BF)


def middle_kernel(n_chip):
    def body(w_ref, b_ref, *refs):
        cots, sums = refs[:n_chip], refs[n_chip : 2 * n_chip]
        act_ref, keep_ref, piece_ref, line_ref, send_ref, local_ref = refs[2 * n_chip :]
        tile, width = cots[0].shape
        rows = n_chip * tile
        piece = piece_ref.shape[0]
        c = lax.axis_index("col")
        blocks = []
        for u in range(n_chip):
            total = sums[0][u * tile : (u + 1) * tile, :].astype(F32)
            for v in range(1, n_chip):
                total = total + sums[v][(u ^ v) * tile : ((u ^ v) + 1) * tile, :].astype(F32)
            blocks.append(total.astype(BF))
        agg = jnp.concatenate(blocks, axis=0)
        cot = jnp.concatenate([ref[...] for ref in cots], axis=0).astype(F32)
        preact = dot(agg, w_ref[...]) + b_ref[...].astype(F32)
        sig = jax.nn.sigmoid(preact)
        act_ref[...] = (preact[:tile] * sig[:tile]).astype(BF)
        grad = (cot * (sig * (1.0 + preact * (1.0 - sig)))).astype(BF)
        gagg = dot(grad, w_ref[...], 1, 1).astype(BF)
        keep_ref[...] = gagg
        send_ref[:rows, :] = gagg
        local_ref[...] = dot(agg, grad, 0, 0)
        mine = pl.multiple_of(own_piece(c, n_chip) * piece, piece)
        other = pl.multiple_of(own_piece(jnp.bitwise_xor(c, 1), n_chip) * piece, piece)
        piece_ref[...] = local_ref[pl.ds(mine, piece), :]
        send_ref[rows : rows + piece, :] = local_ref[pl.ds(other, piece), :].astype(BF)
        line = jnp.sum(grad.astype(F32), axis=0, keepdims=True)
        line_ref[...] = line
        send_ref[rows + piece :, :] = two_rows(line)

    return body


def backward_kernel(at_ref, keep_ref, got_ref, piece_ref, line_ref, *outs):
    outs, part_ref = outs[:-1], outs[-1]
    rows, piece = keep_ref.shape[0], piece_ref.shape[0]
    tile = at_ref.shape[0] // len(outs)
    part_ref[:piece, :] = (piece_ref[...] + got_ref[rows : rows + piece, :].astype(F32)).astype(BF)
    lines = got_ref[rows + piece :, :].astype(F32)
    part_ref[piece:, :] = two_rows(line_ref[...] + lines[0:1] + lines[1:2])
    g = jnp.concatenate([keep_ref[...], got_ref[:rows, :]], axis=0)
    for p, out in enumerate(outs):
        out[...] = dot(at_ref[p * tile : (p + 1) * tile, :], g).astype(BF)


def total_of(refs):
    total = refs[0][...].astype(F32)
    for ref in refs[1:]:
        total = total + ref[...].astype(F32)
    return total


def piece_kernel(*refs):
    ins, (piece_ref, line_ref) = refs[:-2], refs[-2:]
    piece = piece_ref.shape[0]
    total = total_of(ins)
    piece_ref[...] = total[:piece].astype(BF)
    line_ref[...] = total[piece : piece + 1] + total[piece + 1 : piece + 2]


def last_kernel(n_row, n_col):
    def body(act_ref, line_ref, *refs):
        feats, pieces = refs[:n_row], refs[n_row : n_row + n_col]
        act_out, feat_out, weight_out, bias_out = refs[n_row + n_col :]
        piece = pieces[0].shape[0]
        c = lax.axis_index("col")
        act_out[...] = act_ref[...]
        bias_out[...] = line_ref[...]
        feat_out[...] = total_of(feats).astype(BF)
        for q, ref in enumerate(pieces):
            first = own_piece(jnp.bitwise_xor(c, q), n_col // 2) * piece
            weight_out[pl.ds(pl.multiple_of(first, piece), piece), :] = ref[...].astype(F32)

    return body


def swap(x, axis, n, by):
    return lax.ppermute(x, axis, [(i, i ^ by) for i in range(n)])


def deal(xs, axis):
    n = len(xs)
    got = {by: swap(xs[by], axis, n, by) for by in [*range(2, n), 1]}
    return [xs[0]] + [got[by] for by in range(1, n)]


def spread(x, axis, n):
    return deal([x] * n, axis)


def shards(n_row, n_col, features, adj_tiles, columns, counts, weight, bias_term, cotangent):
    tile, width = features.shape
    n_chip = n_col // 2
    piece = width // n_col
    half = n_chip * tile
    xs = spread(features, "row", n_row)
    cots = [cotangent] + [swap(cotangent, "col", n_col, 2 * v) for v in range(1, n_chip)]
    a, at = call(
        dense_kernel(n_chip),
        (shape(n_col * tile, n_row * tile), shape(n_row * tile, n_col * tile)),
        smem=2,
        count=3,
    )(columns.transpose(1, 2, 0), counts.T, adj_tiles)
    keep, send = call(
        forward_kernel(n_row),
        (shape(half, width, dtype=F32), shape(half, width)),
        count=n_row + n_chip,
    )(a, *xs, *cots[1:])
    chip = call(chip_kernel, shape(half, width), count=2)(keep, swap(send, "col", n_col, 1))
    sums = [chip] + [swap(chip, "col", n_col, 2 * v) for v in range(1, n_chip)]
    act, keep, mine, line, send = call(
        middle_kernel(n_chip),
        (
            shape(tile, width),
            shape(half, width),
            shape(piece, width, dtype=F32),
            shape(1, width, dtype=F32),
            shape(half + piece + PAD, width),
        ),
        count=2 + 2 * n_chip,
        scratch=[pltpu.VMEM((width, width), F32)],
    )(weight, bias_term.reshape(1, width), *cots, *sums)
    *feats, part = call(
        backward_kernel, (shape(tile, width),) * n_row + (shape(piece + PAD, width),), count=5
    )(at, keep, swap(send, "col", n_col, 1), mine, line)
    whole, line = call(
        piece_kernel, (shape(piece, width), shape(1, width, dtype=F32)), count=n_row
    )(*spread(part, "row", n_row))
    act, grad_features, grad_weight, grad_bias = call(
        last_kernel(n_row, n_col),
        (
            shape(tile, width),
            shape(tile, width),
            shape(width, width, dtype=F32),
            shape(1, width, dtype=F32),
        ),
        count=2 + n_row + n_col,
    )(act, line, *deal(feats, "row"), *spread(whole, "col", n_col))
    return act, grad_features, grad_weight, grad_bias.reshape(width)


def solution(mesh):
    n_row, n_col = mesh.shape["row"], mesh.shape["col"]
    placed = (
        P(("groups", "row", "col"), None),
        P(("groups", "row"), "col", None, None, None),
        P(("groups", "row"), "col", None),
        P(("groups", "row"), "col"),
        P(),
        P(),
        P(("groups", "row", "col"), None),
    )

    def body(*args):
        return shards(n_row, n_col, *args)

    return jax.shard_map(
        body,
        mesh=mesh,
        in_specs=placed,
        out_specs=(
            P(("groups", "row", "col"), None),
            P(("groups", "row", "col"), None),
            P("groups", None),
            P("groups"),
        ),
        check_vma=False,
    )
```

```python
import jax
import jax.numpy as jnp
from jax import lax
from jax.experimental import pallas as pl
from jax.experimental.pallas import tpu as pltpu
from jax.sharding import PartitionSpec as P

BF = jnp.bfloat16
F32 = jnp.float32
LIMIT = 48 * 1024 * 1024
PAD = 16


def dot(a, b, ca=1, cb=0):
    return lax.dot_general(a, b, (((ca,), (cb,)), ((), ())), preferred_element_type=F32)


def call(body, outs, smem=0, count=1, scratch=()):
    vm = pl.BlockSpec(memory_space=pltpu.VMEM)
    sm = pl.BlockSpec(memory_space=pltpu.SMEM)
    return pl.pallas_call(
        body,
        in_specs=[sm] * smem + [vm] * (count - smem),
        out_specs=jax.tree.map(lambda _: vm, outs),
        out_shape=outs,
        scratch_shapes=scratch,
        compiler_params=pltpu.CompilerParams(vmem_limit_bytes=LIMIT),
    )


def shape(*dims, dtype=BF):
    return jax.ShapeDtypeStruct(dims, dtype)


def own_piece(c, n_chip):
    return lax.rem(c, 2) * n_chip + lax.div(c, 2)


def dense_kernel(n_chip):
    def body(cols_ref, cnts_ref, tiles_ref, a_ref, at_ref):
        trows, _, slots, tile, _ = tiles_ref.shape
        r = lax.axis_index("row")
        c = lax.axis_index("col")
        a_ref[...] = jnp.zeros_like(a_ref)
        at_ref[...] = jnp.zeros_like(at_ref)

        def put(step, carry):
            t = step // slots
            k = step % slots

            @pl.when(k < cnts_ref[0, t])
            def _():
                q = own_piece(jnp.bitwise_xor(t, c), n_chip)
                p = jnp.bitwise_xor(cols_ref[0, k, t], r)
                here = tiles_ref[t, 0, k]
                qs = pl.ds(pl.multiple_of(q * tile, tile), tile)
                ps = pl.ds(pl.multiple_of(p * tile, tile), tile)
                a_ref[qs, ps] = here
                at_ref[ps, qs] = here.T

            return carry

        lax.fori_loop(0, trows * slots, put, 0)

    return body


def forward_kernel(n_row, n_cot):
    def body(a_ref, *refs):
        ins, (keep_ref, send_ref, *outs) = refs[:n_row], refs[n_row + n_cot :]
        for ref, out in zip(refs[n_row:], outs):
            out[...] = ref[...]
        half = keep_ref.shape[0]
        x = jnp.concatenate([ref[...] for ref in ins[::-1]], axis=0)
        send_ref[...] = dot(a_ref[half:, :], x).astype(BF)
        keep_ref[...] = dot(a_ref[:half, :], x)

    return body


def chip_kernel(keep_ref, got_ref, out_ref):
    out_ref[...] = (keep_ref[...] + got_ref[...].astype(F32)).astype(BF)


def two_rows(line):
    high = line.astype(BF).astype(F32)
    which = lax.broadcasted_iota(jnp.int32, (PAD, line.shape[1]), 0)
    return jnp.where(which == 0, high, jnp.where(which == 1, line - high, 0.0)).astype(BF)


def middle_kernel(n_chip):
    def body(w_ref, b_ref, *refs):
        cots, sums = refs[:n_chip], refs[n_chip : 2 * n_chip]
        act_ref, keep_ref, piece_ref, line_ref, send_ref, local_ref = refs[2 * n_chip :]
        tile, width = cots[0].shape
        rows = n_chip * tile
        piece = piece_ref.shape[0]
        c = lax.axis_index("col")
        blocks = []
        for u in range(n_chip):
            total = sums[0][u * tile : (u + 1) * tile, :].astype(F32)
            for v in range(1, n_chip):
                total = total + sums[v][(u ^ v) * tile : ((u ^ v) + 1) * tile, :].astype(F32)
            blocks.append(total.astype(BF))
        agg = jnp.concatenate(blocks, axis=0)
        cot = jnp.concatenate([ref[...] for ref in cots], axis=0).astype(F32)
        preact = dot(agg, w_ref[...]) + b_ref[...].astype(F32)
        sig = jax.nn.sigmoid(preact)
        act_ref[...] = (preact[:tile] * sig[:tile]).astype(BF)
        grad = (cot * (sig * (1.0 + preact * (1.0 - sig)))).astype(BF)
        gagg = dot(grad, w_ref[...], 1, 1).astype(BF)
        keep_ref[...] = gagg
        send_ref[:rows, :] = gagg
        local_ref[...] = dot(agg, grad, 0, 0)
        mine = pl.multiple_of(own_piece(c, n_chip) * piece, piece)
        other = pl.multiple_of(own_piece(jnp.bitwise_xor(c, 1), n_chip) * piece, piece)
        piece_ref[...] = local_ref[pl.ds(mine, piece), :]
        send_ref[rows : rows + piece, :] = local_ref[pl.ds(other, piece), :].astype(BF)
        line = jnp.sum(grad.astype(F32), axis=0, keepdims=True)
        line_ref[...] = line
        send_ref[rows + piece :, :] = two_rows(line)

    return body


def part_kernel(got_ref, piece_ref, line_ref, part_ref):
    piece = piece_ref.shape[0]
    rows = got_ref.shape[0] - piece - PAD
    part_ref[:piece, :] = (piece_ref[...] + got_ref[rows : rows + piece, :].astype(F32)).astype(BF)
    lines = got_ref[rows + piece :, :].astype(F32)
    part_ref[piece:, :] = two_rows(line_ref[...] + lines[0:1] + lines[1:2])


def backward_kernel(at_ref, keep_ref, got_ref, *outs):
    rows = keep_ref.shape[0]
    tile = at_ref.shape[0] // len(outs)
    g = jnp.concatenate([keep_ref[...], got_ref[:rows, :]], axis=0)
    for p, out in enumerate(outs):
        out[...] = dot(at_ref[p * tile : (p + 1) * tile, :], g).astype(BF)


def total_of(refs):
    total = refs[0][...].astype(F32)
    for ref in refs[1:]:
        total = total + ref[...].astype(F32)
    return total


def piece_kernel(*refs):
    ins, (piece_ref, line_ref) = refs[:-2], refs[-2:]
    piece = piece_ref.shape[0]
    total = total_of(ins)
    piece_ref[...] = total[:piece].astype(BF)
    line_ref[...] = total[piece : piece + 1] + total[piece + 1 : piece + 2]


def last_kernel(n_row, n_col):
    def body(act_ref, line_ref, *refs):
        feats, pieces = refs[:n_row], refs[n_row : n_row + n_col]
        act_out, feat_out, weight_out, bias_out = refs[n_row + n_col :]
        piece = pieces[0].shape[0]
        c = lax.axis_index("col")
        act_out[...] = act_ref[...]
        bias_out[...] = line_ref[...]
        feat_out[...] = total_of(feats).astype(BF)
        for q, ref in enumerate(pieces):
            first = own_piece(jnp.bitwise_xor(c, q), n_col // 2) * piece
            weight_out[pl.ds(pl.multiple_of(first, piece), piece), :] = ref[...].astype(F32)

    return body


def swap(x, axis, n, by):
    return lax.ppermute(x, axis, [(i, i ^ by) for i in range(n)])


def deal(xs, axis):
    n = len(xs)
    got = {by: swap(xs[by], axis, n, by) for by in [*range(2, n), 1]}
    return [xs[0]] + [got[by] for by in range(1, n)]


def spread(x, axis, n):
    return deal([x] * n, axis)


def shards(n_row, n_col, features, adj_tiles, columns, counts, weight, bias_term, cotangent):
    tile, width = features.shape
    n_chip = n_col // 2
    piece = width // n_col
    half = n_chip * tile
    xs = spread(features, "row", n_row)
    cots = [cotangent] + [swap(cotangent, "col", n_col, 2 * v) for v in range(1, n_chip)]
    a, at = call(
        dense_kernel(n_chip),
        (shape(n_col * tile, n_row * tile), shape(n_row * tile, n_col * tile)),
        smem=2,
        count=3,
    )(columns.transpose(1, 2, 0), counts.T, adj_tiles)
    keep, send, *cots[1:] = call(
        forward_kernel(n_row, n_chip - 1),
        (shape(half, width, dtype=F32), shape(half, width)) + (shape(tile, width),) * (n_chip - 1),
        count=n_row + n_chip,
    )(a, *xs[::-1], *cots[1:])
    chip = call(chip_kernel, shape(half, width), count=2)(keep, swap(send, "col", n_col, 1))
    sums = [chip] + [swap(chip, "col", n_col, 2 * v) for v in range(1, n_chip)]
    act, keep, mine, line, send = call(
        middle_kernel(n_chip),
        (
            shape(tile, width),
            shape(half, width),
            shape(piece, width, dtype=F32),
            shape(1, width, dtype=F32),
            shape(half + piece + PAD, width),
        ),
        count=2 + 2 * n_chip,
        scratch=[pltpu.VMEM((width, width), F32)],
    )(weight, bias_term.reshape(1, width), *cots, *sums)
    got = swap(send, "col", n_col, 1)
    part = call(part_kernel, shape(piece + PAD, width), count=3)(got, mine, line)
    feats = call(backward_kernel, (shape(tile, width),) * n_row, count=3)(at, keep, got)
    whole, line = call(
        piece_kernel, (shape(piece, width), shape(1, width, dtype=F32)), count=n_row
    )(*spread(part, "row", n_row)[::-1])
    act, grad_features, grad_weight, grad_bias = call(
        last_kernel(n_row, n_col),
        (
            shape(tile, width),
            shape(tile, width),
            shape(width, width, dtype=F32),
            shape(1, width, dtype=F32),
        ),
        count=2 + n_row + n_col,
    )(act, line, *deal(feats, "row")[::-1], *spread(whole, "col", n_col))
    return act, grad_features, grad_weight, grad_bias.reshape(width)


def solution(mesh):
    n_row, n_col = mesh.shape["row"], mesh.shape["col"]
    placed = (
        P(("groups", "row", "col"), None),
        P(("groups", "row"), "col", None, None, None),
        P(("groups", "row"), "col", None),
        P(("groups", "row"), "col"),
        P(),
        P(),
        P(("groups", "row", "col"), None),
    )

    def body(*args):
        return shards(n_row, n_col, *args)

    return jax.shard_map(
        body,
        mesh=mesh,
        in_specs=placed,
        out_specs=(
            P(("groups", "row", "col"), None),
            P(("groups", "row", "col"), None),
            P("groups", None),
            P("groups"),
        ),
        check_vma=False,
    )
```

```python
import jax
import jax.numpy as jnp
from jax import lax
from jax.experimental import pallas as pl
from jax.experimental.pallas import tpu as pltpu
from jax.sharding import PartitionSpec as P

BF = jnp.bfloat16
F32 = jnp.float32
LIMIT = 48 * 1024 * 1024
PAD = 16


def dot(a, b, ca=1, cb=0):
    return lax.dot_general(a, b, (((ca,), (cb,)), ((), ())), preferred_element_type=F32)


def call(body, outs, smem=0, count=1, scratch=()):
    vm = pl.BlockSpec(memory_space=pltpu.VMEM)
    sm = pl.BlockSpec(memory_space=pltpu.SMEM)
    return pl.pallas_call(
        body,
        in_specs=[sm] * smem + [vm] * (count - smem),
        out_specs=jax.tree.map(lambda _: vm, outs),
        out_shape=outs,
        scratch_shapes=scratch,
        compiler_params=pltpu.CompilerParams(vmem_limit_bytes=LIMIT),
    )


def shape(*dims, dtype=BF):
    return jax.ShapeDtypeStruct(dims, dtype)


def place_of(c, n_chip):
    return lax.rem(c, 2) * n_chip + lax.div(c, 2)


def dense_kernel(n_chip):
    def body(cols_ref, cnts_ref, tiles_ref, a_ref, at_ref):
        trows, _, slots, tile, _ = tiles_ref.shape
        r = lax.axis_index("row")
        c = lax.axis_index("col")
        a_ref[...] = jnp.zeros_like(a_ref)
        at_ref[...] = jnp.zeros_like(at_ref)

        def put(step, carry):
            t = step // slots
            k = step % slots

            @pl.when(k < cnts_ref[0, t])
            def _():
                q = place_of(jnp.bitwise_xor(t, c), n_chip)
                p = jnp.bitwise_xor(cols_ref[0, k, t], r)
                here = tiles_ref[t, 0, k]
                qs = pl.ds(pl.multiple_of(q * tile, tile), tile)
                ps = pl.ds(pl.multiple_of(p * tile, tile), tile)
                a_ref[qs, ps] = here
                at_ref[ps, qs] = here.T

            return carry

        lax.fori_loop(0, trows * slots, put, 0)

    return body


def forward_kernel(n_row, n_cot):
    def body(a_ref, *refs):
        ins, (keep_ref, send_ref, *outs) = refs[:n_row], refs[n_row + n_cot :]
        for ref, out in zip(refs[n_row:], outs):
            out[...] = ref[...]
        half = keep_ref.shape[0]
        x = jnp.concatenate([ref[...] for ref in ins[::-1]], axis=0)
        send_ref[...] = dot(a_ref[half:, :], x).astype(BF)
        keep_ref[...] = dot(a_ref[:half, :], x)

    return body


def chip_kernel(keep_ref, got_ref, out_ref):
    out_ref[...] = (keep_ref[...] + got_ref[...].astype(F32)).astype(BF)


def two_rows(line):
    high = line.astype(BF).astype(F32)
    which = lax.broadcasted_iota(jnp.int32, (PAD, line.shape[1]), 0)
    return jnp.where(which == 0, high, jnp.where(which == 1, line - high, 0.0)).astype(BF)


def middle_kernel(n_chip):
    def body(w_ref, b_ref, *refs):
        sums, cots = refs[:n_chip], refs[n_chip : 2 * n_chip]
        act_ref, keep_ref, part_ref, send_ref, agg_ref, grad_ref, local_ref = refs[2 * n_chip :]
        tile, width = cots[0].shape
        rows, piece = n_chip * tile, width // 2
        c = lax.axis_index("col")
        chip, core = lax.div(c, 2), lax.rem(c, 2)
        blocks = []
        for u in range(n_chip):
            total = sums[0][u * tile : (u + 1) * tile, :].astype(F32)
            for v in range(1, n_chip):
                total = total + sums[v][(u ^ v) * tile : ((u ^ v) + 1) * tile, :].astype(F32)
            blocks.append(total.astype(BF))
        agg = jnp.concatenate(blocks, axis=0)
        cot = jnp.concatenate([ref[...] for ref in cots], axis=0).astype(F32)
        preact = dot(agg, w_ref[...]) + b_ref[...].astype(F32)
        sig = jax.nn.sigmoid(preact)
        act_ref[...] = (preact[:tile] * sig[:tile]).astype(BF)
        grad = (cot * (sig * (1.0 + preact * (1.0 - sig)))).astype(BF)
        gagg = dot(grad, w_ref[...], 1, 1).astype(BF)
        keep_ref[...] = gagg
        send_ref[:rows, :] = gagg
        for u in range(n_chip):
            here = pl.ds(pl.multiple_of(jnp.bitwise_xor(chip, u) * tile, tile), tile)
            agg_ref[here, :] = blocks[u]
            grad_ref[here, :] = grad[u * tile : (u + 1) * tile, :]
        grad = grad_ref[...]
        local_ref[...] = dot(agg_ref[...], grad, 0, 0)
        mine = pl.multiple_of(core * piece, piece)
        other = pl.multiple_of((1 - core) * piece, piece)
        lines = two_rows(jnp.sum(grad.astype(F32), axis=0, keepdims=True))
        part_ref[:piece, :] = local_ref[pl.ds(mine, piece), :].astype(BF)
        part_ref[piece:, :] = lines
        send_ref[rows : rows + piece, :] = local_ref[pl.ds(other, piece), :].astype(BF)
        send_ref[rows + piece :, :] = lines

    return body


def sum_lines(refs, first):
    total = refs[0][first : first + PAD, :].astype(F32)
    for ref in refs[1:]:
        total = total + ref[first : first + PAD, :].astype(F32)
    return total[0:1] + total[1:2]


def backward_kernel(at_ref, keep_ref, got_ref, part_ref, *outs):
    rows, tile = keep_ref.shape[0], outs[0].shape[0] - PAD
    piece = part_ref.shape[0] - PAD
    mine, other = part_ref[...].astype(F32), got_ref[rows:, :].astype(F32)
    total = mine + other
    outs[1][tile + PAD :, :] = total[:piece].astype(BF)
    lines = two_rows(total[piece : piece + 1] + total[piece + 1 : piece + 2])
    g = jnp.concatenate([keep_ref[...], got_ref[:rows, :]], axis=0)
    for p, out in enumerate(outs):
        out[:tile, :] = dot(at_ref[p * tile : (p + 1) * tile, :], g).astype(BF)
        out[tile : tile + PAD, :] = lines


def pair_kernel(a_ref, b_ref, out_ref):
    first = a_ref.shape[0] - out_ref.shape[0]
    out_ref[...] = (a_ref[first:, :].astype(F32) + b_ref[first:, :].astype(F32)).astype(BF)


def sum_kernel(a_ref, b_ref, *refs):
    feats, (part_ref, feat_ref, line_ref) = refs[:-3], refs[-3:]
    part_ref[...] = (a_ref[...].astype(F32) + b_ref[...].astype(F32)).astype(BF)
    tile = feat_ref.shape[0]
    total = feats[0][:tile, :].astype(F32)
    for ref in feats[1:]:
        total = total + ref[:tile, :].astype(F32)
    feat_ref[...] = total.astype(BF)
    line_ref[...] = sum_lines(feats, tile)


def last_kernel(act_ref, feat_ref, line_ref, mine_ref, got_ref, *outs):
    act_out, feat_out, weight_out, bias_out = outs
    piece = mine_ref.shape[0]
    core = lax.rem(lax.axis_index("col"), 2)
    act_out[...] = act_ref[...]
    feat_out[...] = feat_ref[...]
    bias_out[...] = line_ref[...]
    mine = pl.multiple_of(core * piece, piece)
    other = pl.multiple_of((1 - core) * piece, piece)
    weight_out[pl.ds(mine, piece), :] = mine_ref[...].astype(F32)
    weight_out[pl.ds(other, piece), :] = got_ref[...].astype(F32)


def swap(x, axis, n, by):
    return lax.ppermute(x, axis, [(i, i ^ by) for i in range(n)])


def deal(xs, axis):
    n = len(xs)
    got = {by: swap(xs[by], axis, n, by) for by in range(1, n)}
    return [xs[0]] + [got[by] for by in range(1, n)]


def spread(x, axis, n):
    return deal([x] * n, axis)


def shards(n_row, n_col, features, adj_tiles, columns, counts, weight, bias_term, cotangent):
    tile, width = features.shape
    n_chip = n_col // 2
    piece = width // 2
    half = n_chip * tile
    xs = spread(features, "row", n_row)
    cots = [cotangent] + [swap(cotangent, "col", n_col, 2 * v) for v in range(1, n_chip)]
    a, at = call(
        dense_kernel(n_chip),
        (shape(n_col * tile, n_row * tile), shape(n_row * tile, n_col * tile)),
        smem=2,
        count=3,
    )(columns.transpose(1, 2, 0), counts.T, adj_tiles)
    keep, send, *cots[1:] = call(
        forward_kernel(n_row, n_chip - 1),
        (shape(half, width, dtype=F32), shape(half, width)) + (shape(tile, width),) * (n_chip - 1),
        count=n_row + n_chip,
    )(a, *xs[::-1], *cots[1:])
    chip = call(chip_kernel, shape(half, width), count=2)(keep, swap(send, "col", n_col, 1))
    sums = [chip] + [swap(chip, "col", n_col, 2 * v) for v in range(1, n_chip)]
    act, keep, part, send = call(
        middle_kernel(n_chip),
        (
            shape(tile, width),
            shape(half, width),
            shape(piece + PAD, width),
            shape(half + piece + PAD, width),
        ),
        count=2 + 2 * n_chip,
        scratch=[
            pltpu.VMEM((half, width), BF),
            pltpu.VMEM((half, width), BF),
            pltpu.VMEM((width, width), F32),
        ],
    )(weight, bias_term.reshape(1, width), *sums, *cots)
    messages = [shape(tile + PAD, width)] * n_row
    messages[1] = shape(tile + PAD + piece, width)
    sent = call(backward_kernel, tuple(messages), count=4)(
        at, keep, swap(send, "col", n_col, 1), part
    )
    feats = deal(sent, "row")
    part = call(pair_kernel, shape(piece, width), count=2)(sent[1], feats[1])
    by = 2
    while 2 * by < n_row:
        part = call(pair_kernel, shape(piece, width), count=2)(part, swap(part, "row", n_row, by))
        by *= 2
    line = shape(1, width, dtype=F32)
    part, grad_features, grad_bias = call(
        sum_kernel, (shape(piece, width), shape(tile, width), line), count=2 + n_row
    )(part, swap(part, "row", n_row, by), *feats)
    act, grad_features, grad_weight, grad_bias = call(
        last_kernel,
        (shape(tile, width), shape(tile, width), shape(width, width, dtype=F32), line),
        count=5,
    )(act, grad_features, grad_bias, part, swap(part, "col", n_col, 1))
    return act, grad_features, grad_weight, grad_bias.reshape(width)


def solution(mesh):
    n_row, n_col = mesh.shape["row"], mesh.shape["col"]
    placed = (
        P(("groups", "row", "col"), None),
        P(("groups", "row"), "col", None, None, None),
        P(("groups", "row"), "col", None),
        P(("groups", "row"), "col"),
        P(),
        P(),
        P(("groups", "row", "col"), None),
    )

    def body(*args):
        return shards(n_row, n_col, *args)

    return jax.shard_map(
        body,
        mesh=mesh,
        in_specs=placed,
        out_specs=(
            P(("groups", "row", "col"), None),
            P(("groups", "row", "col"), None),
            P("groups", None),
            P("groups"),
        ),
        check_vma=False,
    )
```

```python
import jax
import jax.numpy as jnp
from jax import lax
from jax.experimental import pallas as pl
from jax.experimental.pallas import tpu as pltpu
from jax.sharding import PartitionSpec as P

BF = jnp.bfloat16
F32 = jnp.float32
LIMIT = 48 * 1024 * 1024
PAD = 16


def dot(a, b, ca=1, cb=0):
    return lax.dot_general(a, b, (((ca,), (cb,)), ((), ())), preferred_element_type=F32)


def call(body, outs, smem=0, count=1, scratch=()):
    vm = pl.BlockSpec(memory_space=pltpu.VMEM)
    sm = pl.BlockSpec(memory_space=pltpu.SMEM)
    return pl.pallas_call(
        body,
        in_specs=[sm] * smem + [vm] * (count - smem),
        out_specs=jax.tree.map(lambda _: vm, outs),
        out_shape=outs,
        scratch_shapes=scratch,
        compiler_params=pltpu.CompilerParams(vmem_limit_bytes=LIMIT),
    )


def shape(*dims, dtype=BF):
    return jax.ShapeDtypeStruct(dims, dtype)


def place_of(c, n_chip):
    return lax.rem(c, 2) * n_chip + lax.div(c, 2)


def reversed_bits(p, n):
    total, bit = 0, 1
    while bit < n:
        total = 2 * total + lax.rem(lax.div(p, bit), 2)
        bit *= 2
    return total


def dense_kernel(n_chip, n_row):
    def body(cols_ref, cnts_ref, tiles_ref, a_ref, at_ref):
        trows, _, slots, tile, _ = tiles_ref.shape
        r = lax.axis_index("row")
        c = lax.axis_index("col")
        a_ref[...] = jnp.zeros_like(a_ref)
        at_ref[...] = jnp.zeros_like(at_ref)

        def put(step, carry):
            t = step // slots
            k = step % slots

            @pl.when(k < cnts_ref[0, t])
            def _():
                q = place_of(jnp.bitwise_xor(t, c), n_chip)
                p = jnp.bitwise_xor(cols_ref[0, k, t], r)
                here = tiles_ref[t, 0, k]
                qs = pl.ds(pl.multiple_of(q * tile, tile), tile)
                ps = pl.ds(pl.multiple_of(p * tile, tile), tile)
                a_ref[qs, ps] = here
                rs = pl.ds(pl.multiple_of(reversed_bits(p, n_row) * tile, tile), tile)
                at_ref[rs, qs] = here.T

            return carry

        lax.fori_loop(0, trows * slots, put, 0)

    return body


def forward_kernel(n_row, n_cot):
    def body(a_ref, *refs):
        ins, (keep_ref, send_ref, *outs) = refs[:n_row], refs[n_row + n_cot :]
        for ref, out in zip(refs[n_row:], outs):
            out[...] = ref[...]
        half = keep_ref.shape[0]
        x = jnp.concatenate([ref[...] for ref in ins[::-1]], axis=0)
        send_ref[...] = dot(a_ref[half:, :], x).astype(BF)
        keep_ref[...] = dot(a_ref[:half, :], x)

    return body


def chip_kernel(keep_ref, got_ref, out_ref):
    out_ref[...] = (keep_ref[...] + got_ref[...].astype(F32)).astype(BF)


def two_rows(line):
    high = line.astype(BF).astype(F32)
    which = lax.broadcasted_iota(jnp.int32, (PAD, line.shape[1]), 0)
    return jnp.where(which == 0, high, jnp.where(which == 1, line - high, 0.0)).astype(BF)


def middle_kernel(n_chip):
    def body(w_ref, b_ref, *refs):
        sums, cots = refs[:n_chip], refs[n_chip : 2 * n_chip]
        act_ref, keep_ref, part_ref, send_ref, agg_ref, grad_ref, local_ref = refs[2 * n_chip :]
        tile, width = cots[0].shape
        rows, piece = n_chip * tile, width // 2
        c = lax.axis_index("col")
        chip, core = lax.div(c, 2), lax.rem(c, 2)
        blocks = []
        for u in range(n_chip):
            total = sums[0][u * tile : (u + 1) * tile, :].astype(F32)
            for v in range(1, n_chip):
                total = total + sums[v][(u ^ v) * tile : ((u ^ v) + 1) * tile, :].astype(F32)
            blocks.append(total.astype(BF))
        agg = jnp.concatenate(blocks, axis=0)
        cot = jnp.concatenate([ref[...] for ref in cots], axis=0).astype(F32)
        preact = dot(agg, w_ref[...]) + b_ref[...].astype(F32)
        sig = jax.nn.sigmoid(preact)
        act_ref[...] = (preact[:tile] * sig[:tile]).astype(BF)
        grad = (cot * (sig * (1.0 + preact * (1.0 - sig)))).astype(BF)
        gagg = dot(grad, w_ref[...], 1, 1).astype(BF)
        keep_ref[:rows, :] = gagg
        send_ref[:rows, :] = gagg
        for u in range(n_chip):
            here = pl.ds(pl.multiple_of(jnp.bitwise_xor(chip, u) * tile, tile), tile)
            agg_ref[here, :] = blocks[u]
            grad_ref[here, :] = grad[u * tile : (u + 1) * tile, :]
        grad = grad_ref[...]
        local_ref[...] = dot(agg_ref[...], grad, 0, 0)
        mine = pl.multiple_of(core * piece, piece)
        other = pl.multiple_of((1 - core) * piece, piece)
        lines = two_rows(jnp.sum(grad.astype(F32), axis=0, keepdims=True))
        part_ref[...] = local_ref[pl.ds(mine, piece), :].astype(BF)
        keep_ref[rows:, :] = lines
        send_ref[rows : rows + PAD, :] = lines
        send_ref[rows + PAD :, :] = local_ref[pl.ds(other, piece), :].astype(BF)

    return body


def line_of(rows):
    rows = rows.astype(F32)
    return rows[0:1] + rows[1:2]


def part_kernel(part_ref, got_ref, out_ref):
    piece = out_ref.shape[0]
    first = got_ref.shape[0] - piece
    out_ref[...] = (part_ref[...].astype(F32) + got_ref[first:, :].astype(F32)).astype(BF)


def backward_kernel(at_ref, mine_ref, got_ref, keep_ref, send_ref):
    rows, half = mine_ref.shape[0] - PAD, keep_ref.shape[0] - PAD
    g = jnp.concatenate([mine_ref[:rows, :], got_ref[:rows, :]], axis=0)
    send_ref[:half, :] = dot(at_ref[half:, :], g).astype(BF)
    keep_ref[:half, :] = dot(at_ref[:half, :], g)
    line = two_rows(line_of(mine_ref[rows:, :]) + line_of(got_ref[rows : rows + PAD, :]))
    send_ref[half:, :] = line
    keep_ref[half:, :] = line.astype(F32)


def halve_kernel(in_ref, got_ref, keep_ref, send_ref):
    half, rows = keep_ref.shape[0] - PAD, in_ref.shape[0] - PAD
    send_ref[:half, :] = (in_ref[half:rows, :] + got_ref[half:rows, :].astype(F32)).astype(BF)
    keep_ref[:half, :] = in_ref[:half, :] + got_ref[:half, :].astype(F32)
    line = two_rows(line_of(in_ref[rows:, :]) + line_of(got_ref[rows:, :]))
    send_ref[half:, :] = line
    keep_ref[half:, :] = line.astype(F32)


def last_kernel(act_ref, feat_ref, more_ref, mine_ref, got_ref, *outs):
    act_out, feat_out, weight_out, bias_out = outs
    tile, piece = act_ref.shape[0], mine_ref.shape[0]
    core = lax.rem(lax.axis_index("col"), 2)
    act_out[...] = act_ref[...]
    feat_out[...] = (feat_ref[:tile, :] + more_ref[:tile, :].astype(F32)).astype(BF)
    bias_out[...] = line_of(feat_ref[tile:, :]) + line_of(more_ref[tile:, :])
    mine = pl.multiple_of(core * piece, piece)
    other = pl.multiple_of((1 - core) * piece, piece)
    weight_out[pl.ds(mine, piece), :] = mine_ref[...].astype(F32)
    weight_out[pl.ds(other, piece), :] = got_ref[...].astype(F32)


def swap(x, axis, n, by):
    return lax.ppermute(x, axis, [(i, i ^ by) for i in range(n)])


def deal(xs, axis):
    n = len(xs)
    got = {by: swap(xs[by], axis, n, by) for by in range(1, n)}
    return [xs[0]] + [got[by] for by in range(1, n)]


def spread(x, axis, n):
    return deal([x] * n, axis)


def shards(n_row, n_col, features, adj_tiles, columns, counts, weight, bias_term, cotangent):
    tile, width = features.shape
    n_chip = n_col // 2
    piece = width // 2
    half = n_chip * tile
    xs = spread(features, "row", n_row)
    cots = [cotangent] + [swap(cotangent, "col", n_col, 2 * v) for v in range(1, n_chip)]
    a, at = call(
        dense_kernel(n_chip, n_row),
        (shape(n_col * tile, n_row * tile), shape(n_row * tile, n_col * tile)),
        smem=2,
        count=3,
    )(columns.transpose(1, 2, 0), counts.T, adj_tiles)
    keep, send, *cots[1:] = call(
        forward_kernel(n_row, n_chip - 1),
        (shape(half, width, dtype=F32), shape(half, width)) + (shape(tile, width),) * (n_chip - 1),
        count=n_row + n_chip,
    )(a, *xs[::-1], *cots[1:])
    chip = call(chip_kernel, shape(half, width), count=2)(keep, swap(send, "col", n_col, 1))
    sums = [chip] + [swap(chip, "col", n_col, 2 * v) for v in range(1, n_chip)]
    act, keep, part, send = call(
        middle_kernel(n_chip),
        (
            shape(tile, width),
            shape(half + PAD, width),
            shape(piece, width),
            shape(half + PAD + piece, width),
        ),
        count=2 + 2 * n_chip,
        scratch=[
            pltpu.VMEM((half, width), BF),
            pltpu.VMEM((half, width), BF),
            pltpu.VMEM((width, width), F32),
        ],
    )(weight, bias_term.reshape(1, width), *sums, *cots)
    got = swap(send, "col", n_col, 1)
    part = call(part_kernel, shape(piece, width), count=2)(part, got)
    rows = n_row * tile // 2
    feats, send = call(
        backward_kernel, (shape(rows + PAD, width, dtype=F32), shape(rows + PAD, width)), count=3
    )(at, keep, got)
    by = 1
    while by < n_row:
        part = call(part_kernel, shape(piece, width), count=2)(
            part, swap(part, "row", n_row, by)
        )
        got = swap(send, "row", n_row, by)
        by *= 2
        if by < n_row:
            rows //= 2
            feats, send = call(
                halve_kernel, (shape(rows + PAD, width, dtype=F32), shape(rows + PAD, width)), count=2
            )(feats, got)
    act, grad_features, grad_weight, grad_bias = call(
        last_kernel,
        (
            shape(tile, width),
            shape(tile, width),
            shape(width, width, dtype=F32),
            shape(1, width, dtype=F32),
        ),
        count=5,
    )(act, feats, got, part, swap(part, "col", n_col, 1))
    return act, grad_features, grad_weight, grad_bias.reshape(width)


def solution(mesh):
    n_row, n_col = mesh.shape["row"], mesh.shape["col"]
    placed = (
        P(("groups", "row", "col"), None),
        P(("groups", "row"), "col", None, None, None),
        P(("groups", "row"), "col", None),
        P(("groups", "row"), "col"),
        P(),
        P(),
        P(("groups", "row", "col"), None),
    )

    def body(*args):
        return shards(n_row, n_col, *args)

    return jax.shard_map(
        body,
        mesh=mesh,
        in_specs=placed,
        out_specs=(
            P(("groups", "row", "col"), None),
            P(("groups", "row", "col"), None),
            P("groups", None),
            P("groups"),
        ),
        check_vma=False,
    )
```

```python
import jax
import jax.numpy as jnp
from jax import lax
from jax.experimental import pallas as pl
from jax.experimental.pallas import tpu as pltpu
from jax.sharding import PartitionSpec as P

BF = jnp.bfloat16
F32 = jnp.float32
LIMIT = 48 * 1024 * 1024
PAD = 16


def dot(a, b, ca=1, cb=0):
    return lax.dot_general(a, b, (((ca,), (cb,)), ((), ())), preferred_element_type=F32)


def call(body, outs, smem=0, count=1, scratch=()):
    vm = pl.BlockSpec(memory_space=pltpu.VMEM)
    sm = pl.BlockSpec(memory_space=pltpu.SMEM)
    return pl.pallas_call(
        body,
        in_specs=[sm] * smem + [vm] * (count - smem),
        out_specs=jax.tree.map(lambda _: vm, outs),
        out_shape=outs,
        scratch_shapes=scratch,
        compiler_params=pltpu.CompilerParams(vmem_limit_bytes=LIMIT),
    )


def shape(*dims, dtype=BF):
    return jax.ShapeDtypeStruct(dims, dtype)


def place_of(c, n_chip):
    return lax.rem(c, 2) * n_chip + lax.div(c, 2)


def reversed_bits(p, n):
    total, bit = 0, 1
    while bit < n:
        total = 2 * total + lax.rem(lax.div(p, bit), 2)
        bit *= 2
    return total


def dense_kernel(n_chip, n_row):
    def body(cols_ref, cnts_ref, tiles_ref, a_ref, at_ref):
        trows, _, slots, tile, _ = tiles_ref.shape
        r = lax.axis_index("row")
        c = lax.axis_index("col")
        a_ref[...] = jnp.zeros_like(a_ref)
        at_ref[...] = jnp.zeros_like(at_ref)

        def put(step, carry):
            t = step // slots
            k = step % slots

            @pl.when(k < cnts_ref[0, t])
            def _():
                q = place_of(jnp.bitwise_xor(t, c), n_chip)
                p = jnp.bitwise_xor(cols_ref[0, k, t], r)
                here = tiles_ref[t, 0, k]
                qs = pl.ds(pl.multiple_of(q * tile, tile), tile)
                ps = pl.ds(pl.multiple_of(p * tile, tile), tile)
                a_ref[qs, ps] = here
                rs = pl.ds(pl.multiple_of(reversed_bits(p, n_row) * tile, tile), tile)
                at_ref[rs, qs] = here.T

            return carry

        lax.fori_loop(0, trows * slots, put, 0)

    return body


def forward_kernel(n_row, n_cot):
    def body(a_ref, *refs):
        ins, (keep_ref, send_ref, *outs) = refs[:n_row], refs[n_row + n_cot :]
        for ref, out in zip(refs[n_row:], outs):
            out[...] = ref[...]
        half = keep_ref.shape[0]
        x = jnp.concatenate([ref[...] for ref in ins[::-1]], axis=0)
        send_ref[...] = dot(a_ref[half:, :], x).astype(BF)
        keep_ref[...] = dot(a_ref[:half, :], x)

    return body


def chip_kernel(keep_ref, got_ref, out_ref):
    out_ref[...] = (keep_ref[...] + got_ref[...].astype(F32)).astype(BF)


def two_rows(line):
    high = line.astype(BF).astype(F32)
    which = lax.broadcasted_iota(jnp.int32, (PAD, line.shape[1]), 0)
    return jnp.where(which == 0, high, jnp.where(which == 1, line - high, 0.0)).astype(BF)


def middle_kernel(n_chip):
    def body(w_ref, b_ref, *refs):
        sums, cots = refs[:n_chip], refs[n_chip : 2 * n_chip]
        act_ref, keep_ref, part_ref, send_ref, agg_ref, grad_ref, local_ref = refs[2 * n_chip :]
        tile, width = cots[0].shape
        rows, piece = n_chip * tile, width // 2
        c = lax.axis_index("col")
        chip, core = lax.div(c, 2), lax.rem(c, 2)
        blocks = []
        for u in range(n_chip):
            total = sums[0][u * tile : (u + 1) * tile, :].astype(F32)
            for v in range(1, n_chip):
                total = total + sums[v][(u ^ v) * tile : ((u ^ v) + 1) * tile, :].astype(F32)
            blocks.append(total.astype(BF))
        agg = jnp.concatenate(blocks, axis=0)
        cot = jnp.concatenate([ref[...] for ref in cots], axis=0).astype(F32)
        preact = dot(agg, w_ref[...]) + b_ref[...].astype(F32)
        sig = jax.nn.sigmoid(preact)
        act_ref[...] = (preact[:tile] * sig[:tile]).astype(BF)
        grad = (cot * (sig * (1.0 + preact * (1.0 - sig)))).astype(BF)
        gagg = dot(grad, w_ref[...], 1, 1).astype(BF)
        keep_ref[...] = gagg
        send_ref[:rows, :] = gagg
        for u in range(n_chip):
            here = pl.ds(pl.multiple_of(jnp.bitwise_xor(chip, u) * tile, tile), tile)
            agg_ref[here, :] = blocks[u]
            grad_ref[here, :] = grad[u * tile : (u + 1) * tile, :]
        grad = grad_ref[...]
        local_ref[...] = dot(agg_ref[...], grad, 0, 0)
        mine = pl.multiple_of(core * piece, piece)
        other = pl.multiple_of((1 - core) * piece, piece)
        lines = two_rows(jnp.sum(grad.astype(F32), axis=0, keepdims=True))
        part_ref[:piece, :] = local_ref[pl.ds(mine, piece), :].astype(BF)
        part_ref[piece:, :] = lines
        send_ref[rows : rows + piece, :] = local_ref[pl.ds(other, piece), :].astype(BF)
        send_ref[rows + piece :, :] = lines

    return body


def add_parts(a, b):
    piece = a.shape[0] - PAD
    a, b = a.astype(F32), b.astype(F32)
    total = a + b
    line = total[piece : piece + 1] + total[piece + 1 : piece + 2]
    return jnp.concatenate([total[:piece].astype(BF), two_rows(line)], axis=0)


def part_kernel(part_ref, got_ref, out_ref):
    first = got_ref.shape[0] - part_ref.shape[0]
    out_ref[...] = add_parts(part_ref[...], got_ref[first:, :])


def last_part_kernel(part_ref, got_ref, out_ref, line_ref):
    piece = out_ref.shape[0]
    total = part_ref[...].astype(F32) + got_ref[...].astype(F32)
    out_ref[...] = total[:piece].astype(BF)
    line_ref[...] = total[piece : piece + 1] + total[piece + 1 : piece + 2]


def backward_kernel(at_ref, mine_ref, got_ref, keep_ref, send_ref):
    rows, half = mine_ref.shape[0], keep_ref.shape[0]
    g = jnp.concatenate([mine_ref[...], got_ref[:rows, :]], axis=0)
    send_ref[...] = dot(at_ref[half:, :], g).astype(BF)
    keep_ref[...] = dot(at_ref[:half, :], g)


def halve_kernel(in_ref, got_ref, keep_ref, send_ref):
    half = keep_ref.shape[0]
    send_ref[...] = (in_ref[half:, :] + got_ref[half:, :].astype(F32)).astype(BF)
    keep_ref[...] = in_ref[:half, :] + got_ref[:half, :].astype(F32)


def last_kernel(act_ref, feat_ref, more_ref, line_ref, mine_ref, got_ref, *outs):
    act_out, feat_out, weight_out, bias_out = outs
    piece = mine_ref.shape[0]
    core = lax.rem(lax.axis_index("col"), 2)
    act_out[...] = act_ref[...]
    feat_out[...] = (feat_ref[...] + more_ref[...].astype(F32)).astype(BF)
    bias_out[...] = line_ref[...]
    mine = pl.multiple_of(core * piece, piece)
    other = pl.multiple_of((1 - core) * piece, piece)
    weight_out[pl.ds(mine, piece), :] = mine_ref[...].astype(F32)
    weight_out[pl.ds(other, piece), :] = got_ref[...].astype(F32)


def swap(x, axis, n, by):
    return lax.ppermute(x, axis, [(i, i ^ by) for i in range(n)])


def deal(xs, axis):
    n = len(xs)
    got = {by: swap(xs[by], axis, n, by) for by in range(1, n)}
    return [xs[0]] + [got[by] for by in range(1, n)]


def spread(x, axis, n):
    return deal([x] * n, axis)


def shards(n_row, n_col, features, adj_tiles, columns, counts, weight, bias_term, cotangent):
    tile, width = features.shape
    n_chip = n_col // 2
    piece = width // 2
    half = n_chip * tile
    xs = spread(features, "row", n_row)
    cots = [cotangent] + [swap(cotangent, "col", n_col, 2 * v) for v in range(1, n_chip)]
    a, at = call(
        dense_kernel(n_chip, n_row),
        (shape(n_col * tile, n_row * tile), shape(n_row * tile, n_col * tile)),
        smem=2,
        count=3,
    )(columns.transpose(1, 2, 0), counts.T, adj_tiles)
    keep, send, *cots[1:] = call(
        forward_kernel(n_row, n_chip - 1),
        (shape(half, width, dtype=F32), shape(half, width)) + (shape(tile, width),) * (n_chip - 1),
        count=n_row + n_chip,
    )(a, *xs[::-1], *cots[1:])
    chip = call(chip_kernel, shape(half, width), count=2)(keep, swap(send, "col", n_col, 1))
    sums = [chip] + [swap(chip, "col", n_col, 2 * v) for v in range(1, n_chip)]
    act, keep, part, send = call(
        middle_kernel(n_chip),
        (
            shape(tile, width),
            shape(half, width),
            shape(piece + PAD, width),
            shape(half + piece + PAD, width),
        ),
        count=2 + 2 * n_chip,
        scratch=[
            pltpu.VMEM((half, width), BF),
            pltpu.VMEM((half, width), BF),
            pltpu.VMEM((width, width), F32),
        ],
    )(weight, bias_term.reshape(1, width), *sums, *cots)
    got = swap(send, "col", n_col, 1)
    part = call(part_kernel, shape(piece + PAD, width), count=2)(part, got)
    rows = n_row * tile // 2
    feats, send = call(
        backward_kernel, (shape(rows, width, dtype=F32), shape(rows, width)), count=3
    )(at, keep, got)
    by = 1
    while by < n_row:
        other = swap(part, "row", n_row, by)
        got = swap(send, "row", n_row, by)
        by *= 2
        if by < n_row:
            part = call(part_kernel, shape(piece + PAD, width), count=2)(part, other)
            rows //= 2
            feats, send = call(
                halve_kernel, (shape(rows, width, dtype=F32), shape(rows, width)), count=2
            )(feats, got)
    part, grad_bias = call(
        last_part_kernel, (shape(piece, width), shape(1, width, dtype=F32)), count=2
    )(part, other)
    act, grad_features, grad_weight, grad_bias = call(
        last_kernel,
        (
            shape(tile, width),
            shape(tile, width),
            shape(width, width, dtype=F32),
            shape(1, width, dtype=F32),
        ),
        count=6,
    )(act, feats, got, grad_bias, part, swap(part, "col", n_col, 1))
    return act, grad_features, grad_weight, grad_bias.reshape(width)


def solution(mesh):
    n_row, n_col = mesh.shape["row"], mesh.shape["col"]
    placed = (
        P(("groups", "row", "col"), None),
        P(("groups", "row"), "col", None, None, None),
        P(("groups", "row"), "col", None),
        P(("groups", "row"), "col"),
        P(),
        P(),
        P(("groups", "row", "col"), None),
    )

    def body(*args):
        return shards(n_row, n_col, *args)

    return jax.shard_map(
        body,
        mesh=mesh,
        in_specs=placed,
        out_specs=(
            P(("groups", "row", "col"), None),
            P(("groups", "row", "col"), None),
            P("groups", None),
            P("groups"),
        ),
        check_vma=False,
    )
```

```python
import jax
import jax.numpy as jnp
from jax import lax
from jax.experimental import pallas as pl
from jax.experimental.pallas import tpu as pltpu
from jax.sharding import PartitionSpec as P

BF = jnp.bfloat16
F32 = jnp.float32
LIMIT = 48 * 1024 * 1024
PAD = 16


def dot(a, b, ca=1, cb=0):
    return lax.dot_general(a, b, (((ca,), (cb,)), ((), ())), preferred_element_type=F32)


def call(body, outs, smem=0, count=1, scratch=()):
    vm = pl.BlockSpec(memory_space=pltpu.VMEM)
    sm = pl.BlockSpec(memory_space=pltpu.SMEM)
    return pl.pallas_call(
        body,
        in_specs=[sm] * smem + [vm] * (count - smem),
        out_specs=jax.tree.map(lambda _: vm, outs),
        out_shape=outs,
        scratch_shapes=scratch,
        compiler_params=pltpu.CompilerParams(vmem_limit_bytes=LIMIT),
    )


def shape(*dims, dtype=BF):
    return jax.ShapeDtypeStruct(dims, dtype)


def place_of(c, n_chip):
    return lax.rem(c, 2) * n_chip + lax.div(c, 2)


def reversed_bits(p, n):
    total, bit = 0, 1
    while bit < n:
        total = 2 * total + lax.rem(lax.div(p, bit), 2)
        bit *= 2
    return total


def dense_kernel(n_chip, n_row):
    def body(cols_ref, cnts_ref, tiles_ref, a_ref, at_ref):
        trows, _, slots, tile, _ = tiles_ref.shape
        r = lax.axis_index("row")
        c = lax.axis_index("col")
        a_ref[...] = jnp.zeros_like(a_ref)
        at_ref[...] = jnp.zeros_like(at_ref)

        def put(step, carry):
            t = step // slots
            k = step % slots

            @pl.when(k < cnts_ref[0, t])
            def _():
                q = place_of(jnp.bitwise_xor(t, c), n_chip)
                p = jnp.bitwise_xor(cols_ref[0, k, t], r)
                here = tiles_ref[t, 0, k]
                qs = pl.ds(pl.multiple_of(q * tile, tile), tile)
                ps = pl.ds(pl.multiple_of(p * tile, tile), tile)
                a_ref[qs, ps] = here
                turned = jnp.where(lax.rem(c, 2) == 0, reversed_bits(p, n_row), p)
                rs = pl.ds(pl.multiple_of(turned * tile, tile), tile)
                at_ref[rs, qs] = here.T

            return carry

        lax.fori_loop(0, trows * slots, put, 0)

    return body


def forward_kernel(n_row, n_cot):
    def body(a_ref, *refs):
        ins, (keep_ref, send_ref, *outs) = refs[:n_row], refs[n_row + n_cot :]
        for ref, out in zip(refs[n_row:], outs):
            out[...] = ref[...]
        half = keep_ref.shape[0]
        x = jnp.concatenate([ref[...] for ref in ins[::-1]], axis=0)
        send_ref[...] = dot(a_ref[half:, :], x).astype(BF)
        keep_ref[...] = dot(a_ref[:half, :], x)

    return body


def chip_kernel(keep_ref, got_ref, out_ref):
    out_ref[...] = (keep_ref[...] + got_ref[...].astype(F32)).astype(BF)


def two_rows(line):
    high = line.astype(BF).astype(F32)
    which = lax.broadcasted_iota(jnp.int32, (PAD, line.shape[1]), 0)
    return jnp.where(which == 0, high, jnp.where(which == 1, line - high, 0.0)).astype(BF)


def middle_kernel(n_chip):
    def body(w_ref, b_ref, *refs):
        sums, cots = refs[:n_chip], refs[n_chip : 2 * n_chip]
        act_ref, keep_ref, part_ref, send_ref, agg_ref, grad_ref, local_ref = refs[2 * n_chip :]
        tile, width = cots[0].shape
        rows, piece = n_chip * tile, width // 2
        c = lax.axis_index("col")
        chip, core = lax.div(c, 2), lax.rem(c, 2)
        blocks = []
        for u in range(n_chip):
            total = sums[0][u * tile : (u + 1) * tile, :].astype(F32)
            for v in range(1, n_chip):
                total = total + sums[v][(u ^ v) * tile : ((u ^ v) + 1) * tile, :].astype(F32)
            blocks.append(total.astype(BF))
        agg = jnp.concatenate(blocks, axis=0)
        cot = jnp.concatenate([ref[...] for ref in cots], axis=0).astype(F32)
        preact = dot(agg, w_ref[...]) + b_ref[...].astype(F32)
        sig = jax.nn.sigmoid(preact)
        act_ref[...] = (preact[:tile] * sig[:tile]).astype(BF)
        grad = (cot * (sig * (1.0 + preact * (1.0 - sig)))).astype(BF)
        gagg = dot(grad, w_ref[...], 1, 1).astype(BF)
        keep_ref[...] = gagg
        send_ref[:rows, :] = gagg
        for u in range(n_chip):
            here = pl.ds(pl.multiple_of(jnp.bitwise_xor(chip, u) * tile, tile), tile)
            agg_ref[here, :] = blocks[u]
            grad_ref[here, :] = grad[u * tile : (u + 1) * tile, :]
        grad = grad_ref[...]
        local_ref[...] = dot(agg_ref[...], grad, 0, 0)
        mine = pl.multiple_of(core * piece, piece)
        other = pl.multiple_of((1 - core) * piece, piece)
        lines = two_rows(jnp.sum(grad.astype(F32), axis=0, keepdims=True))
        part_ref[:piece, :] = local_ref[pl.ds(mine, piece), :].astype(BF)
        part_ref[piece:, :] = lines
        send_ref[rows : rows + piece, :] = local_ref[pl.ds(other, piece), :].astype(BF)
        send_ref[rows + piece :, :] = lines

    return body


def add_parts(a, b):
    piece = a.shape[0] - PAD
    a, b = a.astype(F32), b.astype(F32)
    total = a + b
    line = total[piece : piece + 1] + total[piece + 1 : piece + 2]
    return jnp.concatenate([total[:piece].astype(BF), two_rows(line)], axis=0)


def part_kernel(part_ref, got_ref, out_ref):
    first = got_ref.shape[0] - part_ref.shape[0]
    out_ref[...] = add_parts(part_ref[...], got_ref[first:, :])


def last_part_kernel(part_ref, got_ref, out_ref, line_ref):
    piece = out_ref.shape[0]
    total = part_ref[...].astype(F32) + got_ref[...].astype(F32)
    out_ref[...] = total[:piece].astype(BF)
    line_ref[...] = total[piece : piece + 1] + total[piece + 1 : piece + 2]


def backward_kernel(at_ref, mine_ref, got_ref, keep_ref, send_ref):
    rows, half = mine_ref.shape[0], keep_ref.shape[0]
    g = jnp.concatenate([mine_ref[...], got_ref[:rows, :]], axis=0)
    send_ref[...] = dot(at_ref[half:, :], g).astype(BF)
    keep_ref[...] = dot(at_ref[:half, :], g)


def halve_kernel(in_ref, got_ref, keep_ref, send_ref):
    half = keep_ref.shape[0]
    send_ref[...] = (in_ref[half:, :] + got_ref[half:, :].astype(F32)).astype(BF)
    keep_ref[...] = in_ref[:half, :] + got_ref[:half, :].astype(F32)


def last_kernel(act_ref, feat_ref, more_ref, line_ref, mine_ref, got_ref, *outs):
    act_out, feat_out, weight_out, bias_out = outs
    piece = mine_ref.shape[0]
    core = lax.rem(lax.axis_index("col"), 2)
    act_out[...] = act_ref[...]
    feat_out[...] = (feat_ref[...] + more_ref[...].astype(F32)).astype(BF)
    bias_out[...] = line_ref[...]
    mine = pl.multiple_of(core * piece, piece)
    other = pl.multiple_of((1 - core) * piece, piece)
    weight_out[pl.ds(mine, piece), :] = mine_ref[...].astype(F32)
    weight_out[pl.ds(other, piece), :] = got_ref[...].astype(F32)


def swap(x, axis, n, by):
    return lax.ppermute(x, axis, [(i, i ^ by) for i in range(n)])


def step(x, n_row, n_col, by):
    pairs = []
    for i in range(n_row):
        for j in range(n_col):
            bit = by if j % 2 == 0 else n_row // 2 // by
            pairs.append((i * n_col + j, (i ^ bit) * n_col + j))
    return lax.ppermute(x, ("row", "col"), pairs)


def deal(xs, axis):
    n = len(xs)
    got = {by: swap(xs[by], axis, n, by) for by in range(1, n)}
    return [xs[0]] + [got[by] for by in range(1, n)]


def spread(x, axis, n):
    return deal([x] * n, axis)


def shards(n_row, n_col, features, adj_tiles, columns, counts, weight, bias_term, cotangent):
    tile, width = features.shape
    n_chip = n_col // 2
    piece = width // 2
    half = n_chip * tile
    xs = spread(features, "row", n_row)
    cots = [cotangent] + [swap(cotangent, "col", n_col, 2 * v) for v in range(1, n_chip)]
    a, at = call(
        dense_kernel(n_chip, n_row),
        (shape(n_col * tile, n_row * tile), shape(n_row * tile, n_col * tile)),
        smem=2,
        count=3,
    )(columns.transpose(1, 2, 0), counts.T, adj_tiles)
    keep, send, *cots[1:] = call(
        forward_kernel(n_row, n_chip - 1),
        (shape(half, width, dtype=F32), shape(half, width)) + (shape(tile, width),) * (n_chip - 1),
        count=n_row + n_chip,
    )(a, *xs[::-1], *cots[1:])
    chip = call(chip_kernel, shape(half, width), count=2)(keep, swap(send, "col", n_col, 1))
    sums = [chip] + [swap(chip, "col", n_col, 2 * v) for v in range(1, n_chip)]
    act, keep, part, send = call(
        middle_kernel(n_chip),
        (
            shape(tile, width),
            shape(half, width),
            shape(piece + PAD, width),
            shape(half + piece + PAD, width),
        ),
        count=2 + 2 * n_chip,
        scratch=[
            pltpu.VMEM((half, width), BF),
            pltpu.VMEM((half, width), BF),
            pltpu.VMEM((width, width), F32),
        ],
    )(weight, bias_term.reshape(1, width), *sums, *cots)
    got = swap(send, "col", n_col, 1)
    part = call(part_kernel, shape(piece + PAD, width), count=2)(part, got)
    rows = n_row * tile // 2
    feats, send = call(
        backward_kernel, (shape(rows, width, dtype=F32), shape(rows, width)), count=3
    )(at, keep, got)
    by = 1
    while by < n_row:
        other = step(part, n_row, n_col, by)
        got = step(send, n_row, n_col, by)
        by *= 2
        if by < n_row:
            part = call(part_kernel, shape(piece + PAD, width), count=2)(part, other)
            rows //= 2
            feats, send = call(
                halve_kernel, (shape(rows, width, dtype=F32), shape(rows, width)), count=2
            )(feats, got)
    part, grad_bias = call(
        last_part_kernel, (shape(piece, width), shape(1, width, dtype=F32)), count=2
    )(part, other)
    act, grad_features, grad_weight, grad_bias = call(
        last_kernel,
        (
            shape(tile, width),
            shape(tile, width),
            shape(width, width, dtype=F32),
            shape(1, width, dtype=F32),
        ),
        count=6,
    )(act, feats, got, grad_bias, part, swap(part, "col", n_col, 1))
    return act, grad_features, grad_weight, grad_bias.reshape(width)


def solution(mesh):
    n_row, n_col = mesh.shape["row"], mesh.shape["col"]
    placed = (
        P(("groups", "row", "col"), None),
        P(("groups", "row"), "col", None, None, None),
        P(("groups", "row"), "col", None),
        P(("groups", "row"), "col"),
        P(),
        P(),
        P(("groups", "row", "col"), None),
    )

    def body(*args):
        return shards(n_row, n_col, *args)

    return jax.shard_map(
        body,
        mesh=mesh,
        in_specs=placed,
        out_specs=(
            P(("groups", "row", "col"), None),
            P(("groups", "row", "col"), None),
            P("groups", None),
            P("groups"),
        ),
        check_vma=False,
    )
```

```python
import jax
import jax.numpy as jnp
from jax import lax
from jax.experimental import pallas as pl
from jax.experimental.pallas import tpu as pltpu
from jax.sharding import PartitionSpec as P

BF = jnp.bfloat16
F32 = jnp.float32
LIMIT = 48 * 1024 * 1024
PAD = 16


def dot(a, b, ca=1, cb=0):
    return lax.dot_general(a, b, (((ca,), (cb,)), ((), ())), preferred_element_type=F32)


def call(body, outs, smem=0, count=1, scratch=()):
    vm = pl.BlockSpec(memory_space=pltpu.VMEM)
    sm = pl.BlockSpec(memory_space=pltpu.SMEM)
    return pl.pallas_call(
        body,
        in_specs=[sm] * smem + [vm] * (count - smem),
        out_specs=jax.tree.map(lambda _: vm, outs),
        out_shape=outs,
        scratch_shapes=scratch,
        compiler_params=pltpu.CompilerParams(vmem_limit_bytes=LIMIT),
    )


def shape(*dims, dtype=BF):
    return jax.ShapeDtypeStruct(dims, dtype)


def place_of(c, n_chip):
    return lax.rem(c, 2) * n_chip + lax.div(c, 2)


def reversed_bits(p, n):
    total, bit = 0, 1
    while bit < n:
        total = 2 * total + lax.rem(lax.div(p, bit), 2)
        bit *= 2
    return total


def dense_kernel(n_chip, n_row):
    def body(cols_ref, cnts_ref, tiles_ref, a_ref, at_ref):
        trows, _, slots, tile, _ = tiles_ref.shape
        r = lax.axis_index("row")
        c = lax.axis_index("col")
        a_ref[...] = jnp.zeros_like(a_ref)
        at_ref[...] = jnp.zeros_like(at_ref)

        def put(step, carry):
            t = step // slots
            k = step % slots

            @pl.when(k < cnts_ref[0, t])
            def _():
                q = place_of(jnp.bitwise_xor(t, c), n_chip)
                p = jnp.bitwise_xor(cols_ref[0, k, t], r)
                here = tiles_ref[t, 0, k]
                qs = pl.ds(pl.multiple_of(q * tile, tile), tile)
                ps = pl.ds(pl.multiple_of(p * tile, tile), tile)
                a_ref[qs, ps] = here
                turned = jnp.where(lax.rem(c, 2) == 0, reversed_bits(p, n_row), p)
                rs = pl.ds(pl.multiple_of(turned * tile, tile), tile)
                at_ref[rs, qs] = here.T

            return carry

        lax.fori_loop(0, trows * slots, put, 0)

    return body


def forward_kernel(n_row, n_cot):
    def body(a_ref, *refs):
        ins, (keep_ref, send_ref, *outs) = refs[:n_row], refs[n_row + n_cot :]
        for ref, out in zip(refs[n_row:], outs):
            out[...] = ref[...]
        half = keep_ref.shape[0]
        x = jnp.concatenate([ref[...] for ref in ins[::-1]], axis=0)
        send_ref[...] = dot(a_ref[half:, :], x).astype(BF)
        keep_ref[...] = dot(a_ref[:half, :], x)

    return body


def chip_kernel(keep_ref, got_ref, out_ref):
    out_ref[...] = (keep_ref[...] + got_ref[...].astype(F32)).astype(BF)


def two_rows(line):
    high = line.astype(BF).astype(F32)
    which = lax.broadcasted_iota(jnp.int32, (PAD, line.shape[1]), 0)
    return jnp.where(which == 0, high, jnp.where(which == 1, line - high, 0.0)).astype(BF)


def middle_kernel(n_chip):
    def body(w_ref, b_ref, *refs):
        sums, cots = refs[:n_chip], refs[n_chip : 2 * n_chip]
        act_ref, keep_ref, part_ref, send_ref, agg_ref, grad_ref, local_ref = refs[2 * n_chip :]
        tile, width = cots[0].shape
        rows, piece = n_chip * tile, width // 2
        c = lax.axis_index("col")
        chip, core = lax.div(c, 2), lax.rem(c, 2)
        blocks = []
        for u in range(n_chip):
            total = sums[0][u * tile : (u + 1) * tile, :].astype(F32)
            for v in range(1, n_chip):
                total = total + sums[v][(u ^ v) * tile : ((u ^ v) + 1) * tile, :].astype(F32)
            blocks.append(total.astype(BF))
        agg = jnp.concatenate(blocks, axis=0)
        cot = jnp.concatenate([ref[...] for ref in cots], axis=0).astype(F32)
        preact = dot(agg, w_ref[...]) + b_ref[...].astype(F32)
        sig = jax.nn.sigmoid(preact)
        act_ref[...] = (preact[:tile] * sig[:tile]).astype(BF)
        grad = (cot * (sig * (1.0 + preact * (1.0 - sig)))).astype(BF)
        gagg = dot(grad, w_ref[...], 1, 1).astype(BF)
        keep_ref[:rows, :] = gagg
        send_ref[:rows, :] = gagg
        for u in range(n_chip):
            here = pl.ds(pl.multiple_of(jnp.bitwise_xor(chip, u) * tile, tile), tile)
            agg_ref[here, :] = blocks[u]
            grad_ref[here, :] = grad[u * tile : (u + 1) * tile, :]
        grad = grad_ref[...]
        local_ref[...] = dot(agg_ref[...], grad, 0, 0)
        mine = pl.multiple_of(core * piece, piece)
        other = pl.multiple_of((1 - core) * piece, piece)
        lines = two_rows(jnp.sum(grad.astype(F32), axis=0, keepdims=True))
        part_ref[...] = local_ref[pl.ds(mine, piece), :].astype(BF)
        keep_ref[rows:, :] = lines
        send_ref[rows : rows + PAD, :] = lines
        send_ref[rows + PAD :, :] = local_ref[pl.ds(other, piece), :].astype(BF)

    return body


def line_of(ref):
    rows = ref[ref.shape[0] - PAD :, :].astype(F32)
    return rows[0:1] + rows[1:2]


def part_kernel(part_ref, got_ref, out_ref):
    piece = out_ref.shape[0]
    first = got_ref.shape[0] - piece
    out_ref[...] = (part_ref[...].astype(F32) + got_ref[first:, :].astype(F32)).astype(BF)


def backward_kernel(at_ref, mine_ref, got_ref, keep_ref, stay_ref, pass_ref):
    rows, first, size = mine_ref.shape[0] - PAD, keep_ref.shape[0], stay_ref.shape[0]
    g = jnp.concatenate([mine_ref[:rows, :], got_ref[:rows, :]], axis=0)
    pass_ref[:size, :] = dot(at_ref[first + size :, :], g).astype(BF)
    other = got_ref[rows : rows + PAD, :].astype(F32)
    pass_ref[size:, :] = two_rows(line_of(mine_ref) + (other[0:1] + other[1:2]))
    stay_ref[...] = dot(at_ref[first : first + size, :], g).astype(BF)
    keep_ref[...] = dot(at_ref[:first, :], g)


def sum_of(refs, firsts, rows):
    total = None
    for ref, first in zip(refs, firsts):
        term = ref[first : first + rows, :].astype(F32)
        total = term if total is None else total + term
    return total


def range_kernel(firsts, with_line):
    def body(sent_ref, got_ref, *refs):
        out_ref = refs[-1]
        size = out_ref.shape[0] - PAD * with_line
        out_ref[:size, :] = sum_of(refs[:-1], firsts, size).astype(BF)
        if with_line:
            out_ref[size:, :] = two_rows(line_of(sent_ref) + line_of(got_ref))

    return body


def last_kernel(act_ref, sent_ref, line_ref, mine_ref, got_ref, *refs):
    terms, (act_out, feat_out, weight_out, bias_out) = refs[:-4], refs[-4:]
    piece = mine_ref.shape[0]
    core = lax.rem(lax.axis_index("col"), 2)
    act_out[...] = act_ref[...]
    feat_out[...] = sum_of(terms, [0] * len(terms), feat_out.shape[0]).astype(BF)
    bias_out[...] = line_of(sent_ref) + line_of(line_ref)
    mine = pl.multiple_of(core * piece, piece)
    other = pl.multiple_of((1 - core) * piece, piece)
    weight_out[pl.ds(mine, piece), :] = mine_ref[...].astype(F32)
    weight_out[pl.ds(other, piece), :] = got_ref[...].astype(F32)


def swap(x, axis, n, by):
    return lax.ppermute(x, axis, [(i, i ^ by) for i in range(n)])


def step(x, n_row, n_col, by):
    pairs = []
    for i in range(n_row):
        for j in range(n_col):
            bit = by if j % 2 == 0 else n_row // 2 // by
            pairs.append((i * n_col + j, (i ^ bit) * n_col + j))
    return lax.ppermute(x, ("row", "col"), pairs)


def deal(xs, axis):
    n = len(xs)
    got = {by: swap(xs[by], axis, n, by) for by in range(1, n)}
    return [xs[0]] + [got[by] for by in range(1, n)]


def spread(x, axis, n):
    return deal([x] * n, axis)


def shards(n_row, n_col, features, adj_tiles, columns, counts, weight, bias_term, cotangent):
    tile, width = features.shape
    n_chip = n_col // 2
    piece = width // 2
    half = n_chip * tile
    xs = spread(features, "row", n_row)
    cots = [cotangent] + [swap(cotangent, "col", n_col, 2 * v) for v in range(1, n_chip)]
    a, at = call(
        dense_kernel(n_chip, n_row),
        (shape(n_col * tile, n_row * tile), shape(n_row * tile, n_col * tile)),
        smem=2,
        count=3,
    )(columns.transpose(1, 2, 0), counts.T, adj_tiles)
    keep, send, *cots[1:] = call(
        forward_kernel(n_row, n_chip - 1),
        (shape(half, width, dtype=F32), shape(half, width)) + (shape(tile, width),) * (n_chip - 1),
        count=n_row + n_chip,
    )(a, *xs[::-1], *cots[1:])
    chip = call(chip_kernel, shape(half, width), count=2)(keep, swap(send, "col", n_col, 1))
    sums = [chip] + [swap(chip, "col", n_col, 2 * v) for v in range(1, n_chip)]
    act, keep, part, send = call(
        middle_kernel(n_chip),
        (
            shape(tile, width),
            shape(half + PAD, width),
            shape(piece, width),
            shape(half + PAD + piece, width),
        ),
        count=2 + 2 * n_chip,
        scratch=[
            pltpu.VMEM((half, width), BF),
            pltpu.VMEM((half, width), BF),
            pltpu.VMEM((width, width), F32),
        ],
    )(weight, bias_term.reshape(1, width), *sums, *cots)
    got = swap(send, "col", n_col, 1)
    part = call(part_kernel, shape(piece, width), count=2)(part, got)
    live = n_row * tile // 2
    size = live // 2
    keep, *sends = call(
        backward_kernel,
        (shape(live, width, dtype=F32), shape(size, width), shape(size + PAD, width)),
        count=3,
    )(at, keep, got)
    terms, by = [(keep, 0, live)], 1
    while True:
        other = step(part, n_row, n_col, by)
        sent, gots = sends[-1], [step(x, n_row, n_col, by) for x in reversed(sends)][::-1]
        terms += [(x, i * size, size) for i, x in enumerate(gots)]
        part = call(part_kernel, shape(piece, width), count=2)(part, other)
        by *= 2
        if by == n_row:
            break
        live //= 2
        size = live if live == tile else live // 2
        sends = []
        for first in range(live, 2 * live, size):
            over = [(x, first - at) for x, at, rows in terms if at <= first < at + rows]
            last = first + size == 2 * live
            sends.append(
                call(
                    range_kernel([at for _, at in over], last),
                    shape(size + PAD * last, width),
                    count=2 + len(over),
                )(sent, gots[-1], *[x for x, _ in over])
            )
        terms = [(x, at, rows) for x, at, rows in terms if at < live]
    act, grad_features, grad_weight, grad_bias = call(
        last_kernel,
        (
            shape(tile, width),
            shape(tile, width),
            shape(width, width, dtype=F32),
            shape(1, width, dtype=F32),
        ),
        count=5 + len(terms),
    )(act, sent, gots[-1], part, swap(part, "col", n_col, 1), *[x for x, _, _ in terms])
    return act, grad_features, grad_weight, grad_bias.reshape(width)


def solution(mesh):
    n_row, n_col = mesh.shape["row"], mesh.shape["col"]
    placed = (
        P(("groups", "row", "col"), None),
        P(("groups", "row"), "col", None, None, None),
        P(("groups", "row"), "col", None),
        P(("groups", "row"), "col"),
        P(),
        P(),
        P(("groups", "row", "col"), None),
    )

    def body(*args):
        return shards(n_row, n_col, *args)

    return jax.shard_map(
        body,
        mesh=mesh,
        in_specs=placed,
        out_specs=(
            P(("groups", "row", "col"), None),
            P(("groups", "row", "col"), None),
            P("groups", None),
            P("groups"),
        ),
        check_vma=False,
    )
```

```python
import jax
import jax.numpy as jnp
from jax import lax
from jax.experimental import pallas as pl
from jax.experimental.pallas import tpu as pltpu
from jax.sharding import PartitionSpec as P

BF = jnp.bfloat16
F32 = jnp.float32
LIMIT = 48 * 1024 * 1024
PAD = 16


def dot(a, b, ca=1, cb=0):
    return lax.dot_general(a, b, (((ca,), (cb,)), ((), ())), preferred_element_type=F32)


def call(body, outs, smem=0, count=1, scratch=()):
    vm = pl.BlockSpec(memory_space=pltpu.VMEM)
    sm = pl.BlockSpec(memory_space=pltpu.SMEM)
    return pl.pallas_call(
        body,
        in_specs=[sm] * smem + [vm] * (count - smem),
        out_specs=jax.tree.map(lambda _: vm, outs),
        out_shape=outs,
        scratch_shapes=scratch,
        compiler_params=pltpu.CompilerParams(vmem_limit_bytes=LIMIT),
    )


def shape(*dims, dtype=BF):
    return jax.ShapeDtypeStruct(dims, dtype)


def place_of(c, n_chip):
    return lax.rem(c, 2) * n_chip + lax.div(c, 2)


def reversed_bits(p, n):
    total, bit = 0, 1
    while bit < n:
        total = 2 * total + lax.rem(lax.div(p, bit), 2)
        bit *= 2
    return total


def dense_kernel(n_chip):
    def body(cols_ref, cnts_ref, tiles_ref, a_ref):
        trows, _, slots, tile, _ = tiles_ref.shape
        r = lax.axis_index("row")
        c = lax.axis_index("col")
        a_ref[...] = jnp.zeros_like(a_ref)

        def put(step, carry):
            t = step // slots
            k = step % slots

            @pl.when(k < cnts_ref[0, t])
            def _():
                q = place_of(jnp.bitwise_xor(t, c), n_chip)
                p = jnp.bitwise_xor(cols_ref[0, k, t], r)
                qs = pl.ds(pl.multiple_of(q * tile, tile), tile)
                ps = pl.ds(pl.multiple_of(p * tile, tile), tile)
                a_ref[qs, ps] = tiles_ref[t, 0, k]

            return carry

        lax.fori_loop(0, trows * slots, put, 0)

    return body


def transpose_kernel(n_row):
    def body(a_ref, at_ref):
        tile = at_ref.shape[0] // n_row
        core = lax.rem(lax.axis_index("col"), 2)

        def turn(p, carry):
            place = jnp.where(core == 0, reversed_bits(p, n_row), p)
            here = a_ref[:, pl.ds(pl.multiple_of(p * tile, tile), tile)]
            at_ref[pl.ds(pl.multiple_of(place * tile, tile), tile), :] = here.T
            return carry

        lax.fori_loop(0, n_row, turn, 0)

    return body


def forward_kernel(n_row, n_cot):
    def body(a_ref, *refs):
        ins, (keep_ref, send_ref, *outs) = refs[:n_row], refs[n_row + n_cot :]
        for ref, out in zip(refs[n_row:], outs):
            out[...] = ref[...]
        half = keep_ref.shape[0]
        x = jnp.concatenate([ref[...] for ref in ins[::-1]], axis=0)
        send_ref[...] = dot(a_ref[half:, :], x).astype(BF)
        keep_ref[...] = dot(a_ref[:half, :], x)

    return body


def chip_kernel(keep_ref, got_ref, out_ref):
    out_ref[...] = (keep_ref[...] + got_ref[...].astype(F32)).astype(BF)


def two_rows(line):
    high = line.astype(BF).astype(F32)
    which = lax.broadcasted_iota(jnp.int32, (PAD, line.shape[1]), 0)
    return jnp.where(which == 0, high, jnp.where(which == 1, line - high, 0.0)).astype(BF)


def middle_kernel(n_chip):
    def body(w_ref, b_ref, *refs):
        sums, cots = refs[:n_chip], refs[n_chip : 2 * n_chip]
        act_ref, keep_ref, part_ref, send_ref, agg_ref, grad_ref, local_ref = refs[2 * n_chip + 1 :]
        tile, width = cots[0].shape
        rows, piece = n_chip * tile, width // 2
        c = lax.axis_index("col")
        chip, core = lax.div(c, 2), lax.rem(c, 2)
        blocks = []
        for u in range(n_chip):
            total = sums[0][u * tile : (u + 1) * tile, :].astype(F32)
            for v in range(1, n_chip):
                total = total + sums[v][(u ^ v) * tile : ((u ^ v) + 1) * tile, :].astype(F32)
            blocks.append(total.astype(BF))
        agg = jnp.concatenate(blocks, axis=0)
        cot = jnp.concatenate([ref[...] for ref in cots], axis=0).astype(F32)
        preact = dot(agg, w_ref[...]) + b_ref[...].astype(F32)
        sig = jax.nn.sigmoid(preact)
        act_ref[...] = (preact[:tile] * sig[:tile]).astype(BF)
        grad = (cot * (sig * (1.0 + preact * (1.0 - sig)))).astype(BF)
        gagg = dot(grad, w_ref[...], 1, 1).astype(BF)
        keep_ref[:rows, :] = gagg
        send_ref[:rows, :] = gagg
        for u in range(n_chip):
            here = pl.ds(pl.multiple_of(jnp.bitwise_xor(chip, u) * tile, tile), tile)
            agg_ref[here, :] = blocks[u]
            grad_ref[here, :] = grad[u * tile : (u + 1) * tile, :]
        grad = grad_ref[...]
        local_ref[...] = dot(agg_ref[...], grad, 0, 0)
        mine = pl.multiple_of(core * piece, piece)
        other = pl.multiple_of((1 - core) * piece, piece)
        lines = two_rows(jnp.sum(grad.astype(F32), axis=0, keepdims=True))
        part_ref[...] = local_ref[pl.ds(mine, piece), :].astype(BF)
        keep_ref[rows:, :] = lines
        send_ref[rows : rows + PAD, :] = lines
        send_ref[rows + PAD :, :] = local_ref[pl.ds(other, piece), :].astype(BF)

    return body


def line_of(ref):
    rows = ref[ref.shape[0] - PAD :, :].astype(F32)
    return rows[0:1] + rows[1:2]


def part_kernel(part_ref, got_ref, out_ref):
    piece = out_ref.shape[0]
    first = got_ref.shape[0] - piece
    out_ref[...] = (part_ref[...].astype(F32) + got_ref[first:, :].astype(F32)).astype(BF)


def backward_kernel(at_ref, mine_ref, got_ref, keep_ref, stay_ref, pass_ref):
    rows, first, size = mine_ref.shape[0] - PAD, keep_ref.shape[0], stay_ref.shape[0]
    g = jnp.concatenate([mine_ref[:rows, :], got_ref[:rows, :]], axis=0)
    pass_ref[:size, :] = dot(at_ref[first + size :, :], g).astype(BF)
    other = got_ref[rows : rows + PAD, :].astype(F32)
    pass_ref[size:, :] = two_rows(line_of(mine_ref) + (other[0:1] + other[1:2]))
    stay_ref[...] = dot(at_ref[first : first + size, :], g).astype(BF)
    keep_ref[...] = dot(at_ref[:first, :], g)


def sum_of(refs, firsts, rows):
    total = None
    for ref, first in zip(refs, firsts):
        term = ref[first : first + rows, :].astype(F32)
        total = term if total is None else total + term
    return total


def range_kernel(firsts, with_line):
    def body(sent_ref, got_ref, *refs):
        out_ref = refs[-1]
        size = out_ref.shape[0] - PAD * with_line
        out_ref[:size, :] = sum_of(refs[:-1], firsts, size).astype(BF)
        if with_line:
            out_ref[size:, :] = two_rows(line_of(sent_ref) + line_of(got_ref))

    return body


def last_kernel(act_ref, sent_ref, line_ref, mine_ref, got_ref, *refs):
    terms, (act_out, feat_out, weight_out, bias_out) = refs[:-4], refs[-4:]
    piece = mine_ref.shape[0]
    core = lax.rem(lax.axis_index("col"), 2)
    act_out[...] = act_ref[...]
    feat_out[...] = sum_of(terms, [0] * len(terms), feat_out.shape[0]).astype(BF)
    bias_out[...] = line_of(sent_ref) + line_of(line_ref)
    mine = pl.multiple_of(core * piece, piece)
    other = pl.multiple_of((1 - core) * piece, piece)
    weight_out[pl.ds(mine, piece), :] = mine_ref[...].astype(F32)
    weight_out[pl.ds(other, piece), :] = got_ref[...].astype(F32)


def swap(x, axis, n, by):
    return lax.ppermute(x, axis, [(i, i ^ by) for i in range(n)])


def step(x, n_row, n_col, by):
    pairs = []
    for i in range(n_row):
        for j in range(n_col):
            bit = by if j % 2 == 0 else n_row // 2 // by
            pairs.append((i * n_col + j, (i ^ bit) * n_col + j))
    return lax.ppermute(x, ("row", "col"), pairs)


def deal(xs, axis):
    n = len(xs)
    got = {by: swap(xs[by], axis, n, by) for by in range(1, n)}
    return [xs[0]] + [got[by] for by in range(1, n)]


def spread(x, axis, n):
    return deal([x] * n, axis)


def shards(n_row, n_col, features, adj_tiles, columns, counts, weight, bias_term, cotangent):
    tile, width = features.shape
    n_chip = n_col // 2
    piece = width // 2
    half = n_chip * tile
    xs = spread(features, "row", n_row)
    cots = [cotangent] + [swap(cotangent, "col", n_col, 2 * v) for v in range(1, n_chip)]
    columns, counts = columns.transpose(1, 2, 0), counts.T
    a = call(
        dense_kernel(n_chip),
        shape(n_col * tile, n_row * tile),
        count=3,
        smem=2,
    )(columns, counts, adj_tiles)
    at = call(transpose_kernel(n_row), shape(n_row * tile, n_col * tile), count=1)(a)
    keep, send, *cots[1:] = call(
        forward_kernel(n_row, n_chip - 1),
        (shape(half, width, dtype=F32), shape(half, width)) + (shape(tile, width),) * (n_chip - 1),
        count=n_row + n_chip,
    )(a, *xs[::-1], *cots[1:])
    chip = call(chip_kernel, shape(half, width), count=2)(keep, swap(send, "col", n_col, 1))
    sums = [chip] + [swap(chip, "col", n_col, 2 * v) for v in range(1, n_chip)]
    act, keep, part, send = call(
        middle_kernel(n_chip),
        (
            shape(tile, width),
            shape(half + PAD, width),
            shape(piece, width),
            shape(half + PAD + piece, width),
        ),
        count=3 + 2 * n_chip,
        scratch=[
            pltpu.VMEM((half, width), BF),
            pltpu.VMEM((half, width), BF),
            pltpu.VMEM((width, width), F32),
        ],
    )(weight, bias_term.reshape(1, width), *sums, *cots, at)
    got = swap(send, "col", n_col, 1)
    part = call(part_kernel, shape(piece, width), count=2)(part, got)
    live = n_row * tile // 2
    size = live // 2
    keep, *sends = call(
        backward_kernel,
        (shape(live, width, dtype=F32), shape(size, width), shape(size + PAD, width)),
        count=3,
    )(at, keep, got)
    terms, by = [(keep, 0, live)], 1
    while True:
        other = step(part, n_row, n_col, by)
        sent, gots = sends[-1], [step(x, n_row, n_col, by) for x in reversed(sends)][::-1]
        terms += [(x, i * size, size) for i, x in enumerate(gots)]
        part = call(part_kernel, shape(piece, width), count=2)(part, other)
        by *= 2
        if by == n_row:
            break
        live //= 2
        size = live if live == tile else live // 2
        sends = []
        for first in range(live, 2 * live, size):
            over = [(x, first - at) for x, at, rows in terms if at <= first < at + rows]
            last = first + size == 2 * live
            sends.append(
                call(
                    range_kernel([at for _, at in over], last),
                    shape(size + PAD * last, width),
                    count=2 + len(over),
                )(sent, gots[-1], *[x for x, _ in over])
            )
        terms = [(x, at, rows) for x, at, rows in terms if at < live]
    act, grad_features, grad_weight, grad_bias = call(
        last_kernel,
        (
            shape(tile, width),
            shape(tile, width),
            shape(width, width, dtype=F32),
            shape(1, width, dtype=F32),
        ),
        count=5 + len(terms),
    )(act, sent, gots[-1], part, swap(part, "col", n_col, 1), *[x for x, _, _ in terms])
    return act, grad_features, grad_weight, grad_bias.reshape(width)


def solution(mesh):
    n_row, n_col = mesh.shape["row"], mesh.shape["col"]
    placed = (
        P(("groups", "row", "col"), None),
        P(("groups", "row"), "col", None, None, None),
        P(("groups", "row"), "col", None),
        P(("groups", "row"), "col"),
        P(),
        P(),
        P(("groups", "row", "col"), None),
    )

    def body(*args):
        return shards(n_row, n_col, *args)

    return jax.shard_map(
        body,
        mesh=mesh,
        in_specs=placed,
        out_specs=(
            P(("groups", "row", "col"), None),
            P(("groups", "row", "col"), None),
            P("groups", None),
            P("groups"),
        ),
        check_vma=False,
    )
```

```python
import jax
import jax.numpy as jnp
from jax import lax
from jax.experimental import pallas as pl
from jax.experimental.pallas import tpu as pltpu
from jax.sharding import PartitionSpec as P

BF = jnp.bfloat16
F32 = jnp.float32
LIMIT = 48 * 1024 * 1024
PAD = 16


def dot(a, b, ca=1, cb=0):
    return lax.dot_general(a, b, (((ca,), (cb,)), ((), ())), preferred_element_type=F32)


def call(body, outs, smem=0, count=1, scratch=()):
    vm = pl.BlockSpec(memory_space=pltpu.VMEM)
    sm = pl.BlockSpec(memory_space=pltpu.SMEM)
    return pl.pallas_call(
        body,
        in_specs=[sm] * smem + [vm] * (count - smem),
        out_specs=jax.tree.map(lambda _: vm, outs),
        out_shape=outs,
        scratch_shapes=scratch,
        compiler_params=pltpu.CompilerParams(vmem_limit_bytes=LIMIT),
    )


def shape(*dims, dtype=BF):
    return jax.ShapeDtypeStruct(dims, dtype)


def place_of(c, n_chip):
    return lax.rem(c, 2) * n_chip + lax.div(c, 2)


def reversed_bits(p, n):
    total, bit = 0, 1
    while bit < n:
        total = 2 * total + lax.rem(lax.div(p, bit), 2)
        bit *= 2
    return total


def dense_kernel(n_chip):
    def body(cols_ref, cnts_ref, tiles_ref, a_ref):
        trows, _, slots, tile, _ = tiles_ref.shape
        r = lax.axis_index("row")
        c = lax.axis_index("col")
        a_ref[...] = jnp.zeros_like(a_ref)

        def put(step, carry):
            t = step // slots
            k = step % slots

            @pl.when(k < cnts_ref[0, t])
            def _():
                q = place_of(jnp.bitwise_xor(t, c), n_chip)
                p = jnp.bitwise_xor(cols_ref[0, k, t], r)
                qs = pl.ds(pl.multiple_of(q * tile, tile), tile)
                ps = pl.ds(pl.multiple_of(p * tile, tile), tile)
                a_ref[qs, ps] = tiles_ref[t, 0, k]

            return carry

        lax.fori_loop(0, trows * slots, put, 0)

    return body


def transpose_kernel(n_row):
    def body(a_ref, at_ref):
        tile = at_ref.shape[0] // n_row
        core = lax.rem(lax.axis_index("col"), 2)

        def turn(p, carry):
            place = jnp.where(core == 0, reversed_bits(p, n_row), p)
            here = a_ref[:, pl.ds(pl.multiple_of(p * tile, tile), tile)]
            at_ref[pl.ds(pl.multiple_of(place * tile, tile), tile), :] = here.T
            return carry

        lax.fori_loop(0, n_row, turn, 0)

    return body


def forward_kernel(n_row, n_cot):
    def body(a_ref, *refs):
        ins, (keep_ref, send_ref, *outs) = refs[:n_row], refs[n_row + n_cot :]
        for ref, out in zip(refs[n_row:], outs):
            out[...] = ref[...]
        half = keep_ref.shape[0]
        x = jnp.concatenate([ref[...] for ref in ins[::-1]], axis=0)
        send_ref[...] = dot(a_ref[half:, :], x).astype(BF)
        keep_ref[...] = dot(a_ref[:half, :], x)

    return body


def chip_kernel(keep_ref, got_ref, out_ref):
    out_ref[...] = (keep_ref[...] + got_ref[...].astype(F32)).astype(BF)


def two_rows(line):
    high = line.astype(BF).astype(F32)
    which = lax.broadcasted_iota(jnp.int32, (PAD, line.shape[1]), 0)
    return jnp.where(which == 0, high, jnp.where(which == 1, line - high, 0.0)).astype(BF)


def middle_kernel(n_chip):
    def body(w_ref, b_ref, *refs):
        sums, cots = refs[:n_chip], refs[n_chip : 2 * n_chip]
        act_ref, keep_ref, part_ref, send_ref, agg_ref, grad_ref, local_ref = refs[2 * n_chip + 1 :]
        tile, width = cots[0].shape
        rows, piece = n_chip * tile, width // 2
        c = lax.axis_index("col")
        chip, core = lax.div(c, 2), lax.rem(c, 2)
        blocks = []
        for u in range(n_chip):
            total = sums[0][u * tile : (u + 1) * tile, :].astype(F32)
            for v in range(1, n_chip):
                total = total + sums[v][(u ^ v) * tile : ((u ^ v) + 1) * tile, :].astype(F32)
            blocks.append(total.astype(BF))
        agg = jnp.concatenate(blocks, axis=0)
        cot = jnp.concatenate([ref[...] for ref in cots], axis=0).astype(F32)
        preact = dot(agg, w_ref[...]) + b_ref[...].astype(F32)
        sig = jax.nn.sigmoid(preact)
        act_ref[...] = (preact[:tile] * sig[:tile]).astype(BF)
        grad = (cot * (sig * (1.0 + preact * (1.0 - sig)))).astype(BF)
        gagg = dot(grad, w_ref[...], 1, 1).astype(BF)
        keep_ref[:rows, :] = gagg
        send_ref[:rows, :] = gagg
        for u in range(n_chip):
            here = pl.ds(pl.multiple_of(jnp.bitwise_xor(chip, u) * tile, tile), tile)
            agg_ref[here, :] = blocks[u]
            grad_ref[here, :] = grad[u * tile : (u + 1) * tile, :]
        grad = grad_ref[...]
        local_ref[...] = dot(agg_ref[...], grad, 0, 0)
        mine = pl.multiple_of(core * piece, piece)
        other = pl.multiple_of((1 - core) * piece, piece)
        lines = two_rows(jnp.sum(grad.astype(F32), axis=0, keepdims=True))
        part_ref[...] = local_ref[pl.ds(mine, piece), :].astype(BF)
        keep_ref[rows:, :] = lines
        send_ref[rows : rows + PAD, :] = lines
        send_ref[rows + PAD :, :] = local_ref[pl.ds(other, piece), :].astype(BF)

    return body


def line_of(ref):
    rows = ref[ref.shape[0] - PAD :, :].astype(F32)
    return rows[0:1] + rows[1:2]


def part_kernel(part_ref, got_ref, out_ref):
    piece = out_ref.shape[0]
    first = got_ref.shape[0] - piece
    out_ref[...] = (part_ref[...].astype(F32) + got_ref[first:, :].astype(F32)).astype(BF)


def backward_kernel(at_ref, mine_ref, got_ref, keep_ref, stay_ref, pass_ref):
    rows, first, size = mine_ref.shape[0] - PAD, keep_ref.shape[0], stay_ref.shape[0]
    g = jnp.concatenate([mine_ref[:rows, :], got_ref[:rows, :]], axis=0)
    pass_ref[:size, :] = dot(at_ref[first + size :, :], g).astype(BF)
    other = got_ref[rows : rows + PAD, :].astype(F32)
    pass_ref[size:, :] = two_rows(line_of(mine_ref) + (other[0:1] + other[1:2]))
    stay_ref[...] = dot(at_ref[first : first + size, :], g).astype(BF)
    keep_ref[...] = dot(at_ref[:first, :], g)


def sum_of(refs, firsts, rows):
    total = None
    for ref, first in zip(refs, firsts):
        term = ref[first : first + rows, :].astype(F32)
        total = term if total is None else total + term
    return total


def range_kernel(firsts, with_line):
    def body(_, sent_ref, got_ref, *refs):
        out_ref = refs[-1]
        size = out_ref.shape[0] - PAD * with_line
        out_ref[:size, :] = sum_of(refs[:-1], firsts, size).astype(BF)
        if with_line:
            out_ref[size:, :] = two_rows(line_of(sent_ref) + line_of(got_ref))

    return body


def last_kernel(act_ref, sent_ref, line_ref, mine_ref, got_ref, *refs):
    terms, (act_out, feat_out, weight_out, bias_out) = refs[:-4], refs[-4:]
    piece = mine_ref.shape[0]
    core = lax.rem(lax.axis_index("col"), 2)
    act_out[...] = act_ref[...]
    feat_out[...] = sum_of(terms, [0] * len(terms), feat_out.shape[0]).astype(BF)
    bias_out[...] = line_of(sent_ref) + line_of(line_ref)
    mine = pl.multiple_of(core * piece, piece)
    other = pl.multiple_of((1 - core) * piece, piece)
    weight_out[pl.ds(mine, piece), :] = mine_ref[...].astype(F32)
    weight_out[pl.ds(other, piece), :] = got_ref[...].astype(F32)


def swap(x, axis, n, by):
    return lax.ppermute(x, axis, [(i, i ^ by) for i in range(n)])


def step(x, n_row, n_col, by):
    pairs = []
    for i in range(n_row):
        for j in range(n_col):
            bit = by if j % 2 == 0 else n_row // 2 // by
            pairs.append((i * n_col + j, (i ^ bit) * n_col + j))
    return lax.ppermute(x, ("row", "col"), pairs)


def deal(xs, axis):
    n = len(xs)
    got = {by: swap(xs[by], axis, n, by) for by in range(1, n)}
    return [xs[0]] + [got[by] for by in range(1, n)]


def spread(x, axis, n):
    return deal([x] * n, axis)


def shards(n_row, n_col, features, adj_tiles, columns, counts, weight, bias_term, cotangent):
    tile, width = features.shape
    n_chip = n_col // 2
    piece = width // 2
    half = n_chip * tile
    xs = spread(features, "row", n_row)
    cots = [cotangent] + [swap(cotangent, "col", n_col, 2 * v) for v in range(1, n_chip)]
    columns, counts = columns.transpose(1, 2, 0), counts.T
    a = call(
        dense_kernel(n_chip),
        shape(n_col * tile, n_row * tile),
        count=3,
        smem=2,
    )(columns, counts, adj_tiles)
    at = call(transpose_kernel(n_row), shape(n_row * tile, n_col * tile), count=1)(a)
    keep, send, *cots[1:] = call(
        forward_kernel(n_row, n_chip - 1),
        (shape(half, width, dtype=F32), shape(half, width)) + (shape(tile, width),) * (n_chip - 1),
        count=n_row + n_chip,
    )(a, *xs[::-1], *cots[1:])
    chip = call(chip_kernel, shape(half, width), count=2)(keep, swap(send, "col", n_col, 1))
    sums = [chip] + [swap(chip, "col", n_col, 2 * v) for v in range(1, n_chip)]
    act, keep, part, send = call(
        middle_kernel(n_chip),
        (
            shape(tile, width),
            shape(half + PAD, width),
            shape(piece, width),
            shape(half + PAD + piece, width),
        ),
        count=3 + 2 * n_chip,
        scratch=[
            pltpu.VMEM((half, width), BF),
            pltpu.VMEM((half, width), BF),
            pltpu.VMEM((width, width), F32),
        ],
    )(weight, bias_term.reshape(1, width), *sums, *cots, at)
    got = swap(send, "col", n_col, 1)
    part = call(part_kernel, shape(piece, width), count=2)(part, got)
    live = n_row * tile // 2
    size = live // 2
    keep, *sends = call(
        backward_kernel,
        (shape(live, width, dtype=F32), shape(size, width), shape(size + PAD, width)),
        count=3,
    )(at, keep, got)
    terms, by = [(keep, 0, live)], 1
    while True:
        other = step(part, n_row, n_col, by)
        sent, gots = sends[-1], [step(x, n_row, n_col, by) for x in reversed(sends)][::-1]
        terms += [(x, i * size, size) for i, x in enumerate(gots)]
        part = call(part_kernel, shape(piece, width), count=2)(part, other)
        by *= 2
        if by == n_row:
            break
        live //= 2
        size = live if live == tile else live // 2
        sends = []
        for first in range(live, 2 * live, size):
            over = [(x, first - at) for x, at, rows in terms if at <= first < at + rows]
            last = first + size == 2 * live
            sends.append(
                call(
                    range_kernel([at for _, at in over], last),
                    shape(size + PAD * last, width),
                    count=3 + len(over),
                )(gots[0], sent, gots[-1], *[x for x, _ in over])
            )
        terms = [(x, at, rows) for x, at, rows in terms if at < live]
    act, grad_features, grad_weight, grad_bias = call(
        last_kernel,
        (
            shape(tile, width),
            shape(tile, width),
            shape(width, width, dtype=F32),
            shape(1, width, dtype=F32),
        ),
        count=5 + len(terms),
    )(act, sent, gots[-1], part, swap(part, "col", n_col, 1), *[x for x, _, _ in terms])
    return act, grad_features, grad_weight, grad_bias.reshape(width)


def solution(mesh):
    n_row, n_col = mesh.shape["row"], mesh.shape["col"]
    placed = (
        P(("groups", "row", "col"), None),
        P(("groups", "row"), "col", None, None, None),
        P(("groups", "row"), "col", None),
        P(("groups", "row"), "col"),
        P(),
        P(),
        P(("groups", "row", "col"), None),
    )

    def body(*args):
        return shards(n_row, n_col, *args)

    return jax.shard_map(
        body,
        mesh=mesh,
        in_specs=placed,
        out_specs=(
            P(("groups", "row", "col"), None),
            P(("groups", "row", "col"), None),
            P("groups", None),
            P("groups"),
        ),
        check_vma=False,
    )
```

```python
import jax
import jax.numpy as jnp
from jax import lax
from jax.experimental import pallas as pl
from jax.experimental.pallas import tpu as pltpu
from jax.sharding import PartitionSpec as P

BF = jnp.bfloat16
F32 = jnp.float32
LIMIT = 48 * 1024 * 1024
PAD = 16


def dot(a, b, ca=1, cb=0):
    return lax.dot_general(a, b, (((ca,), (cb,)), ((), ())), preferred_element_type=F32)


def call(body, outs, smem=0, count=1, scratch=()):
    vm = pl.BlockSpec(memory_space=pltpu.VMEM)
    sm = pl.BlockSpec(memory_space=pltpu.SMEM)
    return pl.pallas_call(
        body,
        in_specs=[sm] * smem + [vm] * (count - smem),
        out_specs=jax.tree.map(lambda _: vm, outs),
        out_shape=outs,
        scratch_shapes=scratch,
        compiler_params=pltpu.CompilerParams(vmem_limit_bytes=LIMIT),
    )


def shape(*dims, dtype=BF):
    return jax.ShapeDtypeStruct(dims, dtype)


def place_of(c, n_chip):
    return lax.rem(c, 2) * n_chip + lax.div(c, 2)


def reversed_bits(p, n):
    total, bit = 0, 1
    while bit < n:
        total = 2 * total + lax.rem(lax.div(p, bit), 2)
        bit *= 2
    return total


def dense_kernel(n_chip):
    def body(cols_ref, cnts_ref, tiles_ref, a_ref):
        trows, _, slots, tile, _ = tiles_ref.shape
        r = lax.axis_index("row")
        c = lax.axis_index("col")
        a_ref[...] = jnp.zeros_like(a_ref)

        def put(step, carry):
            t = step // slots
            k = step % slots

            @pl.when(k < cnts_ref[0, t])
            def _():
                q = place_of(jnp.bitwise_xor(t, c), n_chip)
                p = jnp.bitwise_xor(cols_ref[0, k, t], r)
                qs = pl.ds(pl.multiple_of(q * tile, tile), tile)
                ps = pl.ds(pl.multiple_of(p * tile, tile), tile)
                a_ref[qs, ps] = tiles_ref[t, 0, k]

            return carry

        lax.fori_loop(0, trows * slots, put, 0)

    return body


def transpose_kernel(n_row):
    def body(a_ref, at_ref):
        tile = at_ref.shape[0] // n_row
        core = lax.rem(lax.axis_index("col"), 2)

        def turn(p, carry):
            place = jnp.where(core == 0, reversed_bits(p, n_row), p)
            here = a_ref[:, pl.ds(pl.multiple_of(p * tile, tile), tile)]
            at_ref[pl.ds(pl.multiple_of(place * tile, tile), tile), :] = here.T
            return carry

        lax.fori_loop(0, n_row, turn, 0)

    return body


def forward_kernel(n_row, n_cot):
    def body(a_ref, *refs):
        ins, (keep_ref, send_ref, *outs) = refs[:n_row], refs[n_row + n_cot :]
        for ref, out in zip(refs[n_row:], outs):
            out[...] = ref[...]
        half = keep_ref.shape[0]
        x = jnp.concatenate([ref[...] for ref in ins[::-1]], axis=0)
        send_ref[...] = dot(a_ref[half:, :], x).astype(BF)
        keep_ref[...] = dot(a_ref[:half, :], x)

    return body


def chip_kernel(keep_ref, got_ref, out_ref):
    out_ref[...] = (keep_ref[...] + got_ref[...].astype(F32)).astype(BF)


def two_rows(line):
    high = line.astype(BF).astype(F32)
    which = lax.broadcasted_iota(jnp.int32, (PAD, line.shape[1]), 0)
    return jnp.where(which == 0, high, jnp.where(which == 1, line - high, 0.0)).astype(BF)


def middle_kernel(n_chip):
    def body(w_ref, b_ref, *refs):
        sums, cots = refs[:n_chip], refs[n_chip : 2 * n_chip]
        act_ref, keep_ref, part_ref, send_ref, agg_ref, grad_ref, local_ref = refs[2 * n_chip + 1 :]
        tile, width = cots[0].shape
        rows, piece = n_chip * tile, width // 2
        c = lax.axis_index("col")
        chip, core = lax.div(c, 2), lax.rem(c, 2)
        blocks = []
        for u in range(n_chip):
            total = sums[0][u * tile : (u + 1) * tile, :].astype(F32)
            for v in range(1, n_chip):
                total = total + sums[v][(u ^ v) * tile : ((u ^ v) + 1) * tile, :].astype(F32)
            blocks.append(total.astype(BF))
        agg = jnp.concatenate(blocks, axis=0)
        cot = jnp.concatenate([ref[...] for ref in cots], axis=0).astype(F32)
        preact = dot(agg, w_ref[...]) + b_ref[...].astype(F32)
        sig = jax.nn.sigmoid(preact)
        act_ref[...] = (preact[:tile] * sig[:tile]).astype(BF)
        grad = (cot * (sig * (1.0 + preact * (1.0 - sig)))).astype(BF)
        gagg = dot(grad, w_ref[...], 1, 1).astype(BF)
        keep_ref[:rows, :] = gagg
        send_ref[:rows, :] = gagg
        for u in range(n_chip):
            here = pl.ds(pl.multiple_of(jnp.bitwise_xor(chip, u) * tile, tile), tile)
            agg_ref[here, :] = blocks[u]
            grad_ref[here, :] = grad[u * tile : (u + 1) * tile, :]
        grad = grad_ref[...]
        local_ref[...] = dot(agg_ref[...], grad, 0, 0)
        mine = pl.multiple_of(core * piece, piece)
        other = pl.multiple_of((1 - core) * piece, piece)
        lines = two_rows(jnp.sum(grad.astype(F32), axis=0, keepdims=True))
        part_ref[...] = local_ref[pl.ds(mine, piece), :].astype(BF)
        keep_ref[rows:, :] = lines
        send_ref[rows : rows + PAD, :] = lines
        send_ref[rows + PAD :, :] = local_ref[pl.ds(other, piece), :].astype(BF)

    return body


def line_of(ref):
    rows = ref[ref.shape[0] - PAD :, :].astype(F32)
    return rows[0:1] + rows[1:2]


def part_kernel(part_ref, got_ref, out_ref):
    piece = out_ref.shape[0]
    first = got_ref.shape[0] - piece
    out_ref[...] = (part_ref[...].astype(F32) + got_ref[first:, :].astype(F32)).astype(BF)


def backward_kernel(at_ref, mine_ref, got_ref, keep_ref, stay_ref, pass_ref):
    rows, first, size = mine_ref.shape[0] - PAD, keep_ref.shape[0], stay_ref.shape[0]
    g = jnp.concatenate([mine_ref[:rows, :], got_ref[:rows, :]], axis=0)
    pass_ref[:size, :] = dot(at_ref[first + size :, :], g).astype(BF)
    other = got_ref[rows : rows + PAD, :].astype(F32)
    pass_ref[size:, :] = two_rows(line_of(mine_ref) + (other[0:1] + other[1:2]))
    stay_ref[...] = dot(at_ref[first : first + size, :], g).astype(BF)
    keep_ref[...] = dot(at_ref[:first, :], g)


def sum_of(refs, firsts, rows):
    total = None
    for ref, first in zip(refs, firsts):
        term = ref[first : first + rows, :].astype(F32)
        total = term if total is None else total + term
    return total


def range_kernel(firsts, with_line):
    def body(sent_ref, got_ref, *refs):
        out_ref = refs[-1]
        size = out_ref.shape[0] - PAD * with_line
        out_ref[:size, :] = sum_of(refs[:-1], firsts, size).astype(BF)
        if with_line:
            out_ref[size:, :] = two_rows(line_of(sent_ref) + line_of(got_ref))

    return body


def last_kernel(act_ref, sent_ref, line_ref, mine_ref, got_ref, *refs):
    terms, (act_out, feat_out, weight_out, bias_out) = refs[:-4], refs[-4:]
    piece = mine_ref.shape[0]
    core = lax.rem(lax.axis_index("col"), 2)
    act_out[...] = act_ref[...]
    feat_out[...] = sum_of(terms, [0] * len(terms), feat_out.shape[0]).astype(BF)
    bias_out[...] = line_of(sent_ref) + line_of(line_ref)
    mine = pl.multiple_of(core * piece, piece)
    other = pl.multiple_of((1 - core) * piece, piece)
    weight_out[pl.ds(mine, piece), :] = mine_ref[...].astype(F32)
    weight_out[pl.ds(other, piece), :] = got_ref[...].astype(F32)


def swap(x, axis, n, by):
    return lax.ppermute(x, axis, [(i, i ^ by) for i in range(n)])


def step(x, n_row, n_col, by, first=0):
    pairs = []
    for i in range(n_row):
        for j in range(n_col):
            bit = by if j % 2 == first else n_row // 2 // by
            pairs.append((i * n_col + j, (i ^ bit) * n_col + j))
    return lax.ppermute(x, ("row", "col"), pairs)


def deal(xs, axis):
    n = len(xs)
    got = {by: swap(xs[by], axis, n, by) for by in range(1, n)}
    return [xs[0]] + [got[by] for by in range(1, n)]


def spread(x, axis, n):
    return deal([x] * n, axis)


def shards(n_row, n_col, features, adj_tiles, columns, counts, weight, bias_term, cotangent):
    tile, width = features.shape
    n_chip = n_col // 2
    piece = width // 2
    half = n_chip * tile
    xs = spread(features, "row", n_row)
    cots = [cotangent] + [swap(cotangent, "col", n_col, 2 * v) for v in range(1, n_chip)]
    columns, counts = columns.transpose(1, 2, 0), counts.T
    a = call(
        dense_kernel(n_chip),
        shape(n_col * tile, n_row * tile),
        count=3,
        smem=2,
    )(columns, counts, adj_tiles)
    at = call(transpose_kernel(n_row), shape(n_row * tile, n_col * tile), count=1)(a)
    keep, send, *cots[1:] = call(
        forward_kernel(n_row, n_chip - 1),
        (shape(half, width, dtype=F32), shape(half, width)) + (shape(tile, width),) * (n_chip - 1),
        count=n_row + n_chip,
    )(a, *xs[::-1], *cots[1:])
    chip = call(chip_kernel, shape(half, width), count=2)(keep, swap(send, "col", n_col, 1))
    sums = [chip] + [swap(chip, "col", n_col, 2 * v) for v in range(1, n_chip)]
    act, keep, part, send = call(
        middle_kernel(n_chip),
        (
            shape(tile, width),
            shape(half + PAD, width),
            shape(piece, width),
            shape(half + PAD + piece, width),
        ),
        count=3 + 2 * n_chip,
        scratch=[
            pltpu.VMEM((half, width), BF),
            pltpu.VMEM((half, width), BF),
            pltpu.VMEM((width, width), F32),
        ],
    )(weight, bias_term.reshape(1, width), *sums, *cots, at)
    got = swap(send, "col", n_col, 1)
    part = call(part_kernel, shape(piece, width), count=2)(part, got)
    live = n_row * tile // 2
    size = live // 2
    keep, *sends = call(
        backward_kernel,
        (shape(live, width, dtype=F32), shape(size, width), shape(size + PAD, width)),
        count=3,
    )(at, keep, got)
    terms, by = [(keep, 0, live)], 1
    while True:
        other = step(part, n_row, n_col, by, 1)
        sent, gots = sends[-1], [step(x, n_row, n_col, by) for x in reversed(sends)][::-1]
        terms += [(x, i * size, size) for i, x in enumerate(gots)]
        part = call(part_kernel, shape(piece, width), count=2)(part, other)
        by *= 2
        if by == n_row:
            break
        live //= 2
        size = live if live == tile else live // 2
        sends = []
        for first in range(live, 2 * live, size):
            over = [(x, first - at) for x, at, rows in terms if at <= first < at + rows]
            last = first + size == 2 * live
            sends.append(
                call(
                    range_kernel([at for _, at in over], last),
                    shape(size + PAD * last, width),
                    count=2 + len(over),
                )(sent, gots[-1], *[x for x, _ in over])
            )
        terms = [(x, at, rows) for x, at, rows in terms if at < live]
    act, grad_features, grad_weight, grad_bias = call(
        last_kernel,
        (
            shape(tile, width),
            shape(tile, width),
            shape(width, width, dtype=F32),
            shape(1, width, dtype=F32),
        ),
        count=5 + len(terms),
    )(act, sent, gots[-1], part, swap(part, "col", n_col, 1), *[x for x, _, _ in terms])
    return act, grad_features, grad_weight, grad_bias.reshape(width)


def solution(mesh):
    n_row, n_col = mesh.shape["row"], mesh.shape["col"]
    placed = (
        P(("groups", "row", "col"), None),
        P(("groups", "row"), "col", None, None, None),
        P(("groups", "row"), "col", None),
        P(("groups", "row"), "col"),
        P(),
        P(),
        P(("groups", "row", "col"), None),
    )

    def body(*args):
        return shards(n_row, n_col, *args)

    return jax.shard_map(
        body,
        mesh=mesh,
        in_specs=placed,
        out_specs=(
            P(("groups", "row", "col"), None),
            P(("groups", "row", "col"), None),
            P("groups", None),
            P("groups"),
        ),
        check_vma=False,
    )
```

```python
import jax
import jax.numpy as jnp
from jax import lax
from jax.experimental import pallas as pl
from jax.experimental.pallas import tpu as pltpu
from jax.sharding import PartitionSpec as P

BF = jnp.bfloat16
F32 = jnp.float32
LIMIT = 48 * 1024 * 1024
PAD = 16


def dot(a, b, ca=1, cb=0):
    return lax.dot_general(a, b, (((ca,), (cb,)), ((), ())), preferred_element_type=F32)


def call(body, outs, smem=0, count=1, scratch=()):
    vm = pl.BlockSpec(memory_space=pltpu.VMEM)
    sm = pl.BlockSpec(memory_space=pltpu.SMEM)
    return pl.pallas_call(
        body,
        in_specs=[sm] * smem + [vm] * (count - smem),
        out_specs=jax.tree.map(lambda _: vm, outs),
        out_shape=outs,
        scratch_shapes=scratch,
        compiler_params=pltpu.CompilerParams(vmem_limit_bytes=LIMIT),
    )


def shape(*dims, dtype=BF):
    return jax.ShapeDtypeStruct(dims, dtype)


def place_of(c, n_chip):
    return lax.rem(c, 2) * n_chip + lax.div(c, 2)


def reversed_bits(p, n):
    total, bit = 0, 1
    while bit < n:
        total = 2 * total + lax.rem(lax.div(p, bit), 2)
        bit *= 2
    return total


def dense_kernel(n_chip):
    def body(cols_ref, cnts_ref, tiles_ref, a_ref):
        trows, _, slots, tile, _ = tiles_ref.shape
        r = lax.axis_index("row")
        c = lax.axis_index("col")
        a_ref[...] = jnp.zeros_like(a_ref)

        def put(step, carry):
            t = step // slots
            k = step % slots

            @pl.when(k < cnts_ref[0, t])
            def _():
                q = place_of(jnp.bitwise_xor(t, c), n_chip)
                p = jnp.bitwise_xor(cols_ref[0, k, t], r)
                qs = pl.ds(pl.multiple_of(q * tile, tile), tile)
                ps = pl.ds(pl.multiple_of(p * tile, tile), tile)
                a_ref[qs, ps] = tiles_ref[t, 0, k]

            return carry

        lax.fori_loop(0, trows * slots, put, 0)

    return body


def transpose_kernel(n_row):
    def body(a_ref, at_ref):
        tile = at_ref.shape[0] // n_row

        def turn(p, carry):
            place = reversed_bits(p, n_row)
            here = a_ref[:, pl.ds(pl.multiple_of(p * tile, tile), tile)]
            at_ref[pl.ds(pl.multiple_of(place * tile, tile), tile), :] = here.T
            return carry

        lax.fori_loop(0, n_row, turn, 0)

    return body


def forward_kernel(n_row, n_cot):
    def body(a_ref, *refs):
        ins, (keep_ref, send_ref, *outs) = refs[:n_row], refs[n_row + n_cot :]
        for ref, out in zip(refs[n_row:], outs):
            out[...] = ref[...]
        half = keep_ref.shape[0]
        x = jnp.concatenate([ref[...] for ref in ins[::-1]], axis=0)
        send_ref[...] = dot(a_ref[half:, :], x).astype(BF)
        keep_ref[...] = dot(a_ref[:half, :], x)

    return body


def chip_kernel(keep_ref, got_ref, out_ref):
    out_ref[...] = (keep_ref[...] + got_ref[...].astype(F32)).astype(BF)


def two_rows(line):
    high = line.astype(BF).astype(F32)
    which = lax.broadcasted_iota(jnp.int32, (PAD, line.shape[1]), 0)
    return jnp.where(which == 0, high, jnp.where(which == 1, line - high, 0.0)).astype(BF)


def middle_kernel(n_chip):
    def body(w_ref, b_ref, *refs):
        sums, cots = refs[:n_chip], refs[n_chip : 2 * n_chip]
        act_ref, keep_ref, part_ref, send_ref, agg_ref, grad_ref, local_ref = refs[2 * n_chip + 1 :]
        tile, width = cots[0].shape
        rows, piece = n_chip * tile, width // 2
        c = lax.axis_index("col")
        chip, core = lax.div(c, 2), lax.rem(c, 2)
        blocks = []
        for u in range(n_chip):
            total = sums[0][u * tile : (u + 1) * tile, :].astype(F32)
            for v in range(1, n_chip):
                total = total + sums[v][(u ^ v) * tile : ((u ^ v) + 1) * tile, :].astype(F32)
            blocks.append(total.astype(BF))
        agg = jnp.concatenate(blocks, axis=0)
        cot = jnp.concatenate([ref[...] for ref in cots], axis=0).astype(F32)
        preact = dot(agg, w_ref[...]) + b_ref[...].astype(F32)
        sig = jax.nn.sigmoid(preact)
        act_ref[...] = (preact[:tile] * sig[:tile]).astype(BF)
        grad = (cot * (sig * (1.0 + preact * (1.0 - sig)))).astype(BF)
        gagg = dot(grad, w_ref[...], 1, 1).astype(BF)
        keep_ref[:rows, :] = gagg
        send_ref[:rows, :] = gagg
        for u in range(n_chip):
            here = pl.ds(pl.multiple_of(jnp.bitwise_xor(chip, u) * tile, tile), tile)
            agg_ref[here, :] = blocks[u]
            grad_ref[here, :] = grad[u * tile : (u + 1) * tile, :]
        grad = grad_ref[...]
        local_ref[...] = dot(agg_ref[...], grad, 0, 0)
        mine = pl.multiple_of(core * piece, piece)
        other = pl.multiple_of((1 - core) * piece, piece)
        lines = two_rows(jnp.sum(grad.astype(F32), axis=0, keepdims=True))
        part_ref[...] = local_ref[pl.ds(mine, piece), :].astype(BF)
        keep_ref[rows:, :] = lines
        send_ref[rows : rows + PAD, :] = lines
        send_ref[rows + PAD :, :] = local_ref[pl.ds(other, piece), :].astype(BF)

    return body


def line_of(ref):
    rows = ref[ref.shape[0] - PAD :, :].astype(F32)
    return rows[0:1] + rows[1:2]


def part_kernel(part_ref, got_ref, out_ref):
    piece = out_ref.shape[0]
    first = got_ref.shape[0] - piece
    out_ref[...] = (part_ref[...].astype(F32) + got_ref[first:, :].astype(F32)).astype(BF)


def backward_kernel(at_ref, mine_ref, got_ref, keep_ref, stay_ref, pass_ref):
    rows, first, size = mine_ref.shape[0] - PAD, keep_ref.shape[0], stay_ref.shape[0]
    g = jnp.concatenate([mine_ref[:rows, :], got_ref[:rows, :]], axis=0)
    pass_ref[:size, :] = dot(at_ref[first + size :, :], g).astype(BF)
    other = got_ref[rows : rows + PAD, :].astype(F32)
    pass_ref[size:, :] = two_rows(line_of(mine_ref) + (other[0:1] + other[1:2]))
    stay_ref[...] = dot(at_ref[first : first + size, :], g).astype(BF)
    keep_ref[...] = dot(at_ref[:first, :], g)


def sum_of(refs, firsts, rows):
    total = None
    for ref, first in zip(refs, firsts):
        term = ref[first : first + rows, :].astype(F32)
        total = term if total is None else total + term
    return total


def range_kernel(firsts, with_line):
    def body(sent_ref, got_ref, *refs):
        out_ref = refs[-1]
        size = out_ref.shape[0] - PAD * with_line
        out_ref[:size, :] = sum_of(refs[:-1], firsts, size).astype(BF)
        if with_line:
            out_ref[size:, :] = two_rows(line_of(sent_ref) + line_of(got_ref))

    return body


def last_kernel(act_ref, sent_ref, line_ref, mine_ref, got_ref, *refs):
    terms, (act_out, feat_out, weight_out, bias_out) = refs[:-4], refs[-4:]
    piece = mine_ref.shape[0]
    core = lax.rem(lax.axis_index("col"), 2)
    act_out[...] = act_ref[...]
    feat_out[...] = sum_of(terms, [0] * len(terms), feat_out.shape[0]).astype(BF)
    bias_out[...] = line_of(sent_ref) + line_of(line_ref)
    mine = pl.multiple_of(core * piece, piece)
    other = pl.multiple_of((1 - core) * piece, piece)
    weight_out[pl.ds(mine, piece), :] = mine_ref[...].astype(F32)
    weight_out[pl.ds(other, piece), :] = got_ref[...].astype(F32)


def swap(x, axis, n, by):
    return lax.ppermute(x, axis, [(i, i ^ by) for i in range(n)])


def deal(xs, axis):
    n = len(xs)
    got = {by: swap(xs[by], axis, n, by) for by in range(1, n)}
    return [xs[0]] + [got[by] for by in range(1, n)]


def spread(x, axis, n):
    return deal([x] * n, axis)


def shards(n_row, n_col, features, adj_tiles, columns, counts, weight, bias_term, cotangent):
    tile, width = features.shape
    n_chip = n_col // 2
    piece = width // 2
    half = n_chip * tile
    xs = spread(features, "row", n_row)
    cots = [cotangent] + [swap(cotangent, "col", n_col, 2 * v) for v in range(1, n_chip)]
    columns, counts = columns.transpose(1, 2, 0), counts.T
    a = call(
        dense_kernel(n_chip),
        shape(n_col * tile, n_row * tile),
        count=3,
        smem=2,
    )(columns, counts, adj_tiles)
    at = call(transpose_kernel(n_row), shape(n_row * tile, n_col * tile), count=1)(a)
    keep, send, *cots[1:] = call(
        forward_kernel(n_row, n_chip - 1),
        (shape(half, width, dtype=F32), shape(half, width)) + (shape(tile, width),) * (n_chip - 1),
        count=n_row + n_chip,
    )(a, *xs[::-1], *cots[1:])
    chip = call(chip_kernel, shape(half, width), count=2)(keep, swap(send, "col", n_col, 1))
    sums = [chip] + [swap(chip, "col", n_col, 2 * v) for v in range(1, n_chip)]
    act, keep, part, send = call(
        middle_kernel(n_chip),
        (
            shape(tile, width),
            shape(half + PAD, width),
            shape(piece, width),
            shape(half + PAD + piece, width),
        ),
        count=3 + 2 * n_chip,
        scratch=[
            pltpu.VMEM((half, width), BF),
            pltpu.VMEM((half, width), BF),
            pltpu.VMEM((width, width), F32),
        ],
    )(weight, bias_term.reshape(1, width), *sums, *cots, at)
    got = swap(send, "col", n_col, 1)
    part = call(part_kernel, shape(piece, width), count=2)(part, got)
    live = n_row * tile // 2
    size = live // 2
    keep, *sends = call(
        backward_kernel,
        (shape(live, width, dtype=F32), shape(size, width), shape(size + PAD, width)),
        count=3,
    )(at, keep, got)
    terms, by = [(keep, 0, live)], 1
    while True:
        other = swap(part, "row", n_row, n_row // 2 // by)
        sent, gots = sends[-1], [swap(x, "row", n_row, by) for x in reversed(sends)][::-1]
        terms += [(x, i * size, size) for i, x in enumerate(gots)]
        part = call(part_kernel, shape(piece, width), count=2)(part, other)
        by *= 2
        if by == n_row:
            break
        live //= 2
        size = live if live == tile else live // 2
        sends = []
        for first in range(live, 2 * live, size):
            over = [(x, first - at) for x, at, rows in terms if at <= first < at + rows]
            last = first + size == 2 * live
            sends.append(
                call(
                    range_kernel([at for _, at in over], last),
                    shape(size + PAD * last, width),
                    count=2 + len(over),
                )(sent, gots[-1], *[x for x, _ in over])
            )
        terms = [(x, at, rows) for x, at, rows in terms if at < live]
    act, grad_features, grad_weight, grad_bias = call(
        last_kernel,
        (
            shape(tile, width),
            shape(tile, width),
            shape(width, width, dtype=F32),
            shape(1, width, dtype=F32),
        ),
        count=5 + len(terms),
    )(act, sent, gots[-1], part, swap(part, "col", n_col, 1), *[x for x, _, _ in terms])
    return act, grad_features, grad_weight, grad_bias.reshape(width)


def solution(mesh):
    n_row, n_col = mesh.shape["row"], mesh.shape["col"]
    placed = (
        P(("groups", "row", "col"), None),
        P(("groups", "row"), "col", None, None, None),
        P(("groups", "row"), "col", None),
        P(("groups", "row"), "col"),
        P(),
        P(),
        P(("groups", "row", "col"), None),
    )

    def body(*args):
        return shards(n_row, n_col, *args)

    return jax.shard_map(
        body,
        mesh=mesh,
        in_specs=placed,
        out_specs=(
            P(("groups", "row", "col"), None),
            P(("groups", "row", "col"), None),
            P("groups", None),
            P("groups"),
        ),
        check_vma=False,
    )
```

```python
import jax
import jax.numpy as jnp
from jax import lax
from jax.experimental import pallas as pl
from jax.experimental.pallas import tpu as pltpu
from jax.sharding import PartitionSpec as P

BF = jnp.bfloat16
F32 = jnp.float32
LIMIT = 48 * 1024 * 1024
PAD = 16


def dot(a, b, ca=1, cb=0):
    return lax.dot_general(a, b, (((ca,), (cb,)), ((), ())), preferred_element_type=F32)


def call(body, outs, smem=0, count=1, scratch=()):
    vm = pl.BlockSpec(memory_space=pltpu.VMEM)
    sm = pl.BlockSpec(memory_space=pltpu.SMEM)
    return pl.pallas_call(
        body,
        in_specs=[sm] * smem + [vm] * (count - smem),
        out_specs=jax.tree.map(lambda _: vm, outs),
        out_shape=outs,
        scratch_shapes=scratch,
        compiler_params=pltpu.CompilerParams(vmem_limit_bytes=LIMIT),
    )


def shape(*dims, dtype=BF):
    return jax.ShapeDtypeStruct(dims, dtype)


def place_of(c, n_chip):
    return lax.rem(c, 2) * n_chip + lax.div(c, 2)


def reversed_bits(p, n):
    total, bit = 0, 1
    while bit < n:
        total = 2 * total + lax.rem(lax.div(p, bit), 2)
        bit *= 2
    return total


def dense_kernel(n_chip):
    def body(cols_ref, cnts_ref, tiles_ref, a_ref):
        trows, _, slots, tile, _ = tiles_ref.shape
        r = lax.axis_index("row")
        c = lax.axis_index("col")
        a_ref[...] = jnp.zeros_like(a_ref)

        def put(step, carry):
            t = step // slots
            k = step % slots

            @pl.when(k < cnts_ref[0, t])
            def _():
                q = place_of(jnp.bitwise_xor(t, c), n_chip)
                p = jnp.bitwise_xor(cols_ref[0, k, t], r)
                qs = pl.ds(pl.multiple_of(q * tile, tile), tile)
                ps = pl.ds(pl.multiple_of(p * tile, tile), tile)
                a_ref[qs, ps] = tiles_ref[t, 0, k]

            return carry

        lax.fori_loop(0, trows * slots, put, 0)

    return body


def transpose_kernel(n_row):
    def body(a_ref, at_ref):
        tile = at_ref.shape[0] // n_row

        def turn(p, carry):
            place = reversed_bits(p, n_row)
            here = a_ref[:, pl.ds(pl.multiple_of(p * tile, tile), tile)]
            at_ref[pl.ds(pl.multiple_of(place * tile, tile), tile), :] = here.T
            return carry

        lax.fori_loop(0, n_row, turn, 0)

    return body


def forward_kernel(n_row, n_cot):
    def body(a_ref, *refs):
        ins, (keep_ref, send_ref, *outs) = refs[:n_row], refs[n_row + n_cot :]
        for ref, out in zip(refs[n_row:], outs):
            out[...] = ref[...]
        half = keep_ref.shape[0]
        x = jnp.concatenate([ref[...] for ref in ins[::-1]], axis=0)
        send_ref[...] = dot(a_ref[half:, :], x).astype(BF)
        keep_ref[...] = dot(a_ref[:half, :], x)

    return body


def chip_kernel(keep_ref, got_ref, out_ref):
    out_ref[...] = (keep_ref[...] + got_ref[...].astype(F32)).astype(BF)


def two_rows(line):
    high = line.astype(BF).astype(F32)
    which = lax.broadcasted_iota(jnp.int32, (PAD, line.shape[1]), 0)
    return jnp.where(which == 0, high, jnp.where(which == 1, line - high, 0.0)).astype(BF)


def middle_kernel(n_chip):
    def body(w_ref, b_ref, *refs):
        sums, cots = refs[:n_chip], refs[n_chip : 2 * n_chip]
        act_ref, keep_ref, part_ref, send_ref, agg_ref, grad_ref, local_ref = refs[2 * n_chip + 1 :]
        tile, width = cots[0].shape
        rows, piece = n_chip * tile, width // 2
        c = lax.axis_index("col")
        chip, core = lax.div(c, 2), lax.rem(c, 2)
        blocks = []
        for u in range(n_chip):
            total = sums[0][u * tile : (u + 1) * tile, :].astype(F32)
            for v in range(1, n_chip):
                total = total + sums[v][(u ^ v) * tile : ((u ^ v) + 1) * tile, :].astype(F32)
            blocks.append(total.astype(BF))
        agg = jnp.concatenate(blocks, axis=0)
        cot = jnp.concatenate([ref[...] for ref in cots], axis=0).astype(F32)
        preact = dot(agg, w_ref[...]) + b_ref[...].astype(F32)
        sig = jax.nn.sigmoid(preact)
        act_ref[...] = (preact[:tile] * sig[:tile]).astype(BF)
        grad = (cot * (sig * (1.0 + preact * (1.0 - sig)))).astype(BF)
        gagg = dot(grad, w_ref[...], 1, 1).astype(BF)
        keep_ref[:rows, :] = gagg
        send_ref[:rows, :] = gagg
        for u in range(n_chip):
            here = pl.ds(pl.multiple_of(jnp.bitwise_xor(chip, u) * tile, tile), tile)
            agg_ref[here, :] = blocks[u]
            grad_ref[here, :] = grad[u * tile : (u + 1) * tile, :]
        grad = grad_ref[...]
        local_ref[...] = dot(agg_ref[...], grad, 0, 0)
        mine = pl.multiple_of(core * piece, piece)
        other = pl.multiple_of((1 - core) * piece, piece)
        lines = two_rows(jnp.sum(grad.astype(F32), axis=0, keepdims=True))
        part_ref[...] = local_ref[pl.ds(mine, piece), :].astype(BF)
        keep_ref[rows:, :] = lines
        send_ref[rows : rows + PAD, :] = lines
        send_ref[rows + PAD :, :] = local_ref[pl.ds(other, piece), :].astype(BF)

    return body


def line_of(ref):
    rows = ref[ref.shape[0] - PAD :, :].astype(F32)
    return rows[0:1] + rows[1:2]


def part_kernel(part_ref, got_ref, out_ref):
    piece = out_ref.shape[0]
    first = got_ref.shape[0] - piece
    out_ref[...] = (part_ref[...].astype(F32) + got_ref[first:, :].astype(F32)).astype(BF)


def backward_kernel(at_ref, mine_ref, got_ref, keep_ref, stay_ref, pass_ref):
    rows, first, size = mine_ref.shape[0] - PAD, keep_ref.shape[0], stay_ref.shape[0]
    g = jnp.concatenate([mine_ref[:rows, :], got_ref[:rows, :]], axis=0)
    pass_ref[:size, :] = dot(at_ref[first + size :, :], g).astype(BF)
    other = got_ref[rows : rows + PAD, :].astype(F32)
    pass_ref[size:, :] = two_rows(line_of(mine_ref) + (other[0:1] + other[1:2]))
    stay_ref[...] = dot(at_ref[first : first + size, :], g).astype(BF)
    keep_ref[...] = dot(at_ref[:first, :], g)


def sum_of(refs, firsts, rows):
    total = None
    for ref, first in zip(refs, firsts):
        term = ref[first : first + rows, :].astype(F32)
        total = term if total is None else total + term
    return total


def range_kernel(firsts, with_line):
    def body(sent_ref, got_ref, *refs):
        out_ref = refs[-1]
        size = out_ref.shape[0] - PAD * with_line
        out_ref[:size, :] = sum_of(refs[:-1], firsts, size).astype(BF)
        if with_line:
            out_ref[size:, :] = two_rows(line_of(sent_ref) + line_of(got_ref))

    return body


def last_kernel(act_ref, sent_ref, line_ref, mine_ref, got_ref, *refs):
    terms, (act_out, feat_out, weight_out, bias_out) = refs[:-4], refs[-4:]
    piece = mine_ref.shape[0]
    core = lax.rem(lax.axis_index("col"), 2)
    act_out[...] = act_ref[...]
    feat_out[...] = sum_of(terms, [0] * len(terms), feat_out.shape[0]).astype(BF)
    bias_out[...] = line_of(sent_ref) + line_of(line_ref)
    mine = pl.multiple_of(core * piece, piece)
    other = pl.multiple_of((1 - core) * piece, piece)
    weight_out[pl.ds(mine, piece), :] = mine_ref[...].astype(F32)
    weight_out[pl.ds(other, piece), :] = got_ref[...].astype(F32)


def swap(x, axis, n, by):
    return lax.ppermute(x, axis, [(i, i ^ by) for i in range(n)])


def deal(xs, axis):
    n = len(xs)
    got = {by: swap(xs[by], axis, n, by) for by in range(1, n)}
    return [xs[0]] + [got[by] for by in range(1, n)]


def spread(x, axis, n):
    return deal([x] * n, axis)


def shards(n_row, n_col, features, adj_tiles, columns, counts, weight, bias_term, cotangent):
    tile, width = features.shape
    n_chip = n_col // 2
    piece = width // 2
    half = n_chip * tile
    xs = spread(features, "row", n_row)
    cots = [cotangent] + [swap(cotangent, "col", n_col, 2 * v) for v in range(1, n_chip)]
    columns, counts = columns.transpose(1, 2, 0), counts.T
    a = call(
        dense_kernel(n_chip),
        shape(n_col * tile, n_row * tile),
        count=3,
        smem=2,
    )(columns, counts, adj_tiles)
    at = call(transpose_kernel(n_row), shape(n_row * tile, n_col * tile), count=1)(a)
    keep, send, *cots[1:] = call(
        forward_kernel(n_row, n_chip - 1),
        (shape(half, width, dtype=F32), shape(half, width)) + (shape(tile, width),) * (n_chip - 1),
        count=n_row + n_chip,
    )(a, *xs[::-1], *cots[1:])
    chip = call(chip_kernel, shape(half, width), count=2)(keep, swap(send, "col", n_col, 1))
    sums = [chip] + [swap(chip, "col", n_col, 2 * v) for v in range(1, n_chip)]
    act, keep, part, send = call(
        middle_kernel(n_chip),
        (
            shape(tile, width),
            shape(half + PAD, width),
            shape(piece, width),
            shape(half + PAD + piece, width),
        ),
        count=3 + 2 * n_chip,
        scratch=[
            pltpu.VMEM((half, width), BF),
            pltpu.VMEM((half, width), BF),
            pltpu.VMEM((width, width), F32),
        ],
    )(weight, bias_term.reshape(1, width), *sums, *cots, at)
    got = swap(send, "col", n_col, 1)
    part = call(part_kernel, shape(piece, width), count=2)(part, got)
    live = n_row * tile // 2
    size = live // 2
    keep, *sends = call(
        backward_kernel,
        (shape(live, width, dtype=F32), shape(size, width), shape(size + PAD, width)),
        count=3,
    )(at, keep, got)
    terms, by = [(keep, 0, live)], 1
    while True:
        other = swap(part, "row", n_row, by)
        sent, gots = sends[-1], [swap(x, "row", n_row, by) for x in reversed(sends)][::-1]
        terms += [(x, i * size, size) for i, x in enumerate(gots)]
        part = call(part_kernel, shape(piece, width), count=2)(part, other)
        by *= 2
        if by == n_row:
            break
        live //= 2
        size = live if live == tile else live // 2
        sends = []
        for first in range(live, 2 * live, size):
            over = [(x, first - at) for x, at, rows in terms if at <= first < at + rows]
            last = first + size == 2 * live
            sends.append(
                call(
                    range_kernel([at for _, at in over], last),
                    shape(size + PAD * last, width),
                    count=2 + len(over),
                )(sent, gots[-1], *[x for x, _ in over])
            )
        terms = [(x, at, rows) for x, at, rows in terms if at < live]
    act, grad_features, grad_weight, grad_bias = call(
        last_kernel,
        (
            shape(tile, width),
            shape(tile, width),
            shape(width, width, dtype=F32),
            shape(1, width, dtype=F32),
        ),
        count=5 + len(terms),
    )(act, sent, gots[-1], part, swap(part, "col", n_col, 1), *[x for x, _, _ in terms])
    return act, grad_features, grad_weight, grad_bias.reshape(width)


def solution(mesh):
    n_row, n_col = mesh.shape["row"], mesh.shape["col"]
    placed = (
        P(("groups", "row", "col"), None),
        P(("groups", "row"), "col", None, None, None),
        P(("groups", "row"), "col", None),
        P(("groups", "row"), "col"),
        P(),
        P(),
        P(("groups", "row", "col"), None),
    )

    def body(*args):
        return shards(n_row, n_col, *args)

    return jax.shard_map(
        body,
        mesh=mesh,
        in_specs=placed,
        out_specs=(
            P(("groups", "row", "col"), None),
            P(("groups", "row", "col"), None),
            P("groups", None),
            P("groups"),
        ),
        check_vma=False,
    )
```

```python
import jax
import jax.numpy as jnp
from jax import lax
from jax.experimental import pallas as pl
from jax.experimental.pallas import tpu as pltpu
from jax.sharding import PartitionSpec as P

BF = jnp.bfloat16
F32 = jnp.float32
LIMIT = 48 * 1024 * 1024
PAD = 16


def dot(a, b, ca=1, cb=0):
    return lax.dot_general(a, b, (((ca,), (cb,)), ((), ())), preferred_element_type=F32)


def call(body, outs, smem=0, count=1, scratch=()):
    vm = pl.BlockSpec(memory_space=pltpu.VMEM)
    sm = pl.BlockSpec(memory_space=pltpu.SMEM)
    return pl.pallas_call(
        body,
        in_specs=[sm] * smem + [vm] * (count - smem),
        out_specs=jax.tree.map(lambda _: vm, outs),
        out_shape=outs,
        scratch_shapes=scratch,
        compiler_params=pltpu.CompilerParams(vmem_limit_bytes=LIMIT),
    )


def shape(*dims, dtype=BF):
    return jax.ShapeDtypeStruct(dims, dtype)


def place_of(c, n_chip):
    return lax.rem(c, 2) * n_chip + lax.div(c, 2)


def reversed_bits(p, n):
    total, bit = 0, 1
    while bit < n:
        total = 2 * total + lax.rem(lax.div(p, bit), 2)
        bit *= 2
    return total


def dense_kernel(n_chip):
    def body(cols_ref, cnts_ref, tiles_ref, a_ref):
        trows, _, slots, tile, _ = tiles_ref.shape
        r = lax.axis_index("row")
        c = lax.axis_index("col")
        a_ref[...] = jnp.zeros_like(a_ref)

        def put(step, carry):
            t = step // slots
            k = step % slots

            @pl.when(k < cnts_ref[0, t])
            def _():
                q = place_of(jnp.bitwise_xor(t, c), n_chip)
                p = jnp.bitwise_xor(cols_ref[0, k, t], r)
                qs = pl.ds(pl.multiple_of(q * tile, tile), tile)
                ps = pl.ds(pl.multiple_of(p * tile, tile), tile)
                a_ref[qs, ps] = tiles_ref[t, 0, k]

            return carry

        lax.fori_loop(0, trows * slots, put, 0)

    return body


def transpose_kernel(n_row):
    def body(a_ref, at_ref):
        tile = at_ref.shape[0] // n_row

        def turn(p, carry):
            place = reversed_bits(p, n_row)
            here = a_ref[:, pl.ds(pl.multiple_of(p * tile, tile), tile)]
            at_ref[pl.ds(pl.multiple_of(place * tile, tile), tile), :] = here.T
            return carry

        lax.fori_loop(0, n_row, turn, 0)

    return body


def meeting(n_row):
    half = n_row // 2
    return [half] + [p for p in range(n_row - 1, -1, -1) if p != half]


def places(n_row):
    return [meeting(n_row).index(p) for p in range(n_row)]


def forward_kernel(n_row, n_cot):
    def body(a_ref, *refs):
        ins, (keep_ref, send_ref, *outs) = refs[:n_row], refs[n_row + n_cot :]
        for ref, out in zip(refs[n_row:], outs):
            out[...] = ref[...]
        half = keep_ref.shape[0]
        x = jnp.concatenate([ins[i][...] for i in places(n_row)], axis=0)
        send_ref[...] = dot(a_ref[half:, :], x).astype(BF)
        keep_ref[...] = dot(a_ref[:half, :], x)

    return body


def chip_kernel(keep_ref, got_ref, out_ref):
    out_ref[...] = (keep_ref[...] + got_ref[...].astype(F32)).astype(BF)


def two_rows(line):
    high = line.astype(BF).astype(F32)
    which = lax.broadcasted_iota(jnp.int32, (PAD, line.shape[1]), 0)
    return jnp.where(which == 0, high, jnp.where(which == 1, line - high, 0.0)).astype(BF)


def middle_kernel(n_chip):
    def body(w_ref, b_ref, *refs):
        sums, cots = refs[:n_chip], refs[n_chip : 2 * n_chip]
        act_ref, keep_ref, part_ref, send_ref, agg_ref, grad_ref, local_ref = refs[2 * n_chip + 1 :]
        tile, width = cots[0].shape
        rows, piece = n_chip * tile, width // 2
        c = lax.axis_index("col")
        chip, core = lax.div(c, 2), lax.rem(c, 2)
        blocks = []
        for u in range(n_chip):
            total = sums[0][u * tile : (u + 1) * tile, :].astype(F32)
            for v in range(1, n_chip):
                total = total + sums[v][(u ^ v) * tile : ((u ^ v) + 1) * tile, :].astype(F32)
            blocks.append(total.astype(BF))
        agg = jnp.concatenate(blocks, axis=0)
        cot = jnp.concatenate([ref[...] for ref in cots], axis=0).astype(F32)
        preact = dot(agg, w_ref[...]) + b_ref[...].astype(F32)
        sig = jax.nn.sigmoid(preact)
        act_ref[...] = (preact[:tile] * sig[:tile]).astype(BF)
        grad = (cot * (sig * (1.0 + preact * (1.0 - sig)))).astype(BF)
        gagg = dot(grad, w_ref[...], 1, 1).astype(BF)
        keep_ref[:rows, :] = gagg
        send_ref[:rows, :] = gagg
        for u in range(n_chip):
            here = pl.ds(pl.multiple_of(jnp.bitwise_xor(chip, u) * tile, tile), tile)
            agg_ref[here, :] = blocks[u]
            grad_ref[here, :] = grad[u * tile : (u + 1) * tile, :]
        grad = grad_ref[...]
        local_ref[...] = dot(agg_ref[...], grad, 0, 0)
        mine = pl.multiple_of(core * piece, piece)
        other = pl.multiple_of((1 - core) * piece, piece)
        lines = two_rows(jnp.sum(grad.astype(F32), axis=0, keepdims=True))
        part_ref[...] = local_ref[pl.ds(mine, piece), :].astype(BF)
        keep_ref[rows:, :] = lines
        send_ref[rows : rows + PAD, :] = lines
        send_ref[rows + PAD :, :] = local_ref[pl.ds(other, piece), :].astype(BF)

    return body


def line_of(ref):
    rows = ref[ref.shape[0] - PAD :, :].astype(F32)
    return rows[0:1] + rows[1:2]


def part_kernel(part_ref, got_ref, out_ref):
    piece = out_ref.shape[0]
    first = got_ref.shape[0] - piece
    out_ref[...] = (part_ref[...].astype(F32) + got_ref[first:, :].astype(F32)).astype(BF)


def backward_kernel(at_ref, mine_ref, got_ref, keep_ref, stay_ref, pass_ref):
    rows, first, size = mine_ref.shape[0] - PAD, keep_ref.shape[0], stay_ref.shape[0]
    g = jnp.concatenate([mine_ref[:rows, :], got_ref[:rows, :]], axis=0)
    pass_ref[:size, :] = dot(at_ref[first + size :, :], g).astype(BF)
    other = got_ref[rows : rows + PAD, :].astype(F32)
    pass_ref[size:, :] = two_rows(line_of(mine_ref) + (other[0:1] + other[1:2]))
    stay_ref[...] = dot(at_ref[first : first + size, :], g).astype(BF)
    keep_ref[...] = dot(at_ref[:first, :], g)


def sum_of(refs, firsts, rows):
    total = None
    for ref, first in zip(refs, firsts):
        term = ref[first : first + rows, :].astype(F32)
        total = term if total is None else total + term
    return total


def range_kernel(firsts, with_line):
    def body(sent_ref, got_ref, *refs):
        out_ref = refs[-1]
        size = out_ref.shape[0] - PAD * with_line
        out_ref[:size, :] = sum_of(refs[:-1], firsts, size).astype(BF)
        if with_line:
            out_ref[size:, :] = two_rows(line_of(sent_ref) + line_of(got_ref))

    return body


def last_kernel(act_ref, sent_ref, line_ref, mine_ref, got_ref, *refs):
    terms, (act_out, feat_out, weight_out, bias_out) = refs[:-4], refs[-4:]
    piece = mine_ref.shape[0]
    core = lax.rem(lax.axis_index("col"), 2)
    act_out[...] = act_ref[...]
    feat_out[...] = sum_of(terms, [0] * len(terms), feat_out.shape[0]).astype(BF)
    bias_out[...] = line_of(sent_ref) + line_of(line_ref)
    mine = pl.multiple_of(core * piece, piece)
    other = pl.multiple_of((1 - core) * piece, piece)
    weight_out[pl.ds(mine, piece), :] = mine_ref[...].astype(F32)
    weight_out[pl.ds(other, piece), :] = got_ref[...].astype(F32)


def swap(x, axis, n, by):
    return lax.ppermute(x, axis, [(i, i ^ by) for i in range(n)])


def deal(xs, axis):
    n = len(xs)
    got = {by: swap(xs[by], axis, n, by) for by in range(1, n)}
    return [xs[0]] + [got[by] for by in range(1, n)]


def spread(x, axis, n):
    return deal([x] * n, axis)


def shards(n_row, n_col, features, adj_tiles, columns, counts, weight, bias_term, cotangent):
    tile, width = features.shape
    n_chip = n_col // 2
    piece = width // 2
    half = n_chip * tile
    xs = spread(features, "row", n_row)
    cots = [cotangent] + [swap(cotangent, "col", n_col, 2 * v) for v in range(1, n_chip)]
    columns, counts = columns.transpose(1, 2, 0), counts.T
    a = call(
        dense_kernel(n_chip),
        shape(n_col * tile, n_row * tile),
        count=3,
        smem=2,
    )(columns, counts, adj_tiles)
    at = call(transpose_kernel(n_row), shape(n_row * tile, n_col * tile), count=1)(a)
    keep, send, *cots[1:] = call(
        forward_kernel(n_row, n_chip - 1),
        (shape(half, width, dtype=F32), shape(half, width)) + (shape(tile, width),) * (n_chip - 1),
        count=n_row + n_chip,
    )(a, *[xs[p] for p in meeting(n_row)], *cots[1:])
    chip = call(chip_kernel, shape(half, width), count=2)(keep, swap(send, "col", n_col, 1))
    sums = [chip] + [swap(chip, "col", n_col, 2 * v) for v in range(1, n_chip)]
    act, keep, part, send = call(
        middle_kernel(n_chip),
        (
            shape(tile, width),
            shape(half + PAD, width),
            shape(piece, width),
            shape(half + PAD + piece, width),
        ),
        count=3 + 2 * n_chip,
        scratch=[
            pltpu.VMEM((half, width), BF),
            pltpu.VMEM((half, width), BF),
            pltpu.VMEM((width, width), F32),
        ],
    )(weight, bias_term.reshape(1, width), *sums, *cots, at)
    got = swap(send, "col", n_col, 1)
    part = call(part_kernel, shape(piece, width), count=2)(part, got)
    live = n_row * tile // 2
    size = live // 2
    keep, *sends = call(
        backward_kernel,
        (shape(live, width, dtype=F32), shape(size, width), shape(size + PAD, width)),
        count=3,
    )(at, keep, got)
    terms, by = [(keep, 0, live)], 1
    while True:
        other = swap(part, "row", n_row, by)
        sent, gots = sends[-1], [swap(x, "row", n_row, by) for x in reversed(sends)][::-1]
        terms += [(x, i * size, size) for i, x in enumerate(gots)]
        part = call(part_kernel, shape(piece, width), count=2)(part, other)
        by *= 2
        if by == n_row:
            break
        live //= 2
        size = live if live == tile else live // 2
        sends = []
        for first in range(live, 2 * live, size):
            over = [(x, first - at) for x, at, rows in terms if at <= first < at + rows]
            last = first + size == 2 * live
            sends.append(
                call(
                    range_kernel([at for _, at in over], last),
                    shape(size + PAD * last, width),
                    count=2 + len(over),
                )(sent, gots[-1], *[x for x, _ in over])
            )
        terms = [(x, at, rows) for x, at, rows in terms if at < live]
    act, grad_features, grad_weight, grad_bias = call(
        last_kernel,
        (
            shape(tile, width),
            shape(tile, width),
            shape(width, width, dtype=F32),
            shape(1, width, dtype=F32),
        ),
        count=5 + len(terms),
    )(act, sent, gots[-1], part, swap(part, "col", n_col, 1), *[x for x, _, _ in terms])
    return act, grad_features, grad_weight, grad_bias.reshape(width)


def solution(mesh):
    n_row, n_col = mesh.shape["row"], mesh.shape["col"]
    placed = (
        P(("groups", "row", "col"), None),
        P(("groups", "row"), "col", None, None, None),
        P(("groups", "row"), "col", None),
        P(("groups", "row"), "col"),
        P(),
        P(),
        P(("groups", "row", "col"), None),
    )

    def body(*args):
        return shards(n_row, n_col, *args)

    return jax.shard_map(
        body,
        mesh=mesh,
        in_specs=placed,
        out_specs=(
            P(("groups", "row", "col"), None),
            P(("groups", "row", "col"), None),
            P("groups", None),
            P("groups"),
        ),
        check_vma=False,
    )
```

```python
import jax
import jax.numpy as jnp
from jax import lax
from jax.experimental import pallas as pl
from jax.experimental.pallas import tpu as pltpu
from jax.sharding import PartitionSpec as P

BF = jnp.bfloat16
F32 = jnp.float32
LIMIT = 48 * 1024 * 1024
PAD = 16


def dot(a, b, ca=1, cb=0):
    return lax.dot_general(a, b, (((ca,), (cb,)), ((), ())), preferred_element_type=F32)


def call(body, outs, smem=0, count=1, scratch=()):
    vm = pl.BlockSpec(memory_space=pltpu.VMEM)
    sm = pl.BlockSpec(memory_space=pltpu.SMEM)
    return pl.pallas_call(
        body,
        in_specs=[sm] * smem + [vm] * (count - smem),
        out_specs=jax.tree.map(lambda _: vm, outs),
        out_shape=outs,
        scratch_shapes=scratch,
        compiler_params=pltpu.CompilerParams(vmem_limit_bytes=LIMIT),
    )


def shape(*dims, dtype=BF):
    return jax.ShapeDtypeStruct(dims, dtype)


def place_of(c, n_chip):
    return lax.rem(c, 2) * n_chip + lax.div(c, 2)


def reversed_bits(p, n):
    total, bit = 0, 1
    while bit < n:
        total = 2 * total + lax.rem(lax.div(p, bit), 2)
        bit *= 2
    return total


def dense_kernel(n_chip):
    def body(cols_ref, cnts_ref, tiles_ref, a_ref):
        trows, _, slots, tile, _ = tiles_ref.shape
        r = lax.axis_index("row")
        c = lax.axis_index("col")
        a_ref[...] = jnp.zeros_like(a_ref)

        def put(step, carry):
            t = step // slots
            k = step % slots

            @pl.when(k < cnts_ref[0, t])
            def _():
                q = place_of(jnp.bitwise_xor(t, c), n_chip)
                p = jnp.bitwise_xor(cols_ref[0, k, t], r)
                qs = pl.ds(pl.multiple_of(q * tile, tile), tile)
                ps = pl.ds(pl.multiple_of(p * tile, tile), tile)
                a_ref[qs, ps] = tiles_ref[t, 0, k]

            return carry

        lax.fori_loop(0, trows * slots, put, 0)

    return body


def transpose_kernel(n_row):
    def body(a_ref, at_ref):
        tile = at_ref.shape[0] // n_row

        def turn(p, carry):
            place = reversed_bits(p, n_row)
            here = a_ref[:, pl.ds(pl.multiple_of(p * tile, tile), tile)]
            at_ref[pl.ds(pl.multiple_of(place * tile, tile), tile), :] = here.T
            return carry

        lax.fori_loop(0, n_row, turn, 0)

    return body


def meeting(n_row):
    half = n_row // 2
    return [half] + [p for p in range(n_row - 1, -1, -1) if p != half]


def places(n_row):
    return [meeting(n_row).index(p) for p in range(n_row)]


def forward_kernel(n_row, n_cot):
    def body(a_ref, *refs):
        far = n_row - 2
        ins = refs[:far] + refs[far + n_cot : n_row + n_cot]
        keep_ref, send_ref, *outs = refs[n_row + n_cot :]
        for ref, out in zip(refs[far:], outs):
            out[...] = ref[...]
        half = keep_ref.shape[0]
        x = jnp.concatenate([ins[i][...] for i in places(n_row)], axis=0)
        send_ref[...] = dot(a_ref[half:, :], x).astype(BF)
        keep_ref[...] = dot(a_ref[:half, :], x)

    return body


def chip_kernel(keep_ref, got_ref, out_ref):
    out_ref[...] = (keep_ref[...] + got_ref[...].astype(F32)).astype(BF)


def two_rows(line):
    high = line.astype(BF).astype(F32)
    which = lax.broadcasted_iota(jnp.int32, (PAD, line.shape[1]), 0)
    return jnp.where(which == 0, high, jnp.where(which == 1, line - high, 0.0)).astype(BF)


def middle_kernel(n_chip):
    def body(w_ref, b_ref, *refs):
        sums, cots = refs[:n_chip], refs[n_chip : 2 * n_chip]
        act_ref, keep_ref, part_ref, send_ref, agg_ref, grad_ref, local_ref = refs[2 * n_chip + 1 :]
        tile, width = cots[0].shape
        rows, piece = n_chip * tile, width // 2
        c = lax.axis_index("col")
        chip, core = lax.div(c, 2), lax.rem(c, 2)
        blocks = []
        for u in range(n_chip):
            total = sums[0][u * tile : (u + 1) * tile, :].astype(F32)
            for v in range(1, n_chip):
                total = total + sums[v][(u ^ v) * tile : ((u ^ v) + 1) * tile, :].astype(F32)
            blocks.append(total.astype(BF))
        agg = jnp.concatenate(blocks, axis=0)
        cot = jnp.concatenate([ref[...] for ref in cots], axis=0).astype(F32)
        preact = dot(agg, w_ref[...]) + b_ref[...].astype(F32)
        sig = jax.nn.sigmoid(preact)
        act_ref[...] = (preact[:tile] * sig[:tile]).astype(BF)
        grad = (cot * (sig * (1.0 + preact * (1.0 - sig)))).astype(BF)
        gagg = dot(grad, w_ref[...], 1, 1).astype(BF)
        keep_ref[:rows, :] = gagg
        send_ref[:rows, :] = gagg
        for u in range(n_chip):
            here = pl.ds(pl.multiple_of(jnp.bitwise_xor(chip, u) * tile, tile), tile)
            agg_ref[here, :] = blocks[u]
            grad_ref[here, :] = grad[u * tile : (u + 1) * tile, :]
        grad = grad_ref[...]
        local_ref[...] = dot(agg_ref[...], grad, 0, 0)
        mine = pl.multiple_of(core * piece, piece)
        other = pl.multiple_of((1 - core) * piece, piece)
        lines = two_rows(jnp.sum(grad.astype(F32), axis=0, keepdims=True))
        part_ref[...] = local_ref[pl.ds(mine, piece), :].astype(BF)
        keep_ref[rows:, :] = lines
        send_ref[rows : rows + PAD, :] = lines
        send_ref[rows + PAD :, :] = local_ref[pl.ds(other, piece), :].astype(BF)

    return body


def line_of(ref):
    rows = ref[ref.shape[0] - PAD :, :].astype(F32)
    return rows[0:1] + rows[1:2]


def part_kernel(part_ref, got_ref, out_ref):
    piece = out_ref.shape[0]
    first = got_ref.shape[0] - piece
    out_ref[...] = (part_ref[...].astype(F32) + got_ref[first:, :].astype(F32)).astype(BF)


def backward_kernel(at_ref, mine_ref, got_ref, keep_ref, stay_ref, pass_ref):
    rows, first, size = mine_ref.shape[0] - PAD, keep_ref.shape[0], stay_ref.shape[0]
    g = jnp.concatenate([mine_ref[:rows, :], got_ref[:rows, :]], axis=0)
    pass_ref[:size, :] = dot(at_ref[first + size :, :], g).astype(BF)
    other = got_ref[rows : rows + PAD, :].astype(F32)
    pass_ref[size:, :] = two_rows(line_of(mine_ref) + (other[0:1] + other[1:2]))
    stay_ref[...] = dot(at_ref[first : first + size, :], g).astype(BF)
    keep_ref[...] = dot(at_ref[:first, :], g)


def sum_of(refs, firsts, rows):
    total = None
    for ref, first in zip(refs, firsts):
        term = ref[first : first + rows, :].astype(F32)
        total = term if total is None else total + term
    return total


def range_kernel(firsts, with_line):
    def body(sent_ref, got_ref, *refs):
        out_ref = refs[-1]
        size = out_ref.shape[0] - PAD * with_line
        out_ref[:size, :] = sum_of(refs[:-1], firsts, size).astype(BF)
        if with_line:
            out_ref[size:, :] = two_rows(line_of(sent_ref) + line_of(got_ref))

    return body


def last_kernel(act_ref, sent_ref, line_ref, mine_ref, got_ref, *refs):
    terms, (act_out, feat_out, weight_out, bias_out) = refs[:-4], refs[-4:]
    piece = mine_ref.shape[0]
    core = lax.rem(lax.axis_index("col"), 2)
    act_out[...] = act_ref[...]
    feat_out[...] = sum_of(terms, [0] * len(terms), feat_out.shape[0]).astype(BF)
    bias_out[...] = line_of(sent_ref) + line_of(line_ref)
    mine = pl.multiple_of(core * piece, piece)
    other = pl.multiple_of((1 - core) * piece, piece)
    weight_out[pl.ds(mine, piece), :] = mine_ref[...].astype(F32)
    weight_out[pl.ds(other, piece), :] = got_ref[...].astype(F32)


def swap(x, axis, n, by):
    return lax.ppermute(x, axis, [(i, i ^ by) for i in range(n)])


def deal(xs, axis):
    n = len(xs)
    got = {by: swap(xs[by], axis, n, by) for by in range(1, n)}
    return [xs[0]] + [got[by] for by in range(1, n)]


def spread(x, axis, n):
    return deal([x] * n, axis)


def shards(n_row, n_col, features, adj_tiles, columns, counts, weight, bias_term, cotangent):
    tile, width = features.shape
    n_chip = n_col // 2
    piece = width // 2
    half = n_chip * tile
    xs = spread(features, "row", n_row)
    cots = [cotangent] + [swap(cotangent, "col", n_col, 2 * v) for v in range(1, n_chip)]
    columns, counts = columns.transpose(1, 2, 0), counts.T
    a = call(
        dense_kernel(n_chip),
        shape(n_col * tile, n_row * tile),
        count=3,
        smem=2,
    )(columns, counts, adj_tiles)
    at = call(transpose_kernel(n_row), shape(n_row * tile, n_col * tile), count=1)(a)
    met = [xs[p] for p in meeting(n_row)]
    keep, send, *cots[1:] = call(
        forward_kernel(n_row, n_chip - 1),
        (shape(half, width, dtype=F32), shape(half, width)) + (shape(tile, width),) * (n_chip - 1),
        count=n_row + n_chip,
    )(a, *met[:-2], *cots[1:], *met[-2:])
    chip = call(chip_kernel, shape(half, width), count=2)(keep, swap(send, "col", n_col, 1))
    sums = [chip] + [swap(chip, "col", n_col, 2 * v) for v in range(1, n_chip)]
    act, keep, part, send = call(
        middle_kernel(n_chip),
        (
            shape(tile, width),
            shape(half + PAD, width),
            shape(piece, width),
            shape(half + PAD + piece, width),
        ),
        count=3 + 2 * n_chip,
        scratch=[
            pltpu.VMEM((half, width), BF),
            pltpu.VMEM((half, width), BF),
            pltpu.VMEM((width, width), F32),
        ],
    )(weight, bias_term.reshape(1, width), *sums, *cots, at)
    got = swap(send, "col", n_col, 1)
    part = call(part_kernel, shape(piece, width), count=2)(part, got)
    live = n_row * tile // 2
    size = live // 2
    keep, *sends = call(
        backward_kernel,
        (shape(live, width, dtype=F32), shape(size, width), shape(size + PAD, width)),
        count=3,
    )(at, keep, got)
    terms, by = [(keep, 0, live)], 1
    while True:
        other = swap(part, "row", n_row, by)
        sent, gots = sends[-1], [swap(x, "row", n_row, by) for x in reversed(sends)][::-1]
        terms += [(x, i * size, size) for i, x in enumerate(gots)]
        part = call(part_kernel, shape(piece, width), count=2)(part, other)
        by *= 2
        if by == n_row:
            break
        live //= 2
        size = live if live == tile else live // 2
        sends = []
        for first in range(live, 2 * live, size):
            over = [(x, first - at) for x, at, rows in terms if at <= first < at + rows]
            last = first + size == 2 * live
            sends.append(
                call(
                    range_kernel([at for _, at in over], last),
                    shape(size + PAD * last, width),
                    count=2 + len(over),
                )(sent, gots[-1], *[x for x, _ in over])
            )
        terms = [(x, at, rows) for x, at, rows in terms if at < live]
    act, grad_features, grad_weight, grad_bias = call(
        last_kernel,
        (
            shape(tile, width),
            shape(tile, width),
            shape(width, width, dtype=F32),
            shape(1, width, dtype=F32),
        ),
        count=5 + len(terms),
    )(act, sent, gots[-1], part, swap(part, "col", n_col, 1), *[x for x, _, _ in terms])
    return act, grad_features, grad_weight, grad_bias.reshape(width)


def solution(mesh):
    n_row, n_col = mesh.shape["row"], mesh.shape["col"]
    placed = (
        P(("groups", "row", "col"), None),
        P(("groups", "row"), "col", None, None, None),
        P(("groups", "row"), "col", None),
        P(("groups", "row"), "col"),
        P(),
        P(),
        P(("groups", "row", "col"), None),
    )

    def body(*args):
        return shards(n_row, n_col, *args)

    return jax.shard_map(
        body,
        mesh=mesh,
        in_specs=placed,
        out_specs=(
            P(("groups", "row", "col"), None),
            P(("groups", "row", "col"), None),
            P("groups", None),
            P("groups"),
        ),
        check_vma=False,
    )
```
